128 devices in a mesh: dp: 32 (over x_hi, z, y), seq: 4 (over x_lo, core).
Axes of the slice: x: 4 (x_hi: 2, x_lo: 2; x = x_hi * 2 + x_lo), y: 4, z: 4, core: 2. Of those that a mesh axis runs over, the one named last changes fastest.
Arguments:
- inputs: bfloat16 [32, 2048, 1536], P('dp', 'seq'), may hold values from -6 to 6
- cotangent: bfloat16 [32, 2048, 1536], P('dp', 'seq'), may hold values from -6 to 6
- conv_weight: float32 [768, 5, 768], P('dp'), may hold values from -0.09375 to 0.09375
- query_weight: float32 [1536, 512], P('dp'), as said below
- key_weight: float32 [1536, 128], P('dp'), as said below
- value_weight: float32 [1536, 128], P('dp'), may hold values from -0.15625 to 0.15625
- output_weight: float32 [512, 1536], P('dp'), may hold values from -0.25 to 0.25
- conv_gain: float32 [768], P('dp'), may hold values from 0.5 to 1.5
- attention_gain: float32 [1536], P('dp'), may hold values from 0.5 to 1.5
Outputs:
- input_grad: bfloat16 [32, 2048, 1536], P('dp', 'seq')
- conv_grad: float32 [768, 5, 768], P('dp')
- query_grad: float32 [1536, 512], P('dp')
- key_grad: float32 [1536, 128], P('dp')
- value_grad: float32 [1536, 128], P('dp')
- output_grad: float32 [512, 1536], P('dp')
- convnorm_grad: float32 [768], P('dp')
- attnnorm_grad: float32 [1536], P('dp')
The draws below stay inside these ranges and needn't reach their ends.
Inputs may be any that keep to these rules, and one draw needn't show every extreme that they name: `query_weight`: a projection scaled by its fan-in, to which some heads may add a component along the key projection of up to about 30 times the key projection's size, so that scores can reach several hundred. `key_weight`: a projection scaled by its fan-in.
All inputs are finite; a program needn't handle non-finite values.
Results may differ from the reference program's by a relative error of at most 0.035.
The reference program's roundings to bfloat16 on the way count: a program that leaves them out, or rounds other values in their place, can miss the bound.
Values may be sent and summed in bfloat16 or wider, within the bound.
No kernel may reach another device: no remote copies, remote signals or barrier semaphores. Data moves between devices by JAX's collectives and lax.ppermute only.
A program may use at most 192 MiB of HBM per device.

```python
import jax
import jax.numpy as jnp
from jax import lax

D = 1536
C = 768
KW = 5
H = 4
DH = 128
L = 2048
B = 32


def shared_keys(key):
    return jax.random.normal(key, (D, DH), jnp.float32) * D ** (-0.5)


def draw_key_weight(key, part):
    base = shared_keys(key)
    key = jax.random.fold_in(key, 11)
    return base * jax.random.uniform(key, (1, DH), jnp.float32, 0.6, 1.4)


def draw_query_weight(key, part):
    key = jax.random.fold_in(key, 12)
    own = jax.random.normal(key, (D, H * DH), jnp.float32) * D ** (-0.5)
    return own


def spiked(array, rng, source, target, parts, factor):
    def block_of(dim):
        return (jnp.arange(array.shape[dim]) // (array.shape[dim] // parts)).reshape((-1,) + (1,) * (array.ndim - 1 - dim))

    one_side = jax.random.permutation(rng, parts)[block_of(target)]
    second = (block_of(target) + parts // 2) % parts
    return jnp.where((block_of(source) == one_side) | (block_of(source) == second), factor * array, array)


def shard_levels(key, extent, shards, smallest, high):
    level = 1.0
    for axis_at, parts in shards:
        steps = jax.random.uniform(jax.random.fold_in(jax.random.fold_in(key, 6), axis_at), (parts,), jnp.float32, smallest / len(shards), high / len(shards))
        level = level * jnp.repeat(jnp.exp(steps), extent[axis_at] // parts).reshape((-1,) + (1,) * (len(extent) - 1 - axis_at))
    return level


def bell_draw(rng, dims, deviation, most, split=(), held_as=jnp.bfloat16):
    drawn = jax.random.normal(rng, dims, jnp.float32) * deviation
    if len(split) > 0:
        drawn = shard_levels(rng, dims, split, -0.22, 0.18) * drawn
    return jnp.clip(drawn, min=-most, max=most).astype(held_as)


def bell_draw_with(own_key, extent, spread, most, shards, heavy, held_as=jnp.bfloat16):
    result = spread * jax.random.normal(own_key, extent, jnp.float32)
    if shards:
        result = result * shard_levels(own_key, extent, shards, -0.22, 0.18)
    return jnp.clip(spiked(result, jax.random.fold_in(own_key, 3), *heavy), -most, most).astype(held_as)


def setup_inputs(seed: int = 0) -> dict:
    seeds = jax.random.split(jax.random.key(seed), 10)
    return {
        "inputs": bell_draw_with(seeds[0], (B, L, D), 1.0, 6.0, ((0, 32), (1, 4)), (0, 2, 32, 2.75)),
        "cotangent": bell_draw(seeds[1], (B, L, D), 1.0, 6.0, ((0, 32), (1, 4))),
        "conv_weight": bell_draw(seeds[2], (C, KW, C), (C * KW) ** -0.5, 0.09375, ((0, 32),), jnp.float32),
        "query_weight": draw_query_weight(jax.random.fold_in(seeds[9], 71), 0),
        "key_weight": draw_key_weight(jax.random.fold_in(seeds[9], 71), 0),
        "value_weight": bell_draw(seeds[5], (D, DH), D ** -0.5, 0.15625, ((0, 32),), jnp.float32),
        "output_weight": bell_draw(seeds[6], (H * DH, D), (H * DH) ** -0.5, 0.25, ((0, 32),), jnp.float32),
        "conv_gain": jnp.clip(1.0 + 0.1 * jax.random.normal(seeds[7], (C,), jnp.float32), 0.5, 1.5),
        "attention_gain": jnp.clip(1.0 + 0.1 * jax.random.normal(seeds[8], (D,), jnp.float32), 0.5, 1.5),
    }


EPS = 1e-05
ROOT_HALF = 0.7071067811865476
INV_ROOT_TWO_PI = 0.3989422804014327

def gelu_value(before):
    return before * 0.5 * (1.0 + jax.scipy.special.erf(before * ROOT_HALF))

def gelu_slope(before):
    cumulative = 0.5 * (1.0 + jax.scipy.special.erf(before * ROOT_HALF))
    return cumulative + before * INV_ROOT_TWO_PI * jnp.exp(-0.5 * before * before)

def rms_parts(stream):
    inverse = lax.rsqrt(lax.optimization_barrier(jnp.mean(stream * stream, axis=-1, keepdims=True)) + EPS)
    return (inverse, stream * inverse)

def sequence_grads(stream_low, upward_low, weights):
    conv_full, query_full, key_full, value_full, output_full, gain_one, gain_two = weights
    channels = conv_full.shape[0]
    width = conv_full.shape[1]
    reach = width // 2
    head_size = key_full.shape[1]
    heads = query_full.shape[1] // head_size
    stream = stream_low.astype(jnp.float32)
    upward = upward_low.astype(jnp.float32)
    length = stream.shape[0]
    inverse_one, normed_one = rms_parts(stream)
    before = normed_one[:, :channels] * gain_one
    hidden = gelu_value(before).astype(jnp.bfloat16)
    padded = jnp.pad(hidden, ((reach, reach), (0, 0)))
    conv_out = jnp.zeros((length, channels), jnp.float32)
    for offset in range(width):
        conv_out = conv_out + jnp.dot(padded[offset:offset + length], conv_full[:, offset, :], preferred_element_type=jnp.float32)
    middle = jnp.concatenate([stream[:, :channels] + conv_out, stream[:, channels:]], axis=1).astype(jnp.bfloat16)
    inverse_two, normed_two = rms_parts(middle.astype(jnp.float32))
    attn_in = (normed_two * gain_two).astype(jnp.bfloat16)
    queries = jnp.dot(attn_in, query_full, preferred_element_type=jnp.float32).astype(jnp.bfloat16)
    key_rows = jnp.dot(attn_in, key_full, preferred_element_type=jnp.float32).astype(jnp.bfloat16)
    value_rows = jnp.dot(attn_in, value_full, preferred_element_type=jnp.float32).astype(jnp.bfloat16)
    scale = head_size ** (-0.5)
    query_heads = queries.reshape(length, heads, head_size).astype(jnp.float32)
    key_wide = key_rows.astype(jnp.float32)
    value_wide = value_rows.astype(jnp.float32)
    scores = jnp.einsum('qhd,kd->hqk', query_heads, key_wide) * scale
    top = lax.optimization_barrier(jnp.max(scores, axis=-1, keepdims=True))
    raised = jnp.exp(scores - top)
    probs = raised / lax.optimization_barrier(jnp.sum(raised, axis=-1, keepdims=True))
    probs_low = probs.astype(jnp.bfloat16)
    attended = jnp.einsum('hqk,kd->qhd', probs_low.astype(jnp.float32), value_wide).reshape(length, heads * head_size).astype(jnp.bfloat16)
    output_term = jnp.dot(attended.T, upward_low, preferred_element_type=jnp.float32)
    attended_grad = jnp.dot(upward_low, output_full.T, preferred_element_type=jnp.float32).astype(jnp.bfloat16)
    grad_heads = attended_grad.reshape(length, heads, head_size).astype(jnp.float32)
    value_part = jnp.einsum('hqk,qhd->kd', probs_low.astype(jnp.float32), grad_heads)
    prob_grad = jnp.einsum('qhd,kd->hqk', grad_heads, value_wide)
    centre = lax.optimization_barrier(jnp.sum(probs * prob_grad, axis=-1, keepdims=True))
    score_grad = (probs * (prob_grad - centre) * scale).astype(jnp.bfloat16)
    query_grad_rows = jnp.einsum('hqk,kd->qhd', score_grad.astype(jnp.float32), key_wide).reshape(length, heads * head_size).astype(jnp.bfloat16)
    key_part = jnp.einsum('hqk,qhd->kd', score_grad.astype(jnp.float32), query_heads)
    key_grad_low = key_part.astype(jnp.bfloat16)
    value_grad_low = value_part.astype(jnp.bfloat16)
    attn_in_grad = jnp.dot(query_grad_rows, query_full.T, preferred_element_type=jnp.float32)
    attn_in_grad = attn_in_grad + jnp.dot(key_grad_low, key_full.T, preferred_element_type=jnp.float32)
    attn_in_grad = attn_in_grad + jnp.dot(value_grad_low, value_full.T, preferred_element_type=jnp.float32)
    query_term = jnp.dot(attn_in.T, query_grad_rows, preferred_element_type=jnp.float32)
    key_term = jnp.dot(attn_in.T, key_grad_low, preferred_element_type=jnp.float32)
    value_term = jnp.dot(attn_in.T, value_grad_low, preferred_element_type=jnp.float32)
    second_term = lax.optimization_barrier(jnp.sum(attn_in_grad * normed_two, axis=0))
    scaled_grad = attn_in_grad * gain_two
    middle_grad = upward + inverse_two * (scaled_grad - normed_two * lax.optimization_barrier(jnp.mean(scaled_grad * normed_two, axis=-1, keepdims=True)))
    conv_grad_low = middle_grad[:, :channels].astype(jnp.bfloat16)
    padded_grad = jnp.pad(conv_grad_low, ((reach, reach), (0, 0)))
    conv_term = jnp.stack([jnp.dot(padded[offset:offset + length].T, conv_grad_low, preferred_element_type=jnp.float32) for offset in range(width)], axis=1)
    hidden_grad = jnp.zeros((length, channels), jnp.float32)
    for offset in range(width):
        start = 2 * reach - offset
        hidden_grad = hidden_grad + jnp.dot(padded_grad[start:start + length], conv_full[:, offset, :].T, preferred_element_type=jnp.float32)
    before_grad = hidden_grad * gelu_slope(before)
    first_term = lax.optimization_barrier(jnp.sum(before_grad * normed_one[:, :channels], axis=0))
    lifted = before_grad * gain_one
    projected = lax.optimization_barrier(jnp.sum(lifted * normed_one[:, :channels], axis=-1, keepdims=True)) / stream.shape[1]
    widened = jnp.concatenate([lifted, jnp.zeros((length, stream.shape[1] - channels), jnp.float32)], axis=1)
    input_rows = (middle_grad + inverse_one * (widened - normed_one * projected)).astype(jnp.bfloat16)
    return (input_rows, (conv_term, query_term, key_term, value_term, output_term, first_term, second_term))

def reference(inputs, cotangent, conv_weight, query_weight, key_weight, value_weight, output_weight, conv_gain, attention_gain):
    weights = (conv_weight.astype(jnp.bfloat16), query_weight.astype(jnp.bfloat16), key_weight.astype(jnp.bfloat16), value_weight.astype(jnp.bfloat16), output_weight.astype(jnp.bfloat16), lax.optimization_barrier(conv_gain.astype(jnp.bfloat16)).astype(jnp.float32), lax.optimization_barrier(attention_gain.astype(jnp.bfloat16)).astype(jnp.float32))
    masters = (conv_weight, query_weight, key_weight, value_weight, output_weight, conv_gain, attention_gain)
    zeros = tuple((jnp.zeros(master.shape, jnp.float32) for master in masters))

    def step(carry, pair):
        input_rows, terms = sequence_grads(pair[0], pair[1], weights)
        return (tuple((total + term for total, term in zip(carry, terms))), input_rows)
    totals, input_grad = lax.scan(step, zeros, (inputs, cotangent))
    return (input_grad, totals[0], totals[1], totals[2], totals[3], totals[4], totals[5], totals[6])
```

```python
import jax
import jax.numpy as jnp
from jax import lax
from jax.experimental import pallas as pl
from jax.experimental.pallas import tpu as pltpu
from jax.sharding import Mesh
from jax.sharding import PartitionSpec as P

EPS = 1e-05
ROOT_HALF = 0.7071067811865476
INV_ROOT_TWO_PI = 0.3989422804014327
LOG2_E = 1.4426950408889634
AXES = ("xh", "z", "y", "xl", "core")
DP = ("xh", "z", "y")
SEQ = ("xl", "core")
F32 = jnp.float32
BF16 = jnp.bfloat16


def gelu_value(before):
    return before * 0.5 * (1.0 + lax.erf(before * ROOT_HALF))


def gelu_slope(before):
    cumulative = 0.5 * (1.0 + lax.erf(before * ROOT_HALF))
    return cumulative + before * INV_ROOT_TWO_PI * jnp.exp(-0.5 * before * before)


def rms_parts(stream):
    inverse = lax.rsqrt(jnp.mean(stream * stream, axis=-1, keepdims=True) + EPS)
    return (inverse, stream * inverse)


def rotate(block, axis, step):
    return lax.ppermute(block, axis, [(i, (i + step) % 4) for i in range(4)])


def swap(block, axis):
    return lax.ppermute(block, axis, [(0, 1), (1, 0)])


def swap_both(block, axes):
    return lax.ppermute(block, axes, [(i, 3 - i) for i in range(4)])


def gather_four(block, axis, dim):
    place = lax.axis_index(axis)
    shape = block.shape[:dim] + (4,) + block.shape[dim:]
    full = jnp.zeros(shape, block.dtype)
    for step in (0, 1, 3, 2):
        piece = block if step == 0 else rotate(block, axis, step)
        full = lax.dynamic_update_index_in_dim(full, piece, lax.rem(place + 4 - step, 4), dim)
    return full


def scatter_four(block, axis, dim):
    place = lax.axis_index(axis)
    total = lax.dynamic_index_in_dim(block, place, dim, keepdims=False).astype(F32)
    for step in (1, 3, 2):
        piece = lax.dynamic_index_in_dim(block, lax.rem(place + step, 4), dim, keepdims=False)
        total = total + rotate(piece, axis, step).astype(F32)
    return total.astype(BF16)


def sum_four(block, axis):
    total = block
    for step in (1, 3, 2):
        total = total + rotate(block, axis, step)
    return total


def pick(flag, first, second):
    return jnp.where(flag == 0, first, second)


def sum_over_x(low, high):
    place = lax.axis_index("xh")
    keep = pick(place, low, high)
    send = pick(place, high, low)
    near = keep.astype(F32) + swap(keep, "xl").astype(F32)
    far = swap(send, "xh").astype(F32) + swap_both(send, ("xh", "xl")).astype(F32)
    return near + far


def attention_kernel(q_ref, k_ref, v_ref, g_ref, o_ref, dq_ref, dk_ref, dv_ref, dk_sum, dv_sum):
    step = pl.program_id(0)
    scale = 128 ** (-0.5)
    q = q_ref[...]
    k = k_ref[...]
    v = v_ref[...]
    g = g_ref[...]
    nt = (((1,), (1,)), ((), ()))
    tn = (((0,), (0,)), ((), ()))
    scores = lax.dot_general(k, q, nt, preferred_element_type=F32)
    top = jnp.max(scores, axis=0, keepdims=True)
    raised = jnp.exp2((scores - top) * (scale * LOG2_E))
    probs = raised * (1.0 / jnp.sum(raised, axis=0, keepdims=True))
    probs_low = probs.astype(BF16)
    o_ref[...] = lax.dot_general(probs_low, v, tn, preferred_element_type=F32).astype(BF16)
    dv = lax.dot_general(probs_low, g, (((1,), (0,)), ((), ())), preferred_element_type=F32)
    dp = lax.dot_general(v, g, nt, preferred_element_type=F32)
    centre = jnp.sum(probs * dp, axis=0, keepdims=True)
    ds = (probs * ((dp - centre) * scale)).astype(BF16)
    dq_ref[...] = lax.dot_general(ds, k, tn, preferred_element_type=F32).astype(BF16)
    dk = lax.dot_general(ds, q, (((1,), (0,)), ((), ())), preferred_element_type=F32)

    @pl.when(step == 0)
    def _():
        dk_sum[...] = dk
        dv_sum[...] = dv

    @pl.when(step > 0)
    def _():
        dk_sum[...] += dk
        dv_sum[...] += dv

    @pl.when(step == pl.num_programs(0) - 1)
    def _():
        dk_ref[...] = dk_sum[...].astype(BF16)
        dv_ref[...] = dv_sum[...].astype(BF16)


def attention(queries, keys, values, grads, rows=256):
    length, wide = queries.shape
    total, size = keys.shape
    blocks = length // rows
    steps = blocks * (wide // size)
    row_spec = pl.BlockSpec((rows, size), lambda i: (i % blocks, i // blocks))
    full_spec = pl.BlockSpec((total, size), lambda i: (0, 0))
    return pl.pallas_call(
        attention_kernel,
        grid=(steps,),
        in_specs=[row_spec, full_spec, full_spec, row_spec],
        out_specs=[row_spec, row_spec, full_spec, full_spec],
        out_shape=[
            jax.ShapeDtypeStruct((length, wide), BF16),
            jax.ShapeDtypeStruct((length, wide), BF16),
            jax.ShapeDtypeStruct((total, size), BF16),
            jax.ShapeDtypeStruct((total, size), BF16),
        ],
        scratch_shapes=[pltpu.VMEM((total, size), F32), pltpu.VMEM((total, size), F32)],
        compiler_params=pltpu.CompilerParams(
            dimension_semantics=("arbitrary",), vmem_limit_bytes=48 * 1024 * 1024
        ),
        cost_estimate=pl.CostEstimate(
            flops=10 * length * wide * total, bytes_accessed=8 * length * wide, transcendentals=0
        ),
        name="attention",
    )(queries, keys, values, grads)


def on_device(
    inputs,
    cotangent,
    conv_weight,
    query_weight,
    key_weight,
    value_weight,
    output_weight,
    conv_gain,
    attention_gain,
):
    core = lax.axis_index("core")
    xl = lax.axis_index("xl")
    xh = lax.axis_index("xh")
    place = lax.axis_index(DP)
    rows_in, width, channels = conv_weight.shape
    half = channels // 2
    reach = width // 2
    length, model = inputs.shape[1:]
    head_size = key_weight.shape[1]
    query_size = query_weight.shape[1]
    rows_d = query_weight.shape[0]
    rows_o = output_weight.shape[0]
    upward_low = cotangent[0]
    stream_low = inputs[0]

    with jax.named_scope("gather_conv"):
        own = conv_weight.astype(BF16).transpose(1, 0, 2)
        own = pick(core, own[:, :, :half], own[:, :, half:])
        other = swap(own, "xh")
        low = gather_four(pick(xh, own, other), "y", 1)
        low = gather_four(low, "z", 1)
        high = gather_four(pick(xh, other, own), "z", 1)
        high = gather_four(high, "y", 2)
        conv_half = jnp.concatenate(
            [low.reshape(width, half, half), high.reshape(width, half, half)], axis=1
        )

    with jax.named_scope("gather_gains"):
        slot = lax.broadcasted_iota(jnp.int32, (32, rows_in + rows_d), 0)
        gains = jnp.concatenate([conv_gain, attention_gain]).astype(BF16)
        gains = jnp.where(slot == place, gains[None, :], jnp.zeros((), BF16))
        gains = sum_four(gains, "y")
        gains = sum_four(gains, "z")
        gains = (gains + swap(gains, "xh")).astype(F32)
        gain_one = gains[:, :rows_in].reshape(-1)
        gain_two = gains[:, rows_in:].reshape(-1)

    with jax.named_scope("gather_rest"):
        qkv = jnp.concatenate([query_weight, key_weight, value_weight], axis=1).astype(BF16)
        qkv = pick(core, qkv[:, :half], qkv[:, half:])
        out_low = output_weight.astype(BF16)
        out_low = pick(core, out_low[:, :channels], out_low[:, channels:])
        rest = jnp.concatenate([qkv, out_low[:, :half], out_low[:, half:]], axis=0)
        rest_other = swap(rest, "xh")
        rest = jnp.stack([pick(xh, rest, rest_other), pick(xh, rest_other, rest)])
        rest = lax.all_gather(rest, ("z", "y"), axis=1, tiled=False)
        rest_other = swap(rest, "core")
        rest = (pick(core, rest, rest_other), pick(core, rest_other, rest))
        qkv_full = jnp.concatenate(
            [r[:, :, :rows_d].reshape(model, half) for r in rest], axis=1
        )
        out_full = jnp.concatenate(
            [
                r[:, :, start : start + rows_o].reshape(-1, half)
                for r in rest
                for start in (rows_d, rows_d + rows_o)
            ],
            axis=1,
        )

    with jax.named_scope("hidden"):
        partner = swap(stream_low, "core")
        pair = jnp.concatenate(
            [pick(core, stream_low, partner), pick(core, partner, stream_low)], axis=0
        )
        edge = swap(pick(xl, pair[-reach:], pair[:reach]), "xl")
        blank = jnp.zeros_like(edge)
        pair = jnp.concatenate([pick(xl, blank, edge), pair, pick(xl, edge, blank)], axis=0)
        pair_wide = pair.astype(F32)
        _, pair_normed = rms_parts(pair_wide)
        hidden = gelu_value(pair_normed[:, :channels] * gain_one).astype(BF16)

    with jax.named_scope("conv"):
        conv_out = jnp.zeros((2 * length, half), F32)
        for offset in range(width):
            conv_out = conv_out + jnp.dot(
                hidden[offset : offset + 2 * length],
                conv_half[:, :, :][offset],
                preferred_element_type=F32,
            )
        inner = pair[reach : reach + 2 * length]
        middle_half = (
            pick(core, inner[:, :half], inner[:, half:channels]).astype(F32) + conv_out
        ).astype(BF16)
        keep = pick(core, middle_half[:length], middle_half[length:])
        sent = swap(pick(core, middle_half[length:], middle_half[:length]), "core")
        middle = jnp.concatenate(
            [pick(core, keep, sent), pick(core, sent, keep), stream_low[:, channels:]], axis=1
        )
        conv_other = swap(conv_half, "core")

    with jax.named_scope("project"):
        inverse_two, normed_two = rms_parts(middle.astype(F32))
        attn_in = (normed_two * gain_two).astype(BF16)
        kv = jnp.dot(attn_in, qkv_full[:, query_size:], preferred_element_type=F32).astype(BF16)
        queries = jnp.dot(attn_in, qkv_full[:, :query_size], preferred_element_type=F32).astype(BF16)
        attended_grad = lax.dot_general(
            upward_low, out_full, (((1,), (1,)), ((), ())), preferred_element_type=F32
        ).astype(BF16)

    with jax.named_scope("keys"):
        kv_all = jnp.concatenate(
            [kv, swap(kv, "core"), swap(kv, "xl"), swap_both(kv, SEQ)], axis=0
        )

    attended, query_grad_rows, key_part, value_part = attention(
        queries, kv_all[:, :head_size], kv_all[:, head_size:], attended_grad
    )

    with jax.named_scope("key_grads"):
        part = jnp.concatenate([key_part, value_part], axis=1)
        part = [part[i * length : (i + 1) * length] for i in range(4)]
        kv_sum = (
            part[0].astype(F32)
            + swap(part[1], "core").astype(F32)
            + swap(part[2], "xl").astype(F32)
            + swap_both(part[3], SEQ).astype(F32)
        )
        kv_grad_low = kv_sum.astype(BF16)

    with jax.named_scope("projection_grads"):
        tn = (((0,), (0,)), ((), ()))
        nt = (((1,), (1,)), ((), ()))
        output_term = lax.dot_general(attended, upward_low, tn, preferred_element_type=F32)
        query_term = lax.dot_general(attn_in, query_grad_rows, tn, preferred_element_type=F32)
        attn_in_grad = lax.dot_general(
            query_grad_rows, qkv_full[:, :query_size], nt, preferred_element_type=F32
        )
        attn_in_grad = attn_in_grad + lax.dot_general(
            kv_grad_low, qkv_full[:, query_size:], nt, preferred_element_type=F32
        )
        kv_term = lax.dot_general(attn_in, kv_grad_low, tn, preferred_element_type=F32)

    with jax.named_scope("reduce_rest"):
        qkv_term = jnp.concatenate([query_term, kv_term], axis=1).astype(BF16)
        out_term = output_term.astype(BF16)

        def packed(side):
            q_part = pick(side, qkv_term[:, :half], qkv_term[:, half:])
            o_part = pick(side, out_term[:, :channels], out_term[:, channels:])
            return jnp.concatenate(
                [
                    q_part.reshape(2, 4, 4, rows_d, half),
                    o_part[:, :half].reshape(2, 4, 4, rows_o, half),
                    o_part[:, half:].reshape(2, 4, 4, rows_o, half),
                ],
                axis=3,
            )

        rest_term = packed(core).astype(F32) + swap(packed(1 - core), "core").astype(F32)
        rest_term = rest_term.astype(BF16)
        low = scatter_four(scatter_four(rest_term[0], "z", 0), "y", 0)
        high = scatter_four(scatter_four(rest_term[1], "y", 1), "z", 0)
        rest_total = sum_over_x(low, high).astype(BF16)
        rest_other = swap(rest_total, "core")
        rest_pair = (
            pick(core, rest_total, rest_other).astype(F32),
            pick(core, rest_other, rest_total).astype(F32),
        )
        qkv_total = jnp.concatenate([r[:rows_d] for r in rest_pair], axis=1)
        output_total = jnp.concatenate(
            [
                r[start : start + rows_o]
                for r in rest_pair
                for start in (rows_d, rows_d + rows_o)
            ],
            axis=1,
        )

    with jax.named_scope("middle_grad"):
        second_term = jnp.sum(attn_in_grad * normed_two, axis=0)
        scaled_grad = attn_in_grad * gain_two
        middle_grad = upward_low.astype(F32) + inverse_two * (
            scaled_grad - normed_two * jnp.mean(scaled_grad * normed_two, axis=-1, keepdims=True)
        )
        conv_grad_low = middle_grad[:, :channels].astype(BF16)

    with jax.named_scope("conv_grad"):
        cg_keep = pick(core, conv_grad_low[:, :half], conv_grad_low[:, half:])
        cg_sent = swap(pick(core, conv_grad_low[:, half:], conv_grad_low[:, :half]), "core")
        cg_pair = jnp.concatenate(
            [pick(core, cg_keep, cg_sent), pick(core, cg_sent, cg_keep)], axis=0
        )
        conv_term = [
            lax.dot_general(
                hidden[offset : offset + 2 * length], cg_pair, tn, preferred_element_type=F32
            ).astype(BF16)
            for offset in range(width)
        ]

    with jax.named_scope("reduce_conv"):
        conv_term = jnp.stack(conv_term).reshape(width, 2, 4, 4, rows_in, half)
        low = scatter_four(scatter_four(conv_term[:, 0], "z", 1), "y", 1)
        high = scatter_four(scatter_four(conv_term[:, 1], "y", 2), "z", 1)
        conv_total = sum_over_x(low, high).astype(BF16)
        conv_total_other = swap(conv_total, "core")
        conv_total = jnp.concatenate(
            [pick(core, conv_total, conv_total_other), pick(core, conv_total_other, conv_total)],
            axis=2,
        )
        conv_total = conv_total.transpose(1, 0, 2).astype(F32)

    with jax.named_scope("hidden_grad"):
        before_edge = lax.ppermute(conv_grad_low[-reach:], SEQ, [(0, 1), (1, 2), (2, 3)])
        after_edge = lax.ppermute(conv_grad_low[:reach], SEQ, [(1, 0), (2, 1), (3, 2)])
        padded_grad = jnp.concatenate([before_edge, conv_grad_low, after_edge], axis=0)
        first_half = pick(core, conv_half, conv_other)
        second_half = pick(core, conv_other, conv_half)
        hidden_grad = jnp.zeros((length, channels), F32)
        for offset in range(width):
            start = 2 * reach - offset
            piece = padded_grad[start : start + length]
            hidden_grad = hidden_grad + lax.dot_general(
                piece[:, :half], first_half[offset], nt, preferred_element_type=F32
            )
            hidden_grad = hidden_grad + lax.dot_general(
                piece[:, half:], second_half[offset], nt, preferred_element_type=F32
            )

    with jax.named_scope("input_grad"):
        stream = stream_low.astype(F32)
        inverse_one, normed_one = rms_parts(stream)
        before = normed_one[:, :channels] * gain_one
        before_grad = hidden_grad * gelu_slope(before)
        first_term = jnp.sum(before_grad * normed_one[:, :channels], axis=0)
        lifted = before_grad * gain_one
        projected = jnp.sum(lifted * normed_one[:, :channels], axis=-1, keepdims=True) / model
        widened = jnp.concatenate(
            [lifted, jnp.zeros((length, model - channels), F32)], axis=1
        )
        input_rows = (middle_grad + inverse_one * (widened - normed_one * projected)).astype(BF16)

    with jax.named_scope("reduce_gains"):
        terms = jnp.concatenate(
            [first_term.reshape(32, rows_in), second_term.reshape(32, rows_d)], axis=1
        )
        terms = sum_four(terms, "y")
        terms = sum_four(terms, "z")
        terms = lax.dynamic_index_in_dim(terms, place, 0, keepdims=False) + lax.dynamic_index_in_dim(
            swap(terms, "xh"), place, 0, keepdims=False
        )
        terms = (terms + swap(terms, "core")).astype(F32)
        terms = terms + swap(terms, "xl")

    return (
        input_rows[None],
        conv_total,
        qkv_total[:, :query_size],
        qkv_total[:, query_size : query_size + head_size],
        qkv_total[:, query_size + head_size :],
        output_total,
        terms[:rows_in],
        terms[rows_in:],
    )


def solution(mesh):
    grid = Mesh(mesh.devices.reshape(2, 4, 4, 2, 2), AXES)
    in_specs = (
        P(DP, SEQ, None),
        P(DP, SEQ, None),
        P(DP, None, None),
        P(DP, None),
        P(DP, None),
        P(DP, None),
        P(DP, None),
        P(DP),
        P(DP),
    )
    out_specs = (
        P(DP, SEQ, None),
        P(DP, None, None),
        P(DP, None),
        P(DP, None),
        P(DP, None),
        P(DP, None),
        P(DP),
        P(DP),
    )
    return jax.shard_map(
        on_device, mesh=grid, in_specs=in_specs, out_specs=out_specs, check_vma=False
    )
```

```python
import jax
import jax.numpy as jnp
from jax import lax
from jax.experimental import pallas as pl
from jax.experimental.pallas import tpu as pltpu
from jax.sharding import Mesh
from jax.sharding import PartitionSpec as P

EPS = 1e-05
ROOT_HALF = 0.7071067811865476
INV_ROOT_TWO_PI = 0.3989422804014327
LOG2_E = 1.4426950408889634
AXES = ("xh", "z", "y", "xl", "core")
DP = ("xh", "z", "y")
SEQ = ("xl", "core")
F32 = jnp.float32
BF16 = jnp.bfloat16


def gelu_value(before):
    return before * 0.5 * (1.0 + lax.erf(before * ROOT_HALF))


def gelu_slope(before):
    cumulative = 0.5 * (1.0 + lax.erf(before * ROOT_HALF))
    return cumulative + before * INV_ROOT_TWO_PI * jnp.exp(-0.5 * before * before)


def rms_parts(stream):
    inverse = lax.rsqrt(jnp.mean(stream * stream, axis=-1, keepdims=True) + EPS)
    return (inverse, stream * inverse)


def rotate(block, axis, step):
    return lax.ppermute(block, axis, [(i, (i + step) % 4) for i in range(4)])


def swap(block, axis):
    return lax.ppermute(block, axis, [(0, 1), (1, 0)])


def swap_both(block, axes):
    return lax.ppermute(block, axes, [(i, 3 - i) for i in range(4)])


def scatter_four(block, axis, dim):
    place = lax.axis_index(axis)
    total = lax.dynamic_index_in_dim(block, place, dim, keepdims=False).astype(F32)
    for step in (1, 3, 2):
        piece = lax.dynamic_index_in_dim(block, lax.rem(place + step, 4), dim, keepdims=False)
        total = total + rotate(piece, axis, step).astype(F32)
    return total.astype(BF16)


def sum_four(block, axis):
    total = block
    for step in (1, 3, 2):
        total = total + rotate(block, axis, step)
    return total


def after(array, *others):
    for other in others:
        array = array + (other.reshape(-1)[0] * 0).astype(array.dtype)
    return array


def along(block, step, across):
    pairs = []
    for index in range(32):
        xh, z, y = index // 16, index // 4 % 4, index % 4
        if xh == 0:
            y = (y + step) % 4
        else:
            z = (z + step) % 4
        pairs.append((index, (xh ^ across) * 16 + z * 4 + y))
    return lax.ppermute(block, DP, pairs)


def crossing(block, step):
    pairs = []
    for index in range(32):
        xh, z, y = index // 16, index // 4 % 4, index % 4
        if xh == 0:
            z = (z + step) % 4
        else:
            y = (y + step) % 4
        pairs.append((index, (1 - xh) * 16 + z * 4 + y))
    return lax.ppermute(block, DP, pairs)


def pick(flag, first, second):
    return jnp.where(flag == 0, first, second)


def attention_kernel(q_ref, k_ref, v_ref, g_ref, o_ref, dq_ref, dk_ref, dv_ref, dk_sum, dv_sum):
    step = pl.program_id(0)
    scale = 128 ** (-0.5)
    q = q_ref[...]
    k = k_ref[...]
    v = v_ref[...]
    g = g_ref[...]
    nt = (((1,), (1,)), ((), ()))
    tn = (((0,), (0,)), ((), ()))
    scores = lax.dot_general(k, q, nt, preferred_element_type=F32)
    top = jnp.max(scores, axis=0, keepdims=True)
    raised = jnp.exp2((scores - top) * (scale * LOG2_E))
    probs = raised * (1.0 / jnp.sum(raised, axis=0, keepdims=True))
    probs_low = probs.astype(BF16)
    o_ref[...] = lax.dot_general(probs_low, v, tn, preferred_element_type=F32).astype(BF16)
    dv = lax.dot_general(probs_low, g, (((1,), (0,)), ((), ())), preferred_element_type=F32)
    dp = lax.dot_general(v, g, nt, preferred_element_type=F32)
    centre = jnp.sum(probs * dp, axis=0, keepdims=True)
    ds = (probs * ((dp - centre) * scale)).astype(BF16)
    dq_ref[...] = lax.dot_general(ds, k, tn, preferred_element_type=F32).astype(BF16)
    dk = lax.dot_general(ds, q, (((1,), (0,)), ((), ())), preferred_element_type=F32)

    @pl.when(step == 0)
    def _():
        dk_sum[...] = dk
        dv_sum[...] = dv

    @pl.when(step > 0)
    def _():
        dk_sum[...] += dk
        dv_sum[...] += dv

    @pl.when(step == pl.num_programs(0) - 1)
    def _():
        dk_ref[...] = dk_sum[...].astype(BF16)
        dv_ref[...] = dv_sum[...].astype(BF16)


def attention(queries, keys, values, grads, rows=256):
    length, wide = queries.shape
    total, size = keys.shape
    blocks = length // rows
    steps = blocks * (wide // size)
    row_spec = pl.BlockSpec((rows, size), lambda i: (i % blocks, i // blocks))
    full_spec = pl.BlockSpec((total, size), lambda i: (0, 0))
    return pl.pallas_call(
        attention_kernel,
        grid=(steps,),
        in_specs=[row_spec, full_spec, full_spec, row_spec],
        out_specs=[row_spec, row_spec, full_spec, full_spec],
        out_shape=[
            jax.ShapeDtypeStruct((length, wide), BF16),
            jax.ShapeDtypeStruct((length, wide), BF16),
            jax.ShapeDtypeStruct((total, size), BF16),
            jax.ShapeDtypeStruct((total, size), BF16),
        ],
        scratch_shapes=[pltpu.VMEM((total, size), F32), pltpu.VMEM((total, size), F32)],
        compiler_params=pltpu.CompilerParams(
            dimension_semantics=("arbitrary",), vmem_limit_bytes=48 * 1024 * 1024
        ),
        cost_estimate=pl.CostEstimate(
            flops=10 * length * wide * total, bytes_accessed=8 * length * wide, transcendentals=0
        ),
        name="attention",
    )(queries, keys, values, grads)


def prepare_kernel(place_ref, own_ref, partner_ref, edge_ref, *refs):
    pieces, (weight_ref, hidden_ref, gain_ref, wide, sems) = refs[:8], refs[8:]
    z, y, core, xl = [place_ref[i] for i in range(4)]
    copies = []
    for side in range(2):
        for step in range(4):
            for inner in range(4):
                first = lax.rem(z + 4 - (step if side == 0 else inner), 4)
                second = lax.rem(y + 4 - (inner if side == 0 else step), 4)
                copies.append(
                    pltpu.make_async_copy(
                        pieces[4 * side + step].at[inner],
                        weight_ref.at[side, first, second],
                        sems.at[len(copies)],
                    )
                )
    for copy in copies:
        copy.start()
    channels = hidden_ref.shape[1]
    length = own_ref.shape[0]
    for copy in copies:
        copy.wait()
    spare = weight_ref[:, :, :, :, weight_ref.shape[4] - 128 :].astype(F32)
    gains = spare.reshape(channels, 128).T[:8]
    gain_ref[...] = gains
    gain = gains[:1]

    def rows_of(rows):
        _, normed = rms_parts(rows.astype(F32))
        return gelu_value(normed[:, :channels] * gain)

    chunk = 128

    def body(i, carry):
        at = pl.multiple_of(i * chunk, chunk)
        wide[pl.ds(pl.multiple_of(8 + core * length + at, 8), chunk)] = rows_of(
            own_ref[pl.ds(at, chunk)]
        )
        wide[pl.ds(pl.multiple_of(8 + (1 - core) * length + at, 8), chunk)] = rows_of(
            partner_ref[pl.ds(at, chunk)]
        )
        return carry

    lax.fori_loop(0, length // chunk, body, 0)
    edge = rows_of(edge_ref[...])
    reach = edge.shape[0]
    wide[8 - reach : 8] = jnp.where(xl == 1, edge, 0.0)
    end = 8 + 2 * length
    wide[end : end + 16] = jnp.zeros((16, channels), F32)
    wide[end : end + reach] = jnp.where(xl == 0, edge, 0.0)
    for i in range(2 * length // chunk):
        start = 8 - reach + i * chunk
        hidden_ref[i * chunk : (i + 1) * chunk] = wide[start : start + chunk].astype(BF16)
    start = end - reach
    hidden_ref[2 * length : 2 * length + 16] = wide[start : start + 16].astype(BF16)


def prepare(place, own, partner, edge, pieces, channels):
    length = own.shape[0]
    smem = pl.BlockSpec(memory_space=pltpu.SMEM)
    vmem = pl.BlockSpec(memory_space=pltpu.VMEM)
    return pl.pallas_call(
        prepare_kernel,
        in_specs=[smem, vmem, vmem, vmem] + [pl.BlockSpec(memory_space=pl.ANY)] * 8,
        out_specs=[vmem, vmem, vmem],
        out_shape=[
            jax.ShapeDtypeStruct((2, 4) + pieces[0].shape, BF16),
            jax.ShapeDtypeStruct((2 * length + 16, channels), BF16),
            jax.ShapeDtypeStruct((8, channels), F32),
        ],
        scratch_shapes=[
            pltpu.VMEM((2 * length + 32, channels), F32),
            pltpu.SemaphoreType.DMA((32,)),
        ],
        compiler_params=pltpu.CompilerParams(vmem_limit_bytes=40 * 1024 * 1024),
        name="prepare",
    )(place, own, partner, edge, *pieces)


def input_kernel(
    core_ref,
    keep_ref,
    away_ref,
    before_ref,
    after_ref,
    weight_ref,
    other_ref,
    middle_ref,
    stream_ref,
    gain_ref,
    _,
    out_ref,
    term_ref,
    keep_wide,
    away_wide,
):
    step = pl.program_id(0)
    length, half = keep_ref.shape
    rows, model = stream_ref.shape
    channels = 2 * half
    reach = before_ref.shape[0]
    width = 2 * reach + 1
    second = core_ref[0] == 1

    @pl.when(step == 0)
    def _():
        for wide, rows_ref, flip in ((keep_wide, keep_ref, False), (away_wide, away_ref, True)):
            wide[8 : 8 + length] = rows_ref[...].astype(F32)
            for edge_ref, start in ((before_ref, 8 - reach), (after_ref, 8 + length)):
                edge = edge_ref[...].astype(F32)
                sides = (edge[:, :half], edge[:, half:])
                if flip:
                    sides = sides[::-1]
                wide[start : start + reach] = jnp.where(second, sides[1], sides[0])
        term_ref[...] = jnp.zeros(term_ref.shape, F32)

    at = pl.multiple_of(step * rows, rows)
    hidden_grad = jnp.zeros((rows, channels), F32)
    for wide, weights in ((keep_wide, weight_ref), (away_wide, other_ref)):
        block = wide[pl.ds(at, rows + 16)]
        for offset in range(width):
            start = 8 + reach - offset
            hidden_grad = hidden_grad + lax.dot_general(
                block[start : start + rows].astype(BF16),
                weights[:, offset * half : (offset + 1) * half],
                (((1,), (1,)), ((), ())),
                preferred_element_type=F32,
            )
    stream = stream_ref[...].astype(F32)
    inverse, normed = rms_parts(stream)
    gain = gain_ref[...]
    narrow = normed[:, :channels]
    before_grad = hidden_grad * gelu_slope(narrow * gain)
    term_ref[...] += jnp.sum((before_grad * narrow).reshape(rows // 8, 8, channels), axis=0)
    lifted = before_grad * gain
    projected = jnp.sum(lifted * narrow, axis=-1, keepdims=True) * (1.0 / model)
    out_ref[:, :channels] = (
        middle_ref[:, :channels] + inverse * (lifted - narrow * projected)
    ).astype(BF16)
    out_ref[:, channels:] = (
        middle_ref[:, channels:] - inverse * normed[:, channels:] * projected
    ).astype(BF16)


def input_gradient(core, keep, away, before, behind, weights, other, middle, stream, gain, term):
    length, model = stream.shape
    half = keep.shape[1]
    rows = 128
    vmem = pl.BlockSpec(memory_space=pltpu.VMEM)
    row_spec = pl.BlockSpec((rows, model), lambda i: (i, 0))
    input_rows, terms = pl.pallas_call(
        input_kernel,
        grid=(length // rows,),
        in_specs=[pl.BlockSpec(memory_space=pltpu.SMEM)]
        + [vmem] * 6
        + [row_spec, row_spec, vmem, pl.BlockSpec(memory_space=pl.ANY)],
        out_specs=[row_spec, pl.BlockSpec((8, 2 * half), lambda i: (0, 0))],
        out_shape=[
            jax.ShapeDtypeStruct((length, model), BF16),
            jax.ShapeDtypeStruct((8, 2 * half), F32),
        ],
        scratch_shapes=[pltpu.VMEM((length + 16, half), F32)] * 2,
        compiler_params=pltpu.CompilerParams(
            dimension_semantics=("arbitrary",), vmem_limit_bytes=40 * 1024 * 1024
        ),
        cost_estimate=pl.CostEstimate(
            flops=40 * length * half * half, bytes_accessed=16 * length * model, transcendentals=0
        ),
        name="input_gradient",
    )(
        core.reshape(1).astype(jnp.int32), keep, away, before, behind, weights, other, middle,
        stream, gain.reshape(1, -1), term,
    )
    return input_rows, jnp.sum(terms, axis=0)


def on_device(
    inputs,
    cotangent,
    conv_weight,
    query_weight,
    key_weight,
    value_weight,
    output_weight,
    conv_gain,
    attention_gain,
):
    core = lax.axis_index("core")
    xl = lax.axis_index("xl")
    xh = lax.axis_index("xh")
    place = lax.axis_index(DP)
    rows_in, width, channels = conv_weight.shape
    half = channels // 2
    reach = width // 2
    length, model = inputs.shape[1:]
    head_size = key_weight.shape[1]
    query_size = query_weight.shape[1]
    quarter = query_size // 2
    rows_d = query_weight.shape[0]
    rows_o = output_weight.shape[0]
    upward_low = cotangent[0]
    stream_low = inputs[0]
    tn = (((0,), (0,)), ((), ()))
    nt = (((1,), (1,)), ((), ()))

    def both(mine, other):
        return jnp.concatenate([pick(core, mine, other), pick(core, other, mine)], axis=0)

    def own_rows(array):
        return pick(core, array[:length], array[length:])

    def partner_rows(array):
        return pick(core, array[length:], array[:length])

    with jax.named_scope("gather_conv"):
        own = conv_weight.astype(BF16)
        own = pick(core, own[:, :, :half], own[:, :, half:]).reshape(rows_in, width * half)
        gains = jnp.concatenate(
            [
                conv_gain[:, None],
                attention_gain.reshape(rows_in, 2),
                jnp.zeros((rows_in, 125), F32),
            ],
            axis=1,
        )
        own = jnp.concatenate([own, gains.astype(BF16)], axis=1)
        near = [own] + [along(own, step, 0) for step in (1, 2, 3)]
        far = [along(own, step, 1) for step in (0, 1, 2, 3)]
        low = jnp.stack([pick(xh, near[i], far[i]) for i in range(4)])
        high = jnp.stack([pick(xh, far[i], near[i]) for i in range(4)])
        low = [low] + [rotate(low, "z", step) for step in (1, 2, 3)]
        high = [high] + [rotate(high, "y", step) for step in (1, 2, 3)]

    with jax.named_scope("gather_rest"):
        qkv = jnp.concatenate(
            [
                pick(core, query_weight[:, :quarter], query_weight[:, quarter:]),
                pick(core, key_weight, value_weight),
            ],
            axis=1,
        ).astype(BF16)
        rest = jnp.concatenate(
            [qkv] + [output_weight[:, i * half : (i + 1) * half].astype(BF16) for i in range(4)],
            axis=0,
        )
        rest = after(rest, own)
        rest_far = swap(rest, "xh")
        rest = jnp.concatenate(
            [
                pick(xh, rest[:rows_d], rest_far[:rows_d]),
                pick(xh, rest_far[:rows_d], rest[:rows_d]),
                pick(xh ^ core, rest[rows_d:], rest_far[rows_d:]),
            ],
            axis=0,
        )
        rest = lax.all_gather(rest, ("z", "y"), axis=0, tiled=False)
        qkv_half = rest[:, : 2 * rows_d].reshape(16, 2, rows_d, half)
        qkv_half = qkv_half.transpose(1, 0, 2, 3).reshape(model, half)
        out_half = rest[:, 2 * rows_d :].reshape(16, 4, rows_o, half)
        out_half = out_half.transpose(0, 2, 1, 3).reshape(16 * rows_o, model)

    with jax.named_scope("rows"):
        partner = swap(stream_low, "core")
        edge = after(pick(xl, stream_low[-reach:], stream_low[:reach]), own)
        edge = lax.ppermute(edge, SEQ, [(2, 0), (1, 3)]) + lax.ppermute(edge, SEQ, [(2, 1), (1, 2)])
        upward_pair = both(upward_low, swap(upward_low, "core"))
        inner = both(stream_low[:, :channels], partner[:, :channels])
        inner = pick(core, inner[:, :half], inner[:, half:])
        outer = both(stream_low[:, channels:], partner[:, channels:])

    spots = jnp.stack([lax.axis_index("z"), lax.axis_index("y"), core, xl]).astype(jnp.int32)
    conv_half, hidden, gains = prepare(spots, stream_low, partner, edge, low + high, channels)
    conv_half = conv_half.reshape(channels, -1)
    gain_one = gains[0]
    gain_two = gains[1:3].T.reshape(-1)

    def tap(array, offset):
        return array[:, offset * half : (offset + 1) * half]

    with jax.named_scope("conv"):
        conv_out = jnp.zeros((2 * length, half), F32)
        for offset in range(width):
            conv_out = conv_out + jnp.dot(
                hidden[offset : offset + 2 * length],
                tap(conv_half, offset),
                preferred_element_type=F32,
            )
        middle_half = (inner.astype(F32) + conv_out).astype(BF16)
        middle_other = swap(middle_half, "core")
        middle = jnp.concatenate(
            [
                pick(core, middle_half, middle_other),
                pick(core, middle_other, middle_half),
                outer,
            ],
            axis=1,
        )

    with jax.named_scope("project"):
        _, normed_pair = rms_parts(middle.astype(F32))
        attn_pair = (normed_pair * gain_two).astype(BF16)
        kv = jnp.dot(attn_pair, qkv_half[:, quarter:], preferred_element_type=F32).astype(BF16)
        queries = jnp.dot(attn_pair, qkv_half[:, :quarter], preferred_element_type=F32).astype(BF16)
        attended_grad = lax.dot_general(
            upward_pair, out_half, nt, preferred_element_type=F32
        ).astype(BF16)

    with jax.named_scope("keys"):
        kv_far = swap(kv, "xl")
        kv_mine = jnp.concatenate([kv, kv_far], axis=0)
        kv_other = jnp.concatenate([swap(kv, "core"), swap(kv_far, "core")], axis=0)
        keys = pick(core, kv_mine, kv_other)
        values = pick(core, kv_other, kv_mine)

    attended, query_grad_rows, key_part, value_part = attention(
        queries, keys, values, attended_grad
    )

    with jax.named_scope("key_grads"):
        kv_sum = pick(core, key_part, value_part).astype(F32) + swap(
            pick(core, value_part, key_part), "core"
        ).astype(F32)
        kv_sum = kv_sum.astype(BF16)
        kv_grad_low = (
            kv_sum[: 2 * length].astype(F32) + swap(kv_sum[2 * length :], "xl").astype(F32)
        ).astype(BF16)
        query_grad_other = swap(partner_rows(query_grad_rows), "core")
        kv_grad_other = swap(partner_rows(kv_grad_low), "core")

    with jax.named_scope("projection_grads"):
        output_low = lax.dot_general(
            attended, upward_pair, tn, preferred_element_type=F32
        ).astype(BF16)
        query_low = lax.dot_general(
            attn_pair, query_grad_rows, tn, preferred_element_type=F32
        ).astype(BF16)
        qkv_other = swap(qkv_half, "core")
        conv_other = swap(conv_half, "core")
        attn_in_grad = lax.dot_general(
            own_rows(query_grad_rows), qkv_half[:, :quarter], nt, preferred_element_type=F32
        )
        attn_in_grad = attn_in_grad + lax.dot_general(
            query_grad_other, qkv_other[:, :quarter], nt, preferred_element_type=F32
        )
        attn_in_grad = attn_in_grad + lax.dot_general(
            own_rows(kv_grad_low), qkv_half[:, quarter:], nt, preferred_element_type=F32
        )
        attn_in_grad = attn_in_grad + lax.dot_general(
            kv_grad_other, qkv_other[:, quarter:], nt, preferred_element_type=F32
        )

    with jax.named_scope("middle_grad"):
        inverse_two, normed_two = rms_parts(own_rows(middle).astype(F32))
        second_term = jnp.sum(attn_in_grad * normed_two, axis=0)
        scaled_grad = attn_in_grad * gain_two
        middle_grad = upward_low.astype(F32) + inverse_two * (
            scaled_grad - normed_two * jnp.mean(scaled_grad * normed_two, axis=-1, keepdims=True)
        )
        conv_grad_low = middle_grad[:, :channels].astype(BF16)

    with jax.named_scope("conv_grad"):
        cg_keep = pick(core, conv_grad_low[:, :half], conv_grad_low[:, half:])
        cg_away = pick(core, conv_grad_low[:, half:], conv_grad_low[:, :half])
        cg_pair = both(cg_keep, swap(cg_away, "core"))
        before_edge = lax.ppermute(conv_grad_low[-reach:], SEQ, [(0, 1), (1, 2), (2, 3)])
        after_edge = lax.ppermute(conv_grad_low[:reach], SEQ, [(1, 0), (2, 1), (3, 2)])

    with jax.named_scope("reduce_rest"):
        kv_low = lax.dot_general(
            attn_pair, kv_grad_low, tn, preferred_element_type=F32
        ).astype(BF16)
        qkv_low = jnp.concatenate([query_low, kv_low], axis=1).reshape(2, 4, 4, rows_d, half)
        out_blocks = output_low.reshape(4, 4, rows_o, model)
        rest = jnp.concatenate(
            [qkv_low[0], qkv_low[1]]
            + [out_blocks[..., i * half : (i + 1) * half] for i in range(4)],
            axis=2,
        )
        rest = lax.psum_scatter(rest, "z", scatter_dimension=0, tiled=False)
        rest = lax.psum_scatter(rest, "y", scatter_dimension=0, tiled=False)

    with jax.named_scope("conv_grad"):
        conv_term = jnp.stack(
            [
                lax.dot_general(
                    hidden[offset : offset + 2 * length], cg_pair, tn, preferred_element_type=F32
                ).astype(BF16)
                for offset in range(width)
            ]
        )

    with jax.named_scope("reduce_conv"):
        conv_blocks = conv_term.reshape(width, 2, 4, 4, rows_in, half)
        low = scatter_four(conv_blocks[:, 0], "z", 1)
        high = scatter_four(conv_blocks[:, 1], "y", 2)
        stage = low
        z = lax.axis_index("z")
        y = lax.axis_index("y")

        def piece(array, at):
            return lax.dynamic_index_in_dim(array, lax.rem(at, 4), 1, keepdims=False)

        conv_total = pick(xh, piece(low, y), piece(high, z)).astype(F32)
        for step in (1, 2, 3):
            near = pick(xh, piece(low, y + step), piece(high, z + step))
            conv_total = conv_total + along(near, step, 0).astype(F32)
        for step in (0, 1, 2, 3):
            conv_total = conv_total + crossing(
                pick(xh, piece(high, z + step), piece(low, y + step)), step
            ).astype(F32)
        conv_total = conv_total.astype(BF16)
        mine = conv_total.astype(F32) + swap(conv_total, "xl").astype(F32)
        other = swap(conv_total, "core").astype(F32) + swap_both(conv_total, SEQ).astype(F32)
        conv_total = jnp.concatenate([pick(core, mine, other), pick(core, other, mine)], axis=2)
        conv_total = conv_total.transpose(1, 0, 2)

    input_rows, first_term = input_gradient(
        core, cg_keep, cg_away, before_edge, after_edge, conv_half, conv_other, middle_grad,
        stream_low, gain_one, conv_term,
    )

    with jax.named_scope("reduce_gains"):
        terms = jnp.concatenate(
            [first_term.reshape(32, rows_in), second_term.reshape(32, rows_d)], axis=1
        )
        terms = after(terms, stage)
        terms = sum_four(terms, "y")
        terms = sum_four(terms, "z")
        terms = lax.dynamic_index_in_dim(terms, place, 0, keepdims=False) + lax.dynamic_index_in_dim(
            swap(terms, "xh"), place, 0, keepdims=False
        )
        terms = terms + swap(terms, "core")
        terms = terms + swap(terms, "xl")

    with jax.named_scope("reduce_rest"):
        rest = after(rest, stage)
        rest = (rest.astype(F32) + swap(rest, "xl").astype(F32)).astype(BF16)
        rest = (rest.astype(F32) + swap(rest, "xh").astype(F32)).astype(BF16)
        rest = jnp.concatenate(
            [pick(xh, rest[:rows_d], rest[rows_d : 2 * rows_d]), rest[2 * rows_d :]], axis=0
        )
        rest_other = swap(rest, "core")
        first = pick(core, rest, rest_other)
        second = pick(core, rest_other, rest)
        query_total = jnp.concatenate(
            [first[:rows_d, :quarter], second[:rows_d, :quarter]], axis=1
        ).astype(F32)
        key_total = first[:rows_d, quarter:].astype(F32)
        value_total = second[:rows_d, quarter:].astype(F32)
        out_rest = pick(xh, first, second)[rows_d:]
        output_total = jnp.concatenate(
            [out_rest[i * rows_o : (i + 1) * rows_o] for i in range(4)], axis=1
        ).astype(F32)

    return (
        input_rows[None],
        conv_total,
        query_total,
        key_total,
        value_total,
        output_total,
        terms[:rows_in],
        terms[rows_in:],
    )


def solution(mesh):
    grid = Mesh(mesh.devices.reshape(2, 4, 4, 2, 2), AXES)
    in_specs = (
        P(DP, SEQ, None),
        P(DP, SEQ, None),
        P(DP, None, None),
        P(DP, None),
        P(DP, None),
        P(DP, None),
        P(DP, None),
        P(DP),
        P(DP),
    )
    out_specs = (
        P(DP, SEQ, None),
        P(DP, None, None),
        P(DP, None),
        P(DP, None),
        P(DP, None),
        P(DP, None),
        P(DP),
        P(DP),
    )
    return jax.shard_map(
        on_device, mesh=grid, in_specs=in_specs, out_specs=out_specs, check_vma=False
    )
```

```python
import jax
import jax.numpy as jnp
from jax import lax
from jax.experimental import pallas as pl
from jax.experimental.pallas import tpu as pltpu
from jax.sharding import Mesh
from jax.sharding import PartitionSpec as P

EPS = 1e-05
ROOT_HALF = 0.7071067811865476
INV_ROOT_TWO_PI = 0.3989422804014327
LOG2_E = 1.4426950408889634
AXES = ("xh", "z", "y", "xl", "core")
DP = ("xh", "z", "y")
SEQ = ("xl", "core")
F32 = jnp.float32
BF16 = jnp.bfloat16


def gelu_value(before):
    return before * 0.5 * (1.0 + lax.erf(before * ROOT_HALF))


def gelu_slope(before):
    cumulative = 0.5 * (1.0 + lax.erf(before * ROOT_HALF))
    return cumulative + before * INV_ROOT_TWO_PI * jnp.exp(-0.5 * before * before)


def rms_parts(stream):
    inverse = lax.rsqrt(jnp.mean(stream * stream, axis=-1, keepdims=True) + EPS)
    return (inverse, stream * inverse)


def rotate(block, axis, step):
    return lax.ppermute(block, axis, [(i, (i + step) % 4) for i in range(4)])


def swap(block, axis):
    return lax.ppermute(block, axis, [(0, 1), (1, 0)])


def swap_both(block, axes):
    return lax.ppermute(block, axes, [(i, 3 - i) for i in range(4)])


def piece(array, at, dim):
    return lax.dynamic_index_in_dim(array, lax.rem(at, 4), dim, keepdims=False)


def scatter_ring(block, axis, dim):
    place = lax.axis_index(axis)
    total = piece(block, place, dim).astype(F32)
    for step in (2, 1, 3):
        total = total + rotate(piece(block, place + step, dim), axis, step).astype(F32)
    return total.astype(BF16)


def sum_four(block, axis):
    total = block
    for step in (1, 3, 2):
        total = total + rotate(block, axis, step)
    return total


def after(array, *others):
    for other in others:
        array = array + (other.reshape(-1)[0] * 0).astype(array.dtype)
    return array


def pick(flag, first, second):
    return jnp.where(flag == 0, first, second)


def attention_kernel(
    q_ref, k_ref, v_ref, g_ref, o_ref, dq_ref, dk_ref, dv_ref, dk_sum, dv_sum, k_turned, v_turned
):
    step = pl.program_id(0)
    scale = 128 ** (-0.5)

    @pl.when(step == 0)
    def _():
        k_turned[...] = k_ref[...].T
        v_turned[...] = v_ref[...].T

    q = q_ref[...]
    g = g_ref[...]
    nt = (((1,), (1,)), ((), ()))
    scores = lax.dot_general(k_ref[...], q, nt, preferred_element_type=F32)
    top = jnp.max(scores, axis=0, keepdims=True)
    raised = jnp.exp2((scores - top) * (scale * LOG2_E))
    probs = raised * (1.0 / jnp.sum(raised, axis=0, keepdims=True))
    probs_low = probs.astype(BF16)
    o_ref[...] = jnp.dot(v_turned[...], probs_low, preferred_element_type=F32).T.astype(BF16)
    dv = jnp.dot(probs_low, g, preferred_element_type=F32)
    dp = lax.dot_general(v_ref[...], g, nt, preferred_element_type=F32)
    centre = jnp.sum(probs * dp, axis=0, keepdims=True)
    ds = (probs * ((dp - centre) * scale)).astype(BF16)
    dq_ref[...] = jnp.dot(k_turned[...], ds, preferred_element_type=F32).T.astype(BF16)
    dk = jnp.dot(ds, q, preferred_element_type=F32)

    @pl.when(step == 0)
    def _():
        dk_sum[...] = dk
        dv_sum[...] = dv

    @pl.when(step > 0)
    def _():
        dk_sum[...] += dk
        dv_sum[...] += dv

    @pl.when(step == pl.num_programs(0) - 1)
    def _():
        dk_ref[...] = dk_sum[...].astype(BF16)
        dv_ref[...] = dv_sum[...].astype(BF16)


def attention(queries, keys, values, grads, rows=256):
    length, wide = queries.shape
    total, size = keys.shape
    blocks = length // rows
    steps = blocks * (wide // size)
    row_spec = pl.BlockSpec((rows, size), lambda i: (i % blocks, i // blocks))
    full_spec = pl.BlockSpec((total, size), lambda i: (0, 0))
    return pl.pallas_call(
        attention_kernel,
        grid=(steps,),
        in_specs=[row_spec, full_spec, full_spec, row_spec],
        out_specs=[row_spec, row_spec, full_spec, full_spec],
        out_shape=[
            jax.ShapeDtypeStruct((length, wide), BF16),
            jax.ShapeDtypeStruct((length, wide), BF16),
            jax.ShapeDtypeStruct((total, size), BF16),
            jax.ShapeDtypeStruct((total, size), BF16),
        ],
        scratch_shapes=[pltpu.VMEM((total, size), F32)] * 2 + [pltpu.VMEM((size, total), BF16)] * 2,
        compiler_params=pltpu.CompilerParams(
            dimension_semantics=("arbitrary",), vmem_limit_bytes=48 * 1024 * 1024
        ),
        cost_estimate=pl.CostEstimate(
            flops=10 * length * wide * total, bytes_accessed=8 * length * wide, transcendentals=0
        ),
        name="attention",
    )(queries, keys, values, grads)


def prepare_kernel(
    place_ref, own_ref, partner_ref, edge_ref, spare_ref, hidden_ref, gain_ref, wide
):
    core, xl = place_ref[0], place_ref[1]
    channels = hidden_ref.shape[1]
    length = own_ref.shape[0]
    gains = spare_ref[...].astype(F32).T[:8]
    gain_ref[...] = gains
    gain = gains[:1]

    def rows_of(rows):
        _, normed = rms_parts(rows.astype(F32))
        return gelu_value(normed[:, :channels] * gain)

    chunk = 128

    def body(i, carry):
        at = pl.multiple_of(i * chunk, chunk)
        wide[pl.ds(pl.multiple_of(8 + core * length + at, 8), chunk)] = rows_of(
            own_ref[pl.ds(at, chunk)]
        )
        wide[pl.ds(pl.multiple_of(8 + (1 - core) * length + at, 8), chunk)] = rows_of(
            partner_ref[pl.ds(at, chunk)]
        )
        return carry

    lax.fori_loop(0, length // chunk, body, 0)
    edge = rows_of(edge_ref[...])
    reach = edge.shape[0]
    wide[8 - reach : 8] = jnp.where(xl == 1, edge, 0.0)
    end = 8 + 2 * length
    wide[end : end + 16] = jnp.zeros((16, channels), F32)
    wide[end : end + reach] = jnp.where(xl == 0, edge, 0.0)
    for i in range(2 * length // chunk):
        start = 8 - reach + i * chunk
        hidden_ref[i * chunk : (i + 1) * chunk] = wide[start : start + chunk].astype(BF16)
    start = end - reach
    hidden_ref[2 * length : 2 * length + 16] = wide[start : start + 16].astype(BF16)


def prepare(place, own, partner, edge, weights):
    length = own.shape[0]
    channels, wide = weights.shape
    vmem = pl.BlockSpec(memory_space=pltpu.VMEM)
    return pl.pallas_call(
        prepare_kernel,
        grid=(1,),
        in_specs=[
            pl.BlockSpec(memory_space=pltpu.SMEM), vmem, vmem, vmem,
            pl.BlockSpec((channels, 128), lambda i: (0, wide // 128 - 1)),
        ],
        out_specs=[vmem, vmem],
        out_shape=[
            jax.ShapeDtypeStruct((2 * length + 16, channels), BF16),
            jax.ShapeDtypeStruct((8, channels), F32),
        ],
        scratch_shapes=[pltpu.VMEM((2 * length + 32, channels), F32)],
        compiler_params=pltpu.CompilerParams(vmem_limit_bytes=40 * 1024 * 1024),
        name="prepare",
    )(place, own, partner, edge, weights)


def input_kernel(
    core_ref,
    keep_ref,
    away_ref,
    before_ref,
    after_ref,
    weight_ref,
    other_ref,
    middle_ref,
    stream_ref,
    gain_ref,
    out_ref,
    term_ref,
    keep_wide,
    away_wide,
):
    step = pl.program_id(0)
    length, half = keep_ref.shape
    rows, model = stream_ref.shape
    channels = 2 * half
    reach = before_ref.shape[0]
    width = 2 * reach + 1
    second = core_ref[0] == 1

    @pl.when(step == 0)
    def _():
        for wide, rows_ref, flip in ((keep_wide, keep_ref, False), (away_wide, away_ref, True)):
            wide[8 : 8 + length] = rows_ref[...].astype(F32)
            for edge_ref, start in ((before_ref, 8 - reach), (after_ref, 8 + length)):
                edge = edge_ref[...].astype(F32)
                sides = (edge[:, :half], edge[:, half:])
                if flip:
                    sides = sides[::-1]
                wide[start : start + reach] = jnp.where(second, sides[1], sides[0])
        term_ref[...] = jnp.zeros(term_ref.shape, F32)

    at = pl.multiple_of(step * rows, rows)
    hidden_grad = jnp.zeros((rows, channels), F32)
    for wide, weights in ((keep_wide, weight_ref), (away_wide, other_ref)):
        block = wide[pl.ds(at, rows + 16)]
        for offset in range(width):
            start = 8 + reach - offset
            hidden_grad = hidden_grad + lax.dot_general(
                block[start : start + rows].astype(BF16),
                weights[:, offset * half : (offset + 1) * half],
                (((1,), (1,)), ((), ())),
                preferred_element_type=F32,
            )
    stream = stream_ref[...].astype(F32)
    inverse, normed = rms_parts(stream)
    gain = gain_ref[...]
    narrow = normed[:, :channels]
    before_grad = hidden_grad * gelu_slope(narrow * gain)
    term_ref[...] += jnp.sum((before_grad * narrow).reshape(rows // 8, 8, channels), axis=0)
    lifted = before_grad * gain
    projected = jnp.sum(lifted * narrow, axis=-1, keepdims=True) * (1.0 / model)
    out_ref[:, :channels] = (
        middle_ref[:, :channels] + inverse * (lifted - narrow * projected)
    ).astype(BF16)
    out_ref[:, channels:] = (
        middle_ref[:, channels:] - inverse * normed[:, channels:] * projected
    ).astype(BF16)


def input_gradient(core, keep, away, before, behind, weights, other, middle, stream, gain):
    length, model = stream.shape
    half = keep.shape[1]
    rows = 128
    vmem = pl.BlockSpec(memory_space=pltpu.VMEM)
    row_spec = pl.BlockSpec((rows, model), lambda i: (i, 0))
    input_rows, terms = pl.pallas_call(
        input_kernel,
        grid=(length // rows,),
        in_specs=[pl.BlockSpec(memory_space=pltpu.SMEM)]
        + [vmem] * 6
        + [row_spec, row_spec, vmem],
        out_specs=[row_spec, pl.BlockSpec((8, 2 * half), lambda i: (0, 0))],
        out_shape=[
            jax.ShapeDtypeStruct((length, model), BF16),
            jax.ShapeDtypeStruct((8, 2 * half), F32),
        ],
        scratch_shapes=[pltpu.VMEM((length + 16, half), F32)] * 2,
        compiler_params=pltpu.CompilerParams(
            dimension_semantics=("arbitrary",), vmem_limit_bytes=40 * 1024 * 1024
        ),
        cost_estimate=pl.CostEstimate(
            flops=40 * length * half * half, bytes_accessed=16 * length * model, transcendentals=0
        ),
        name="input_gradient",
    )(
        core.reshape(1).astype(jnp.int32), keep, away, before, behind, weights, other, middle,
        stream, gain.reshape(1, -1),
    )
    return input_rows, jnp.sum(terms, axis=0)


def project_kernel(
    core_ref, half_ref, other_ref, own_ref, partner_ref, gain_ref, rest_ref, up_ref,
    attn_ref, query_ref, kv_ref, grad_ref, qkv_ref, out_full,
):
    step = pl.program_id(0)
    rows, half = half_ref.shape
    model = own_ref.shape[1]
    steps = pl.num_programs(0)
    groups = model // 32
    quarter = query_ref.shape[1]
    share = quarter // 16

    @pl.when(step == 0)
    def _():
        for at in range(16):
            for side in range(2):
                start = side * (model // 2) + at * groups
                qkv_ref[start : start + groups] = rest_ref[at, :, side * half : (side + 1) * half]
            third = model // 3
            for part in range(3):
                out_full[at * share : (at + 1) * share, part * third : (part + 1) * third] = rest_ref[
                    at, part * share : (part + 1) * share, 2 * half : 2 * half + third
                ]

    second = core_ref[0] == 1
    mine = half_ref[...].astype(F32)
    other = other_ref[...].astype(F32)
    from_partner = (step >= steps // 2) != second
    at = lax.rem(step, steps // 2) * rows
    at = pl.multiple_of(at, rows)
    outer = jnp.where(
        from_partner,
        partner_ref[pl.ds(at, rows), 2 * half :].astype(F32),
        own_ref[pl.ds(at, rows), 2 * half :].astype(F32),
    )
    middle = jnp.concatenate(
        [jnp.where(second, other, mine), jnp.where(second, mine, other), outer], axis=1
    )
    _, normed = rms_parts(middle)
    attn = (normed * gain_ref[...]).astype(BF16)
    attn_ref[...] = attn
    both = jnp.dot(attn, qkv_ref[...], preferred_element_type=F32).astype(BF16)
    query_ref[...] = both[:, :quarter]
    kv_ref[...] = both[:, quarter:]
    grad_ref[...] = lax.dot_general(
        up_ref[...], out_full[...], (((1,), (1,)), ((), ())), preferred_element_type=F32
    ).astype(BF16)


def project(core, half_rows, other_rows, own, partner, gain, rest, upward, quarter):
    length, half = half_rows.shape
    model = own.shape[1]
    rows = 256
    vmem = pl.BlockSpec(memory_space=pltpu.VMEM)

    def by_rows(wide):
        return pl.BlockSpec((rows, wide), lambda i: (i, 0))

    return pl.pallas_call(
        project_kernel,
        grid=(length // rows,),
        in_specs=[
            pl.BlockSpec(memory_space=pltpu.SMEM), by_rows(half), by_rows(half), vmem, vmem, vmem,
            pl.BlockSpec(rest.shape[:2] + (2 * half + model // 3,), lambda i: (0, 0, 0)),
            by_rows(model),
        ],
        out_specs=[
            by_rows(model), by_rows(quarter), by_rows(half - quarter), by_rows(quarter),
            pl.BlockSpec((model, half), lambda i: (0, 0)),
        ],
        out_shape=[
            jax.ShapeDtypeStruct((length, wide), BF16)
            for wide in (model, quarter, half - quarter, quarter)
        ]
        + [jax.ShapeDtypeStruct((model, half), BF16)],
        scratch_shapes=[pltpu.VMEM((quarter, model), BF16)],
        compiler_params=pltpu.CompilerParams(
            dimension_semantics=("arbitrary",), vmem_limit_bytes=40 * 1024 * 1024
        ),
        cost_estimate=pl.CostEstimate(
            flops=2 * length * model * (half + quarter), bytes_accessed=8 * length * model,
            transcendentals=0,
        ),
        name="project",
    )(
        core.reshape(1).astype(jnp.int32), half_rows, other_rows, own, partner,
        gain.reshape(1, -1), rest, upward,
    )


def projection_kernel(attn_ref, query_ref, attended_ref, upward_ref, out_ref):
    tn = (((0,), (0,)), ((), ()))
    model = attn_ref.shape[1]
    wide = query_ref.shape[1]
    groups = model // 32
    for side in range(2):
        rows = model // 2
        term = lax.dot_general(
            attn_ref[:, side * rows : (side + 1) * rows],
            query_ref[...],
            tn,
            preferred_element_type=F32,
        ).astype(BF16)
        for at in range(16):
            out_ref[at // 4, at % 4, side * groups : (side + 1) * groups] = term[
                at * groups : (at + 1) * groups
            ]
    attended = attended_ref[...]
    share = wide // 16
    for block in range(model // wide):
        term = lax.dot_general(
            attended,
            upward_ref[:, block * wide : (block + 1) * wide],
            tn,
            preferred_element_type=F32,
        ).astype(BF16)
        start = 2 * groups + block * share
        for at in range(16):
            out_ref[at // 4, at % 4, start : start + share] = term[at * share : (at + 1) * share]


def projection_gradient(attn, queries, attended, upward):
    length, model = attn.shape
    wide = queries.shape[1]
    vmem = pl.BlockSpec(memory_space=pltpu.VMEM)
    return pl.pallas_call(
        projection_kernel,
        in_specs=[vmem] * 4,
        out_specs=vmem,
        out_shape=jax.ShapeDtypeStruct((4, 4, model // 8, wide), BF16),
        compiler_params=pltpu.CompilerParams(vmem_limit_bytes=40 * 1024 * 1024),
        cost_estimate=pl.CostEstimate(
            flops=4 * length * model * wide, bytes_accessed=8 * length * model, transcendentals=0
        ),
        name="projection_gradient",
    )(attn, queries, attended, upward)


def on_device(
    inputs,
    cotangent,
    conv_weight,
    query_weight,
    key_weight,
    value_weight,
    output_weight,
    conv_gain,
    attention_gain,
):
    core = lax.axis_index("core")
    xl = lax.axis_index("xl")
    xh = lax.axis_index("xh")
    place = lax.axis_index(DP)
    rows_in, width, channels = conv_weight.shape
    half = channels // 2
    reach = width // 2
    length, model = inputs.shape[1:]
    head_size = key_weight.shape[1]
    query_size = query_weight.shape[1]
    quarter = query_size // 2
    rows_d = query_weight.shape[0]
    rows_o = output_weight.shape[0]
    upward_low = cotangent[0]
    stream_low = inputs[0]
    tn = (((0,), (0,)), ((), ()))
    nt = (((1,), (1,)), ((), ()))

    def both(mine, other):
        return jnp.concatenate([pick(core, mine, other), pick(core, other, mine)], axis=0)

    def own_rows(array):
        return pick(core, array[:length], array[length:])

    def partner_rows(array):
        return pick(core, array[length:], array[:length])

    with jax.named_scope("gather_conv"):
        own = conv_weight.astype(BF16)
        own = pick(core, own[:, :, :half], own[:, :, half:]).reshape(rows_in, width * half)
        gains = jnp.concatenate(
            [
                conv_gain[:, None],
                attention_gain.reshape(rows_in, 2),
                jnp.zeros((rows_in, 125), F32),
            ],
            axis=1,
        )
        own = jnp.concatenate([own, gains.astype(BF16)], axis=1)

    with jax.named_scope("gather"):
        qkv = jnp.concatenate(
            [
                pick(core, query_weight[:, :quarter], query_weight[:, quarter:]),
                pick(core, key_weight, value_weight),
            ],
            axis=1,
        ).astype(BF16)
        third = model // 3
        out_low = jnp.concatenate(
            [output_weight[:, i * third : (i + 1) * third].astype(BF16) for i in range(3)], axis=0
        )
        block = jnp.concatenate(
            [qkv, out_low, jnp.concatenate([own[:, : 2 * third], own[:, 2 * third :]], axis=0)],
            axis=1,
        )
        far = swap(block, "xh")
        pair = [pick(xh, block, far), pick(xh, far, block)]
        start = half + third
        conv_pair = [
            jnp.concatenate(
                [b[:rows_in, start:], b[rows_in:, start:]], axis=1
            )
            for b in pair
        ]
        block = jnp.concatenate(
            [
                pair[0][:, :half],
                pair[1][:, :half],
                pick(xh ^ core, block[:, half:start], far[:, half:start]),
                jnp.concatenate(conv_pair, axis=0),
            ],
            axis=1,
        )
        block = lax.all_gather(block, ("z", "y"), axis=0, tiled=False)
        start = 2 * half + third
        conv_half = block[:, :, start:].reshape(16, 2, rows_in, -1)
        conv_half = conv_half.transpose(1, 0, 2, 3).reshape(channels, -1)

    with jax.named_scope("rows"):
        partner = swap(stream_low, "core")
        edge = after(pick(xl, stream_low[-reach:], stream_low[:reach]), own)
        edge = lax.ppermute(edge, SEQ, [(2, 0), (1, 3)]) + lax.ppermute(edge, SEQ, [(2, 1), (1, 2)])
        upward_pair = both(upward_low, swap(upward_low, "core"))
        inner = both(stream_low[:, :channels], partner[:, :channels])
        inner = pick(core, inner[:, :half], inner[:, half:])

    spots = jnp.stack([core, xl]).astype(jnp.int32)
    hidden, gains = prepare(spots, stream_low, partner, edge, conv_half)
    gain_one = gains[0]
    gain_two = gains[1:3].T.reshape(-1)

    def tap(array, offset):
        return array[:, offset * half : (offset + 1) * half]

    with jax.named_scope("conv"):
        conv_out = jnp.zeros((2 * length, half), F32)
        for offset in range(width):
            conv_out = conv_out + jnp.dot(
                hidden[offset : offset + 2 * length],
                tap(conv_half, offset),
                preferred_element_type=F32,
            )
        middle_half = (inner.astype(F32) + conv_out).astype(BF16)
        middle_other = swap(middle_half, "core")
        middle = jnp.concatenate(
            [
                own_rows(pick(core, middle_half, middle_other)),
                own_rows(pick(core, middle_other, middle_half)),
                stream_low[:, channels:],
            ],
            axis=1,
        )

    attn_pair, queries, kv, attended_grad, qkv_half = project(
        core, middle_half, middle_other, stream_low, partner, gain_two, block, upward_pair, quarter
    )

    with jax.named_scope("keys"):
        kv_far = swap(kv, "xl")
        kv_mine = jnp.concatenate([kv, kv_far], axis=0)
        kv_other = jnp.concatenate([swap(kv, "core"), swap(kv_far, "core")], axis=0)
        keys = pick(core, kv_mine, kv_other)
        values = pick(core, kv_other, kv_mine)

    attended, query_grad_rows, key_part, value_part = attention(
        queries, keys, values, attended_grad
    )

    with jax.named_scope("key_grads"):
        kv_sum = pick(core, key_part, value_part).astype(F32) + swap(
            pick(core, value_part, key_part), "core"
        ).astype(F32)
        kv_sum = kv_sum.astype(BF16)
        kv_grad_low = (
            kv_sum[: 2 * length].astype(F32) + swap(kv_sum[2 * length :], "xl").astype(F32)
        ).astype(BF16)
        query_grad_other = swap(partner_rows(query_grad_rows), "core")
        kv_grad_other = swap(partner_rows(kv_grad_low), "core")

    with jax.named_scope("projection_grads"):
        rest = projection_gradient(attn_pair, query_grad_rows, attended, upward_pair)
        rest_stage = lax.psum_scatter(rest, "z", scatter_dimension=0, tiled=False)
        rest = scatter_ring(rest_stage, "y", 0)
        qkv_other = swap(qkv_half, "core")
        conv_other = swap(conv_half, "core")
        attn_in_grad = lax.dot_general(
            own_rows(query_grad_rows), qkv_half[:, :quarter], nt, preferred_element_type=F32
        )
        attn_in_grad = attn_in_grad + lax.dot_general(
            query_grad_other, qkv_other[:, :quarter], nt, preferred_element_type=F32
        )
        attn_in_grad = attn_in_grad + lax.dot_general(
            own_rows(kv_grad_low), qkv_half[:, quarter:], nt, preferred_element_type=F32
        )
        attn_in_grad = attn_in_grad + lax.dot_general(
            kv_grad_other, qkv_other[:, quarter:], nt, preferred_element_type=F32
        )

    with jax.named_scope("middle_grad"):
        inverse_two, normed_two = rms_parts(middle.astype(F32))
        second_term = jnp.sum(attn_in_grad * normed_two, axis=0)
        scaled_grad = attn_in_grad * gain_two
        middle_grad = upward_low.astype(F32) + inverse_two * (
            scaled_grad - normed_two * jnp.mean(scaled_grad * normed_two, axis=-1, keepdims=True)
        )
        conv_grad_low = middle_grad[:, :channels].astype(BF16)

    with jax.named_scope("conv_grad"):
        cg_keep = pick(core, conv_grad_low[:, :half], conv_grad_low[:, half:])
        cg_away = pick(core, conv_grad_low[:, half:], conv_grad_low[:, :half])
        cg_pair = both(cg_keep, swap(cg_away, "core"))
        before_edge = lax.ppermute(conv_grad_low[-reach:], SEQ, [(0, 1), (1, 2), (2, 3)])
        after_edge = lax.ppermute(conv_grad_low[:reach], SEQ, [(1, 0), (2, 1), (3, 2)])

    with jax.named_scope("key_term"):
        kv_low = lax.dot_general(
            attn_pair, kv_grad_low, tn, preferred_element_type=F32
        ).astype(BF16)
        third = rows_d // 3
        kv_low = kv_low.reshape(2, 4, 4, 3, third, head_size)
        kv_low = jnp.concatenate([kv_low[:, :, :, i] for i in range(3)], axis=-1)
        kv_low = jnp.pad(kv_low, ((0, 0),) * 3 + ((0, rows_in - third), (0, 0)))

    with jax.named_scope("conv_grad"):
        conv_term = [
            lax.dot_general(
                hidden[offset : offset + 2 * length], cg_pair, tn, preferred_element_type=F32
            ).astype(BF16).reshape(2, 4, 4, rows_in, half)
            for offset in range(width)
        ]
        conv_term = jnp.stack(conv_term + [kv_low]).transpose(2, 3, 1, 0, 4, 5)

    with jax.named_scope("reduce_conv"):
        shares = lax.psum_scatter(
            conv_term.reshape(4, 4, -1, half), "z", scatter_dimension=0, tiled=False
        )
        shares = lax.psum_scatter(shares, "y", scatter_dimension=0, tiled=False)
        shares = shares.reshape(2, width + 1, rows_in, half)

    input_rows, first_term = input_gradient(
        core, cg_keep, cg_away, before_edge, after_edge, conv_half, conv_other, middle_grad,
        stream_low, gain_one,
    )

    with jax.named_scope("reduce_gains"):
        terms = jnp.concatenate(
            [first_term.reshape(32, rows_in), second_term.reshape(32, rows_d)], axis=1
        )
        terms = sum_four(terms, "y")
        terms = sum_four(terms, "z")
        terms = lax.dynamic_index_in_dim(terms, place, 0, keepdims=False) + lax.dynamic_index_in_dim(
            swap(terms, "xh"), place, 0, keepdims=False
        )
        terms = terms + swap(terms, "core")
        terms = terms + swap(terms, "xl")

    with jax.named_scope("reduce_conv"):
        total = pick(xh, shares[0], shares[1]).astype(F32)
        total = total + swap(pick(xh, shares[1], shares[0]), "xh").astype(F32)
        total = total.astype(BF16)
        mine = total.astype(F32) + swap(total, "xl").astype(F32)
        other = swap(total, "core").astype(F32) + swap_both(total, SEQ).astype(F32)
        first = pick(core, mine, other)
        second = pick(core, other, mine)
        conv_total = jnp.concatenate([first[:width], second[:width]], axis=2).transpose(1, 0, 2)
        key_total, value_total = [
            jnp.concatenate(
                [
                    side[width, :third, i * head_size : (i + 1) * head_size]
                    for i in range(3)
                ],
                axis=0,
            )
            for side in (first, second)
        ]

    with jax.named_scope("reduce_rest"):
        rest = (rest.astype(F32) + swap(rest, "xl").astype(F32)).astype(BF16)
        rest = (rest.astype(F32) + swap(rest, "xh").astype(F32)).astype(BF16)
        rest = jnp.concatenate(
            [pick(xh, rest[:rows_d], rest[rows_d : 2 * rows_d]), rest[2 * rows_d :]], axis=0
        )
        rest_other = swap(rest, "core")
        first = pick(core, rest, rest_other)
        second = pick(core, rest_other, rest)
        query_total = jnp.concatenate([first[:rows_d], second[:rows_d]], axis=1).astype(F32)
        out_rest = pick(xh, first, second)[rows_d:]
        output_total = jnp.concatenate(
            [out_rest[i * rows_o : (i + 1) * rows_o] for i in range(model // quarter)], axis=1
        ).astype(F32)

    return (
        input_rows[None],
        conv_total,
        query_total,
        key_total,
        value_total,
        output_total,
        terms[:rows_in],
        terms[rows_in:],
    )


def solution(mesh):
    grid = Mesh(mesh.devices.reshape(2, 4, 4, 2, 2), AXES)
    in_specs = (
        P(DP, SEQ, None),
        P(DP, SEQ, None),
        P(DP, None, None),
        P(DP, None),
        P(DP, None),
        P(DP, None),
        P(DP, None),
        P(DP),
        P(DP),
    )
    out_specs = (
        P(DP, SEQ, None),
        P(DP, None, None),
        P(DP, None),
        P(DP, None),
        P(DP, None),
        P(DP, None),
        P(DP),
        P(DP),
    )
    return jax.shard_map(
        on_device, mesh=grid, in_specs=in_specs, out_specs=out_specs, check_vma=False
    )
```

```python
import jax
import jax.numpy as jnp
from jax import lax
from jax.experimental import pallas as pl
from jax.experimental.pallas import tpu as pltpu
from jax.sharding import Mesh
from jax.sharding import PartitionSpec as P

EPS = 1e-05
ROOT_HALF = 0.7071067811865476
INV_ROOT_TWO_PI = 0.3989422804014327
LOG2_E = 1.4426950408889634
AXES = ("xh", "z", "y", "xl", "core")
DP = ("xh", "z", "y")
SEQ = ("xl", "core")
F32 = jnp.float32
BF16 = jnp.bfloat16


def gelu_value(before):
    return before * 0.5 * (1.0 + lax.erf(before * ROOT_HALF))


def gelu_slope(before):
    cumulative = 0.5 * (1.0 + lax.erf(before * ROOT_HALF))
    return cumulative + before * INV_ROOT_TWO_PI * jnp.exp(-0.5 * before * before)


def rms_parts(stream):
    inverse = lax.rsqrt(jnp.mean(stream * stream, axis=-1, keepdims=True) + EPS)
    return (inverse, stream * inverse)


def rotate(block, axis, step):
    return lax.ppermute(block, axis, [(i, (i + step) % 4) for i in range(4)])


def swap(block, axis):
    return lax.ppermute(block, axis, [(0, 1), (1, 0)])


def swap_both(block, axes):
    return lax.ppermute(block, axes, [(i, 3 - i) for i in range(4)])


def piece(array, at, dim):
    return lax.dynamic_index_in_dim(array, lax.rem(at, 4), dim, keepdims=False)


def scatter_ring(block, axis, dim):
    place = lax.axis_index(axis)
    total = piece(block, place, dim).astype(F32)
    for step in (2, 1, 3):
        total = total + rotate(piece(block, place + step, dim), axis, step).astype(F32)
    return total.astype(BF16)


def sum_four(block, axis):
    total = block
    for step in (1, 3, 2):
        total = total + rotate(block, axis, step)
    return total


def after(array, *others):
    for other in others:
        array = array + (other[(0,) * other.ndim] * 0).astype(array.dtype)
    return array


def pick(flag, first, second):
    return jnp.where(flag == 0, first, second)


def attention_kernel(
    core_ref, q_ref, near_ref, far_ref, near_other_ref, far_other_ref, g_ref,
    o_ref, dq_ref, keep_ref, away_ref,
    k_rows, v_rows, k_turned, v_turned, dk_sum, dv_sum,
):
    step = pl.program_id(0)
    scale = 128 ** (-0.5)
    first = core_ref[0] == 0
    rows = near_ref.shape[0]

    @pl.when(step == 0)
    def _():
        for start, mine_ref, other_ref in (
            (0, near_ref, near_other_ref), (rows, far_ref, far_other_ref)
        ):
            mine = mine_ref[...]
            other = other_ref[...]
            k = jnp.where(first, mine, other)
            v = jnp.where(first, other, mine)
            k_rows[start : start + rows] = k
            v_rows[start : start + rows] = v
            k_turned[:, start : start + rows] = k.T
            v_turned[:, start : start + rows] = v.T

    q = q_ref[...]
    g = g_ref[...]
    nt = (((1,), (1,)), ((), ()))
    scores = lax.dot_general(k_rows[...], q, nt, preferred_element_type=F32)
    top = jnp.max(scores, axis=0, keepdims=True)
    raised = jnp.exp2((scores - top) * (scale * LOG2_E))
    probs = raised * (1.0 / jnp.sum(raised, axis=0, keepdims=True))
    probs_low = probs.astype(BF16)
    o_ref[...] = jnp.dot(v_turned[...], probs_low, preferred_element_type=F32).T.astype(BF16)
    dv = jnp.dot(probs_low, g, preferred_element_type=F32)
    dp = lax.dot_general(v_rows[...], g, nt, preferred_element_type=F32)
    centre = jnp.sum(probs * dp, axis=0, keepdims=True)
    ds = (probs * ((dp - centre) * scale)).astype(BF16)
    dq_ref[...] = jnp.dot(k_turned[...], ds, preferred_element_type=F32).T.astype(BF16)
    dk = jnp.dot(ds, q, preferred_element_type=F32)

    @pl.when(step == 0)
    def _():
        dk_sum[...] = dk
        dv_sum[...] = dv

    @pl.when(step > 0)
    def _():
        dk_sum[...] += dk
        dv_sum[...] += dv

    @pl.when(step == pl.num_programs(0) - 1)
    def _():
        dk = dk_sum[...]
        dv = dv_sum[...]
        keep_ref[...] = jnp.where(first, dk, dv).astype(BF16)
        away_ref[...] = jnp.where(first, dv, dk).astype(BF16)


def attention(core, queries, near, far, near_other, far_other, grads, rows=512):
    length, wide = queries.shape
    half, size = near.shape
    total = 2 * half
    blocks = length // rows
    steps = blocks * (wide // size)
    row_spec = pl.BlockSpec((rows, size), lambda i: (i % blocks, i // blocks))
    full_spec = pl.BlockSpec((half, size), lambda i: (0, 0))
    return pl.pallas_call(
        attention_kernel,
        grid=(steps,),
        in_specs=[pl.BlockSpec(memory_space=pltpu.SMEM), row_spec]
        + [full_spec] * 4
        + [row_spec],
        out_specs=[row_spec] * 2 + [pl.BlockSpec((total, size), lambda i: (0, 0))] * 2,
        out_shape=[jax.ShapeDtypeStruct((length, wide), BF16)] * 2
        + [jax.ShapeDtypeStruct((total, size), BF16)] * 2,
        scratch_shapes=[pltpu.VMEM((total, size), BF16)] * 2
        + [pltpu.VMEM((size, total), BF16)] * 2
        + [pltpu.VMEM((total, size), F32)] * 2,
        compiler_params=pltpu.CompilerParams(
            dimension_semantics=("arbitrary",), vmem_limit_bytes=48 * 1024 * 1024
        ),
        cost_estimate=pl.CostEstimate(
            flops=10 * length * wide * total, bytes_accessed=8 * length * wide, transcendentals=0
        ),
        name="attention",
    )(core, queries, near, far, near_other, far_other, grads)


def prepare_kernel(
    place_ref, own_ref, partner_ref, edge_ref, gain_ref, hidden_ref, wide
):
    core, xl = place_ref[0], place_ref[1]
    channels = hidden_ref.shape[1]
    length = own_ref.shape[0]
    gain = gain_ref[...]

    def rows_of(rows):
        _, normed = rms_parts(rows.astype(F32))
        return gelu_value(normed[:, :channels] * gain)

    chunk = 128

    def body(i, carry):
        at = pl.multiple_of(i * chunk, chunk)
        wide[pl.ds(pl.multiple_of(8 + core * length + at, 8), chunk)] = rows_of(
            own_ref[pl.ds(at, chunk)]
        )
        wide[pl.ds(pl.multiple_of(8 + (1 - core) * length + at, 8), chunk)] = rows_of(
            partner_ref[pl.ds(at, chunk)]
        )
        return carry

    lax.fori_loop(0, length // chunk, body, 0)
    edge = rows_of(edge_ref[...])
    reach = edge.shape[0]
    wide[8 - reach : 8] = jnp.where(xl == 1, edge, 0.0)
    end = 8 + 2 * length
    wide[end : end + 16] = jnp.zeros((16, channels), F32)
    wide[end : end + reach] = jnp.where(xl == 0, edge, 0.0)
    for i in range(2 * length // chunk):
        start = 8 - reach + i * chunk
        hidden_ref[i * chunk : (i + 1) * chunk] = wide[start : start + chunk].astype(BF16)
    start = end - reach
    hidden_ref[2 * length : 2 * length + 16] = wide[start : start + 16].astype(BF16)
    hidden_ref[2 * length + 16 :] = jnp.zeros(
        (hidden_ref.shape[0] - 2 * length - 16, channels), BF16
    )


def prepare(place, own, partner, edge, gain):
    length = own.shape[0]
    channels = gain.shape[0]
    vmem = pl.BlockSpec(memory_space=pltpu.VMEM)
    return pl.pallas_call(
        prepare_kernel,
        in_specs=[pl.BlockSpec(memory_space=pltpu.SMEM)] + [vmem] * 4,
        out_specs=vmem,
        out_shape=jax.ShapeDtypeStruct((2 * length + 128, channels), BF16),
        scratch_shapes=[pltpu.VMEM((2 * length + 32, channels), F32)],
        compiler_params=pltpu.CompilerParams(vmem_limit_bytes=40 * 1024 * 1024),
        name="prepare",
    )(place, own, partner, edge, gain.reshape(1, -1))


def conv_kernel(hidden_ref, block_ref, inner_ref, middle_ref, weight_ref, shifted):
    length, half = inner_ref.shape
    rows = shifted.shape[0]
    channels, wide = weight_ref.shape
    group = channels // 32
    for pair in range(8):
        first = block_ref[2 * pair].astype(F32)
        second = block_ref[2 * pair + 1].astype(F32)
        for side in range(2):
            part = slice(side * group, (side + 1) * group)
            start = side * (channels // 2) + pair * 2 * group
            weight_ref[start : start + 2 * group] = jnp.concatenate(
                [first[part], second[part]], axis=0
            ).astype(BF16)
    hidden = hidden_ref[:rows]
    total = jnp.zeros((length, half), F32)
    for tap in range(wide // half):
        shifted[...] = jnp.dot(
            hidden, weight_ref[:, tap * half : (tap + 1) * half], preferred_element_type=F32
        )
        total = total + shifted[tap : tap + length]
    middle_ref[...] = (inner_ref[...].astype(F32) + total).astype(BF16)


def convolve(hidden, block, inner, taps):
    length, half = inner.shape
    channels = hidden.shape[1]
    vmem = pl.BlockSpec(memory_space=pltpu.VMEM)
    return pl.pallas_call(
        conv_kernel,
        grid=(1,),
        in_specs=[
            vmem,
            pl.BlockSpec(block.shape[:2] + (taps * half,), lambda i: (0, 0, 0)),
            vmem,
        ],
        out_specs=[vmem, vmem],
        out_shape=[
            jax.ShapeDtypeStruct((length, half), BF16),
            jax.ShapeDtypeStruct((channels, taps * half), BF16),
        ],
        scratch_shapes=[pltpu.VMEM((length + 16, half), F32)],
        compiler_params=pltpu.CompilerParams(vmem_limit_bytes=40 * 1024 * 1024),
        cost_estimate=pl.CostEstimate(
            flops=2 * taps * channels * half * length, bytes_accessed=8 * channels * channels,
            transcendentals=0,
        ),
        name="convolve",
    )(hidden, block, inner)


def input_kernel(
    keep_ref,
    away_ref,
    before_ref,
    after_ref,
    weight_ref,
    other_ref,
    middle_ref,
    stream_ref,
    gain_ref,
    out_ref,
    term_ref,
    keep_wide,
    away_wide,
):
    step = pl.program_id(0)
    length, half = keep_ref.shape
    rows, model = stream_ref.shape
    channels = 2 * half
    reach = before_ref.shape[0]
    width = 2 * reach + 1

    @pl.when(step == 0)
    def _():
        for wide, rows_ref, flip in ((keep_wide, keep_ref, False), (away_wide, away_ref, True)):
            wide[8 : 8 + length] = rows_ref[...].astype(F32)
            for edge_ref, start in ((before_ref, 8 - reach), (after_ref, 8 + length)):
                edge = edge_ref[...].astype(F32)
                wide[start : start + reach] = edge[:, :half] if flip else edge[:, half:]
        term_ref[...] = jnp.zeros(term_ref.shape, F32)

    at = pl.multiple_of(step * rows, rows)
    hidden_grad = jnp.zeros((rows, channels), F32)
    for wide, weights in ((keep_wide, weight_ref), (away_wide, other_ref)):
        block = wide[pl.ds(at, rows + 16)]
        for offset in range(width):
            start = 8 + reach - offset
            hidden_grad = hidden_grad + lax.dot_general(
                block[start : start + rows].astype(BF16),
                weights[:, offset * half : (offset + 1) * half],
                (((1,), (1,)), ((), ())),
                preferred_element_type=F32,
            )
    stream = stream_ref[...].astype(F32)
    inverse, normed = rms_parts(stream)
    gain = gain_ref[...]
    narrow = normed[:, :channels]
    before_grad = hidden_grad * gelu_slope(narrow * gain)
    term_ref[...] += jnp.sum((before_grad * narrow).reshape(rows // 8, 8, channels), axis=0)
    lifted = before_grad * gain
    projected = jnp.sum(lifted * narrow, axis=-1, keepdims=True) * (1.0 / model)
    out_ref[:, :channels] = (
        middle_ref[:, :channels] + inverse * (lifted - narrow * projected)
    ).astype(BF16)
    out_ref[:, channels:] = (
        middle_ref[:, channels:] - inverse * normed[:, channels:] * projected
    ).astype(BF16)


def input_gradient(keep, away, before, behind, weights, other, middle, stream, gain):
    length, model = stream.shape
    half = keep.shape[1]
    rows = 128
    vmem = pl.BlockSpec(memory_space=pltpu.VMEM)
    row_spec = pl.BlockSpec((rows, model), lambda i: (i, 0))
    input_rows, terms = pl.pallas_call(
        input_kernel,
        grid=(length // rows,),
        in_specs=[vmem] * 6
        + [row_spec, row_spec, vmem],
        out_specs=[row_spec, pl.BlockSpec((8, 2 * half), lambda i: (0, 0))],
        out_shape=[
            jax.ShapeDtypeStruct((length, model), BF16),
            jax.ShapeDtypeStruct((8, 2 * half), F32),
        ],
        scratch_shapes=[pltpu.VMEM((length + 16, half), F32)] * 2,
        compiler_params=pltpu.CompilerParams(
            dimension_semantics=("arbitrary",), vmem_limit_bytes=40 * 1024 * 1024
        ),
        cost_estimate=pl.CostEstimate(
            flops=40 * length * half * half, bytes_accessed=16 * length * model, transcendentals=0
        ),
        name="input_gradient",
    )(
        keep, away, before, behind, weights, other, middle,
        stream, gain.reshape(1, -1),
    )
    return input_rows, jnp.sum(terms, axis=0)


def project_kernel(
    core_ref, half_ref, other_ref, own_ref, partner_ref, gain_ref, rest_ref, last_ref,
    attn_ref, kv_ref, qkv_ref, out_full,
):
    step = pl.program_id(0)
    rows, half = half_ref.shape
    model = gain_ref.shape[1]
    steps = pl.num_programs(0)
    groups = model // 32
    quarter = half - kv_ref.shape[1]
    share = quarter // 16

    @pl.when(step == 0)
    def _():
        for at in range(16):
            rest = jnp.concatenate([rest_ref[at], last_ref[at]], axis=1)
            for side in range(2):
                start = side * (model // 2) + at * groups
                qkv_ref[start : start + groups] = rest[:, side * half : (side + 1) * half]
            third = model // 3
            for part in range(3):
                out_full[at * share : (at + 1) * share, part * third : (part + 1) * third] = rest[
                    part * share : (part + 1) * share, 2 * half :
                ]

    second = core_ref[0] == 1
    mine = half_ref[...].astype(F32)
    other = other_ref[...].astype(F32)
    outer = jnp.where(step >= steps // 2, partner_ref[...], own_ref[...]).astype(F32)
    middle = jnp.concatenate(
        [jnp.where(second, other, mine), jnp.where(second, mine, other), outer], axis=1
    )
    _, normed = rms_parts(middle)
    attn = (normed * gain_ref[...]).astype(BF16)
    attn_ref[...] = attn
    kv_ref[...] = jnp.dot(attn, qkv_ref[:, quarter:], preferred_element_type=F32).astype(BF16)


def project(core, half_rows, other_rows, own, partner, gain, rest, quarter):
    length, half = half_rows.shape
    model = own.shape[1]
    rows = 256
    vmem = pl.BlockSpec(memory_space=pltpu.VMEM)

    steps = length // rows

    def by_rows(wide):
        return pl.BlockSpec(
            (rows, wide), lambda i, core: (lax.rem(i + core[0] * (steps // 2), steps), 0)
        )

    def whole(first, second):
        return pl.BlockSpec((first, second), lambda i, core: (0, 0))

    outer = model - 2 * half
    part = rest.shape[:2] + (rest.shape[2] // 5,)
    return pl.pallas_call(
        project_kernel,
        grid_spec=pltpu.PrefetchScalarGridSpec(
            num_scalar_prefetch=1,
            grid=(steps,),
            in_specs=[
                by_rows(half), by_rows(half),
                pl.BlockSpec((rows, outer), lambda i, core: (lax.min(i, steps // 2 - 1), 1)),
                pl.BlockSpec((rows, outer), lambda i, core: (lax.max(i - steps // 2, 0), 1)),
                whole(1, model),
                pl.BlockSpec(part, lambda i, core: (0, 0, 3)),
                pl.BlockSpec(part, lambda i, core: (0, 0, 4)),
            ],
            out_specs=[
                by_rows(model), by_rows(half - quarter), whole(model, half), whole(quarter, model)
            ],
        ),
        out_shape=[
            jax.ShapeDtypeStruct((length, model), BF16),
            jax.ShapeDtypeStruct((length, half - quarter), BF16),
            jax.ShapeDtypeStruct((model, half), BF16),
            jax.ShapeDtypeStruct((quarter, model), BF16),
        ],
        compiler_params=pltpu.CompilerParams(
            dimension_semantics=("arbitrary",), vmem_limit_bytes=40 * 1024 * 1024
        ),
        cost_estimate=pl.CostEstimate(
            flops=2 * length * model * (half - quarter), bytes_accessed=8 * length * model,
            transcendentals=0,
        ),
        name="project",
    )(core, half_rows, other_rows, own, partner, gain.reshape(1, -1), rest, rest)


def projection_kernel(
    core_ref, attn_ref, query_ref, attended_ref, upward_ref, partner_ref, hidden_ref,
    out_ref, turned_ref,
):
    tn = (((0,), (0,)), ((), ()))
    model = attn_ref.shape[1]
    wide = query_ref.shape[1]
    half = out_ref.shape[3]
    groups = model // 32
    share = wide // 16
    for side in range(2):
        rows = model // 2
        term = lax.dot_general(
            attn_ref[:, side * rows : (side + 1) * rows],
            query_ref[...],
            tn,
            preferred_element_type=F32,
        ).astype(BF16)
        for at in range(16):
            start = at * groups
            line = jnp.concatenate(
                [term[start + i * share : start + (i + 1) * share] for i in range(3)], axis=1
            )
            for i in range(2):
                start = (2 * side + i) * share
                out_ref[at // 4, at % 4, start : start + share] = line[
                    :, i * half : (i + 1) * half
                ]
    length = upward_ref.shape[0]
    core = core_ref[0]
    own = attended_ref[pl.ds(pl.multiple_of(core * length, length), length)]
    partner = attended_ref[pl.ds(pl.multiple_of((1 - core) * length, length), length)]
    for block in range(model // half):
        columns = slice(block * half, (block + 1) * half)
        term = lax.dot_general(own, upward_ref[:, columns], tn, preferred_element_type=F32)
        term = term + lax.dot_general(
            partner, partner_ref[:, columns], tn, preferred_element_type=F32
        )
        term = term.astype(BF16)
        start = (4 + block) * share
        for at in range(16):
            out_ref[at // 4, at % 4, start : start + share] = term[at * share : (at + 1) * share]
    turned_ref[...] = hidden_ref[...].T


def projection_gradient(core, attn, queries, attended, upward, partner, hidden):
    length, model = attn.shape
    wide = queries.shape[1]
    vmem = pl.BlockSpec(memory_space=pltpu.VMEM)
    return pl.pallas_call(
        projection_kernel,
        in_specs=[pl.BlockSpec(memory_space=pltpu.SMEM)] + [vmem] * 6,
        out_specs=[vmem, vmem],
        out_shape=[
            jax.ShapeDtypeStruct((4, 4, 8 * wide // 16, model // 4), BF16),
            jax.ShapeDtypeStruct(hidden.shape[::-1], BF16),
        ],
        compiler_params=pltpu.CompilerParams(vmem_limit_bytes=48 * 1024 * 1024),
        cost_estimate=pl.CostEstimate(
            flops=1000, bytes_accessed=1000, transcendentals=0
        ),
        name="projection_gradient",
    )(core, attn, queries, attended, upward, partner, hidden)


def middle_kernel(
    core_ref, query_ref, query_other_ref, kv_ref, kv_other_ref, weight_ref, other_ref,
    middle_ref, upward_ref, gain_ref, grad_ref, keep_ref, away_ref, term_ref,
):
    step = pl.program_id(0)
    nt = (((1,), (1,)), ((), ()))
    rows, model = middle_ref.shape
    wide = query_ref.shape[1]
    half = keep_ref.shape[1]
    grad = jnp.zeros((rows, model), F32)
    for q_ref, k_ref, w_ref in (
        (query_ref, kv_ref, weight_ref), (query_other_ref, kv_other_ref, other_ref)
    ):
        grad = grad + lax.dot_general(
            q_ref[...], w_ref[:, :wide], nt, preferred_element_type=F32
        )
        grad = grad + lax.dot_general(
            k_ref[...], w_ref[:, wide:], nt, preferred_element_type=F32
        )
    inverse, normed = rms_parts(middle_ref[...].astype(F32))
    product = grad * normed

    @pl.when(step == 0)
    def _():
        term_ref[...] = jnp.zeros(term_ref.shape, F32)

    term_ref[...] += jnp.sum(product.reshape(rows // 8, 8, model), axis=0)
    gain = gain_ref[...]
    mean = jnp.mean(product * gain, axis=-1, keepdims=True)
    result = upward_ref[...].astype(F32) + inverse * (grad * gain - normed * mean)
    grad_ref[...] = result
    low = result[:, :half].astype(BF16)
    high = result[:, half : 2 * half].astype(BF16)
    second = core_ref[0] == 1
    keep_ref[...] = jnp.where(second, high, low)
    away_ref[...] = jnp.where(second, low, high)


def middle_gradient(
    core, queries, queries_other, kv, kv_other, weights, other, middle, upward, gain
):
    length, model = middle.shape
    half = weights.shape[1]
    rows = 128

    def by_rows(wide):
        return pl.BlockSpec((rows, wide), lambda i: (i, 0))

    vmem = pl.BlockSpec(memory_space=pltpu.VMEM)
    grads, keep, away, terms = pl.pallas_call(
        middle_kernel,
        grid=(length // rows,),
        in_specs=[
            pl.BlockSpec(memory_space=pltpu.SMEM),
            by_rows(queries.shape[1]), by_rows(queries.shape[1]),
            by_rows(kv.shape[1]), by_rows(kv.shape[1]),
            vmem, vmem, by_rows(model), by_rows(model), vmem,
        ],
        out_specs=[
            by_rows(model), by_rows(half), by_rows(half),
            pl.BlockSpec((8, model), lambda i: (0, 0)),
        ],
        out_shape=[
            jax.ShapeDtypeStruct((length, model), F32),
            jax.ShapeDtypeStruct((length, half), BF16),
            jax.ShapeDtypeStruct((length, half), BF16),
            jax.ShapeDtypeStruct((8, model), F32),
        ],
        compiler_params=pltpu.CompilerParams(
            dimension_semantics=("arbitrary",), vmem_limit_bytes=40 * 1024 * 1024
        ),
        cost_estimate=pl.CostEstimate(
            flops=4 * length * model * half, bytes_accessed=12 * length * model, transcendentals=0
        ),
        name="middle_gradient",
    )(
        core, queries, queries_other, kv, kv_other, weights, other, middle, upward,
        gain.reshape(1, -1),
    )
    return grads, keep, away, jnp.sum(terms, axis=0)


def conv_term_kernel(core_ref, turned_ref, keep_ref, sent_ref, kv_ref, out_ref, wide):
    length, half = keep_ref.shape
    span = turned_ref.shape[1]
    taps = out_ref.shape[3] - 1
    group = out_ref.shape[4]
    first = core_ref[0] == 0
    keep = keep_ref[...].astype(F32)
    sent = sent_ref[...].astype(F32)
    wide[:8] = jnp.zeros((8, half), F32)
    wide[8 : 8 + length] = jnp.where(first, keep, sent)
    wide[8 + length : 8 + 2 * length] = jnp.where(first, sent, keep)
    wide[8 + 2 * length :] = jnp.zeros((span - 2 * length, half), F32)
    for tap in range(taps):
        shifted = wide[8 - tap : 8 - tap + span].astype(BF16)
        term = jnp.dot(turned_ref[...], shifted, preferred_element_type=F32)
        for at in range(32):
            out_ref[at // 4 % 4, at % 4, at // 16, tap] = term[
                at * group : (at + 1) * group
            ].astype(BF16)
    for at in range(32):
        out_ref[at // 4 % 4, at % 4, at // 16, taps] = kv_ref[at // 16, at // 4 % 4, at % 4]


def conv_terms(core, turned, keep, sent, kv, taps):
    channels, span = turned.shape
    length, half = keep.shape
    vmem = pl.BlockSpec(memory_space=pltpu.VMEM)
    return pl.pallas_call(
        conv_term_kernel,
        in_specs=[pl.BlockSpec(memory_space=pltpu.SMEM)] + [vmem] * 4,
        out_specs=vmem,
        out_shape=jax.ShapeDtypeStruct((4, 4, 2, taps + 1, channels // 32, half), BF16),
        scratch_shapes=[pltpu.VMEM((span + 8, half), F32)],
        compiler_params=pltpu.CompilerParams(vmem_limit_bytes=40 * 1024 * 1024),
        cost_estimate=pl.CostEstimate(
            flops=2 * taps * channels * half * span, bytes_accessed=4 * channels * span,
            transcendentals=0,
        ),
        name="conv_terms",
    )(core, turned, keep, sent, kv)


def on_device(
    inputs,
    cotangent,
    conv_weight,
    query_weight,
    key_weight,
    value_weight,
    output_weight,
    conv_gain,
    attention_gain,
):
    core = lax.axis_index("core")
    xl = lax.axis_index("xl")
    xh = lax.axis_index("xh")
    place = lax.axis_index(DP)
    rows_in, width, channels = conv_weight.shape
    half = channels // 2
    reach = width // 2
    length, model = inputs.shape[1:]
    head_size = key_weight.shape[1]
    query_size = query_weight.shape[1]
    quarter = query_size // 2
    rows_d = query_weight.shape[0]
    rows_o = output_weight.shape[0]
    upward_low = cotangent[0]
    stream_low = inputs[0]
    tn = (((0,), (0,)), ((), ()))
    nt = (((1,), (1,)), ((), ()))

    def both(mine, other):
        return jnp.concatenate([pick(core, mine, other), pick(core, other, mine)], axis=0)

    def own_rows(array):
        return pick(core, array[:length], array[length:])

    def partner_rows(array):
        return pick(core, array[length:], array[:length])

    with jax.named_scope("gather_conv"):
        own = conv_weight.astype(BF16)
        own = pick(core, own[:, :, :half], own[:, :, half:]).reshape(rows_in, width * half)
        own = jnp.pad(own, ((0, 0), (0, 128)))

    with jax.named_scope("gather"):
        qkv = jnp.concatenate(
            [
                pick(core, query_weight[:, :quarter], query_weight[:, quarter:]),
                pick(core, key_weight, value_weight),
            ],
            axis=1,
        ).astype(BF16)
        third = model // 3
        out_low = jnp.concatenate(
            [output_weight[:, i * third : (i + 1) * third].astype(BF16) for i in range(3)], axis=0
        )
        block = jnp.concatenate(
            [qkv, out_low, jnp.concatenate([own[:, : 2 * third], own[:, 2 * third :]], axis=0)],
            axis=1,
        )
        far = swap(block, "xh")
        pair = [pick(xh, block, far), pick(xh, far, block)]
        start = half + third
        left = width * half - 2 * third
        conv_pair = [
            jnp.concatenate([b[:rows_in, start:], b[rows_in:, start : start + left]], axis=1)
            for b in pair
        ]
        block = jnp.concatenate(
            [
                jnp.concatenate(conv_pair, axis=0),
                pair[0][:, :half],
                pair[1][:, :half],
                pick(xh ^ core, block[:, half:start], far[:, half:start]),
            ],
            axis=1,
        )
        own_block = block
        block = lax.all_gather(block, ("z", "y"), axis=0, tiled=False)

    with jax.named_scope("rows"):
        partner = swap(stream_low, "core")
        edge = after(pick(xl, stream_low[-reach:], stream_low[:reach]), own)
        edge = lax.ppermute(edge, SEQ, [(2, 0), (1, 3)]) + lax.ppermute(edge, SEQ, [(2, 1), (1, 2)])
        upward_partner = swap(upward_low, "core")
        inner = both(stream_low[:, :channels], partner[:, :channels])
        inner = pick(core, inner[:, :half], inner[:, half:])

    core_at = core.reshape(1).astype(jnp.int32)
    spots = jnp.stack([core, xl]).astype(jnp.int32)
    with jax.named_scope("gather_gains"):
        slot = lax.broadcasted_iota(jnp.int32, (32, rows_in + rows_d), 0)
        gains = jnp.concatenate([conv_gain, attention_gain]).astype(BF16)
        gains = after(gains, own_block)
        gains = jnp.where(slot == place, gains[None, :], jnp.zeros((), BF16))
        gains = sum_four(gains, "y")
        gains = sum_four(gains, "z")
        gains = (gains + swap(gains, "xh")).astype(F32)
        gain_one = gains[:, :rows_in].reshape(-1)
        gain_two = gains[:, rows_in:].reshape(-1)
    hidden = prepare(spots, stream_low, partner, edge, gain_one)
    with jax.named_scope("conv"):
        middle_half, conv_half = convolve(hidden, block, inner, width)
        middle_other = swap(middle_half, "core")
        middle = jnp.concatenate(
            [
                own_rows(pick(core, middle_half, middle_other)),
                own_rows(pick(core, middle_other, middle_half)),
                stream_low[:, channels:],
            ],
            axis=1,
        )

    attn_pair, kv, qkv_half, out_half = project(
        core_at, middle_half, middle_other, stream_low, partner, gain_two, block, quarter
    )

    with jax.named_scope("project"):
        queries = jnp.dot(attn_pair, qkv_half[:, :quarter], preferred_element_type=F32).astype(BF16)
        upward_pair = both(upward_low, upward_partner)
        attended_grad = lax.dot_general(
            upward_pair, out_half, nt, preferred_element_type=F32
        ).astype(BF16)

    with jax.named_scope("keys"):
        kv_far = swap(kv, "xl")
        kv_near_other = swap(kv, "core")
        kv_far_other = swap(kv_far, "core")

    attended, query_grad_rows, kv_keep, kv_away = attention(
        core_at, queries, kv, kv_far, kv_near_other, kv_far_other, attended_grad
    )

    with jax.named_scope("key_grads"):
        kv_sum = (kv_keep.astype(F32) + swap(kv_away, "core").astype(F32)).astype(BF16)
        kv_grad_low = (
            kv_sum[: 2 * length].astype(F32) + swap(kv_sum[2 * length :], "xl").astype(F32)
        ).astype(BF16)
        query_grad_other = swap(partner_rows(query_grad_rows), "core")
        kv_grad_other = swap(partner_rows(kv_grad_low), "core")

    with jax.named_scope("projection_grads"):
        qkv_other = swap(qkv_half, "core")
        conv_other = swap(conv_half, "core")
        rest, hidden_turned = projection_gradient(
            after(core_at, kv_sum, conv_other, qkv_other), attn_pair, query_grad_rows, attended, upward_low,
            upward_partner, hidden,
        )
        rest = lax.psum_scatter(rest, "z", scatter_dimension=0, tiled=False)

    middle_grad, cg_keep, cg_away, second_term = middle_gradient(
        core_at, own_rows(query_grad_rows), query_grad_other, own_rows(kv_grad_low), kv_grad_other,
        qkv_half, qkv_other, middle, upward_low, gain_two,
    )

    with jax.named_scope("conv_grad"):
        cg_sent = swap(cg_away, "core")

        def ends(rows):
            return jnp.concatenate([cg_keep[rows], cg_away[rows]], axis=1)

        after_edge = lax.ppermute(ends(slice(0, reach)), SEQ, [(1, 0), (2, 1), (3, 2)])
        before_edge = lax.ppermute(ends(slice(length - reach, length)), SEQ, [(0, 1), (1, 2), (2, 3)])

    with jax.named_scope("key_term"):
        kv_low = lax.dot_general(
            attn_pair, kv_grad_low, tn, preferred_element_type=F32
        ).astype(BF16)
        third = rows_d // 3
        kv_low = kv_low.reshape(2, 4, 4, 3, third, head_size)
        kv_low = jnp.concatenate([kv_low[:, :, :, i] for i in range(3)], axis=-1)
        kv_low = jnp.pad(kv_low, ((0, 0),) * 3 + ((0, rows_in - third), (0, 0)))

    conv_term = conv_terms(core_at, hidden_turned, cg_keep, cg_sent, kv_low, width)

    with jax.named_scope("reduce_conv"):
        shares = lax.psum_scatter(
            conv_term.reshape(4, 4, -1, half), "z", scatter_dimension=0, tiled=False
        )

    input_rows, first_term = input_gradient(
        cg_keep, cg_away, before_edge, after_edge, conv_half, conv_other, middle_grad,
        stream_low, gain_one,
    )

    with jax.named_scope("reduce_gains"):
        terms = jnp.concatenate(
            [first_term.reshape(32, rows_in), second_term.reshape(32, rows_d)], axis=1
        )
        terms = sum_four(terms, "z").reshape(2, 4, 4, rows_in + rows_d)
        terms = lax.dynamic_index_in_dim(terms, lax.axis_index("z"), 1, keepdims=False)
        terms = terms.transpose(1, 0, 2)[:, :, None].astype(BF16)
        terms = jnp.pad(terms, ((0, 0), (0, 0), (0, 7), (0, half - rows_in - rows_d)))
        terms = terms.reshape(4, 16, half)

    with jax.named_scope("reduce_all"):
        rest = scatter_ring(rest, "y", 0)
        everything = scatter_ring(jnp.concatenate([shares, terms], axis=1), "y", 0)
        conv_both = 2 * (width + 1) * rows_in
        everything = jnp.concatenate(
            [everything[:conv_both], rest, everything[conv_both:]], axis=0
        )
        conv_rows = (width + 1) * rows_in
        query_rows = rows_d * quarter // half
        out_rows = rows_o * model // half
        sides = []
        start = 0
        for rows in (conv_rows, query_rows, out_rows, 8):
            if rows == out_rows:
                sides.append((everything[start : start + rows],) * 2)
                start += rows
            else:
                sides.append(
                    (everything[start : start + rows], everything[start + rows : start + 2 * rows])
                )
                start += 2 * rows
        keep = jnp.concatenate([pick(xh, a, b) for a, b in sides], axis=0)
        send = jnp.concatenate([pick(xh, b, a) for a, b in sides], axis=0)
        total = (keep.astype(F32) + swap(send, "xh").astype(F32)).astype(BF16)
        mine = total.astype(F32) + swap(total, "xl").astype(F32)
        other = swap(total, "core").astype(F32) + swap_both(total, SEQ).astype(F32)
        first = pick(core, mine, other)
        second = pick(core, other, mine)

        def conv_of(side):
            return side[: width * rows_in].reshape(width, rows_in, half)

        conv_total = jnp.concatenate([conv_of(first), conv_of(second)], axis=2).transpose(1, 0, 2)
        start = width * rows_in
        key_total, value_total = [
            jnp.concatenate(
                [
                    side[start : start + third, i * head_size : (i + 1) * head_size]
                    for i in range(3)
                ],
                axis=0,
            )
            for side in (first, second)
        ]

        def query_of(side):
            line = jnp.concatenate(
                [side[conv_rows : conv_rows + rows_o], side[conv_rows + rows_o : conv_rows + query_rows]],
                axis=1,
            )
            return jnp.concatenate(
                [line[:, i * quarter : (i + 1) * quarter] for i in range(3)], axis=0
            )

        query_total = jnp.concatenate([query_of(first), query_of(second)], axis=1)
        start = conv_rows + query_rows
        out_total = pick(xh, first, second)[start : start + out_rows]
        output_total = jnp.concatenate(
            [out_total[i * rows_o : (i + 1) * rows_o] for i in range(model // half)], axis=1
        )
        terms = (first + second)[start + out_rows, : rows_in + rows_d]

    return (
        input_rows[None],
        conv_total,
        query_total,
        key_total,
        value_total,
        output_total,
        terms[:rows_in],
        terms[rows_in:],
    )


def solution(mesh):
    grid = Mesh(mesh.devices.reshape(2, 4, 4, 2, 2), AXES)
    in_specs = (
        P(DP, SEQ, None),
        P(DP, SEQ, None),
        P(DP, None, None),
        P(DP, None),
        P(DP, None),
        P(DP, None),
        P(DP, None),
        P(DP),
        P(DP),
    )
    out_specs = (
        P(DP, SEQ, None),
        P(DP, None, None),
        P(DP, None),
        P(DP, None),
        P(DP, None),
        P(DP, None),
        P(DP),
        P(DP),
    )
    return jax.shard_map(
        on_device, mesh=grid, in_specs=in_specs, out_specs=out_specs, check_vma=False
    )
```

```python
import jax
import jax.numpy as jnp
from jax import lax
from jax.experimental import pallas as pl
from jax.experimental.pallas import tpu as pltpu
from jax.sharding import Mesh
from jax.sharding import PartitionSpec as P

EPS = 1e-05
ROOT_HALF = 0.7071067811865476
INV_ROOT_TWO_PI = 0.3989422804014327
LOG2_E = 1.4426950408889634
AXES = ("xh", "z", "y", "xl", "core")
DP = ("xh", "z", "y")
SEQ = ("xl", "core")
F32 = jnp.float32
BF16 = jnp.bfloat16


def gelu_value(before):
    return before * 0.5 * (1.0 + lax.erf(before * ROOT_HALF))


def gelu_slope(before):
    cumulative = 0.5 * (1.0 + lax.erf(before * ROOT_HALF))
    return cumulative + before * INV_ROOT_TWO_PI * jnp.exp(-0.5 * before * before)


def rms_parts(stream):
    inverse = lax.rsqrt(jnp.mean(stream * stream, axis=-1, keepdims=True) + EPS)
    return (inverse, stream * inverse)


def rotate(block, axis, step):
    return lax.ppermute(block, axis, [(i, (i + step) % 4) for i in range(4)])


def swap(block, axis):
    return lax.ppermute(block, axis, [(0, 1), (1, 0)])


def swap_both(block, axes):
    return lax.ppermute(block, axes, [(i, 3 - i) for i in range(4)])


def piece(array, at, dim):
    return lax.dynamic_index_in_dim(array, lax.rem(at, 4), dim, keepdims=False)


def scatter_ring(block, axis, dim, *others):
    place = lax.axis_index(axis)
    total = after(piece(block, place, dim).astype(F32), *others)
    for step in (2, 1, 3):
        total = total + rotate(piece(block, place + step, dim), axis, step).astype(F32)
    return total.astype(BF16)


def sum_four(block, axis):
    total = block
    for step in (1, 3, 2):
        total = total + rotate(block, axis, step)
    return total


def after(array, *others):
    for other in others:
        array = array + (other[(0,) * other.ndim] * 0).astype(array.dtype)
    return array


def pick(flag, first, second):
    return jnp.where(flag == 0, first, second)


def attention_kernel(
    core_ref, q_ref, near_ref, far_ref, near_other_ref, far_other_ref, g_ref,
    o_ref, dq_ref, keep_ref, away_ref,
    k_rows, v_rows, k_turned, v_turned, dk_sum, dv_sum,
):
    step = pl.program_id(0)
    scale = 128 ** (-0.5)
    first = core_ref[0] == 0
    rows = near_ref.shape[0]

    @pl.when(step == 0)
    def _():
        for start, mine_ref, other_ref in (
            (0, near_ref, near_other_ref), (rows, far_ref, far_other_ref)
        ):
            mine = mine_ref[...]
            other = other_ref[...]
            k = jnp.where(first, mine, other)
            v = jnp.where(first, other, mine)
            k_rows[start : start + rows] = k
            v_rows[start : start + rows] = v
            k_turned[:, start : start + rows] = k.T
            v_turned[:, start : start + rows] = v.T

    q = q_ref[...]
    g = g_ref[...]
    nt = (((1,), (1,)), ((), ()))
    scores = lax.dot_general(k_rows[...], q, nt, preferred_element_type=F32)
    top = jnp.max(scores, axis=0, keepdims=True)
    raised = jnp.exp2((scores - top) * (scale * LOG2_E))
    probs = raised * (1.0 / jnp.sum(raised, axis=0, keepdims=True))
    probs_low = probs.astype(BF16)
    o_ref[...] = jnp.dot(v_turned[...], probs_low, preferred_element_type=F32).T.astype(BF16)
    dv = jnp.dot(probs_low, g, preferred_element_type=F32)
    dp = lax.dot_general(v_rows[...], g, nt, preferred_element_type=F32)
    centre = jnp.sum(probs * dp, axis=0, keepdims=True)
    ds = (probs * ((dp - centre) * scale)).astype(BF16)
    dq_ref[...] = jnp.dot(k_turned[...], ds, preferred_element_type=F32).T.astype(BF16)
    dk = jnp.dot(ds, q, preferred_element_type=F32)

    @pl.when(step == 0)
    def _():
        dk_sum[...] = dk
        dv_sum[...] = dv

    @pl.when(step > 0)
    def _():
        dk_sum[...] += dk
        dv_sum[...] += dv

    @pl.when(step == pl.num_programs(0) - 1)
    def _():
        dk = dk_sum[...]
        dv = dv_sum[...]
        keep_ref[...] = jnp.where(first, dk, dv).astype(BF16)
        away_ref[...] = jnp.where(first, dv, dk).astype(BF16)


def attention(core, queries, near, far, near_other, far_other, grads, rows=512):
    length, wide = queries.shape
    half, size = near.shape
    total = 2 * half
    blocks = length // rows
    steps = blocks * (wide // size)
    row_spec = pl.BlockSpec((rows, size), lambda i: (i % blocks, i // blocks))
    full_spec = pl.BlockSpec((half, size), lambda i: (0, 0))
    return pl.pallas_call(
        attention_kernel,
        grid=(steps,),
        in_specs=[pl.BlockSpec(memory_space=pltpu.SMEM), row_spec]
        + [full_spec] * 4
        + [row_spec],
        out_specs=[row_spec] * 2 + [pl.BlockSpec((total, size), lambda i: (0, 0))] * 2,
        out_shape=[jax.ShapeDtypeStruct((length, wide), BF16)] * 2
        + [jax.ShapeDtypeStruct((total, size), BF16)] * 2,
        scratch_shapes=[pltpu.VMEM((total, size), BF16)] * 2
        + [pltpu.VMEM((size, total), BF16)] * 2
        + [pltpu.VMEM((total, size), F32)] * 2,
        compiler_params=pltpu.CompilerParams(
            dimension_semantics=("arbitrary",), vmem_limit_bytes=48 * 1024 * 1024
        ),
        cost_estimate=pl.CostEstimate(
            flops=10 * length * wide * total, bytes_accessed=8 * length * wide, transcendentals=0
        ),
        name="attention",
    )(core, queries, near, far, near_other, far_other, grads)


def prepare_kernel(
    place_ref, own_ref, partner_ref, edge_ref, gain_ref, hidden_ref, turned_ref, wide
):
    core, xl = place_ref[0], place_ref[1]
    channels = hidden_ref.shape[1]
    length = own_ref.shape[0]
    gain = gain_ref[...]

    def rows_of(rows):
        _, normed = rms_parts(rows.astype(F32))
        return gelu_value(normed[:, :channels] * gain)

    chunk = 128

    def body(i, carry):
        at = pl.multiple_of(i * chunk, chunk)
        wide[pl.ds(pl.multiple_of(8 + core * length + at, 8), chunk)] = rows_of(
            own_ref[pl.ds(at, chunk)]
        )
        wide[pl.ds(pl.multiple_of(8 + (1 - core) * length + at, 8), chunk)] = rows_of(
            partner_ref[pl.ds(at, chunk)]
        )
        return carry

    lax.fori_loop(0, length // chunk, body, 0)
    edge = rows_of(edge_ref[...])
    reach = edge.shape[0]
    wide[8 - reach : 8] = jnp.where(xl == 1, edge, 0.0)
    end = 8 + 2 * length
    wide[end : end + 16] = jnp.zeros((16, channels), F32)
    wide[end : end + reach] = jnp.where(xl == 0, edge, 0.0)
    for i in range(2 * length // chunk):
        start = 8 - reach + i * chunk
        hidden_ref[i * chunk : (i + 1) * chunk] = wide[start : start + chunk].astype(BF16)
    start = end - reach
    hidden_ref[2 * length : 2 * length + 16] = wide[start : start + 16].astype(BF16)
    hidden_ref[2 * length + 16 :] = jnp.zeros(
        (hidden_ref.shape[0] - 2 * length - 16, channels), BF16
    )
    turned_ref[...] = hidden_ref[...].T


def prepare(place, own, partner, edge, gain):
    length = own.shape[0]
    channels = gain.shape[0]
    vmem = pl.BlockSpec(memory_space=pltpu.VMEM)
    return pl.pallas_call(
        prepare_kernel,
        in_specs=[pl.BlockSpec(memory_space=pltpu.SMEM)] + [vmem] * 4,
        out_specs=[vmem, vmem],
        out_shape=[
            jax.ShapeDtypeStruct((2 * length + 128, channels), BF16),
            jax.ShapeDtypeStruct((channels, 2 * length + 128), BF16),
        ],
        scratch_shapes=[pltpu.VMEM((2 * length + 32, channels), F32)],
        compiler_params=pltpu.CompilerParams(vmem_limit_bytes=40 * 1024 * 1024),
        name="prepare",
    )(place, own, partner, edge, gain.reshape(1, -1))


def conv_kernel(hidden_ref, block_ref, inner_ref, middle_ref, weight_ref, shifted):
    length, half = inner_ref.shape
    rows = shifted.shape[0]
    channels, wide = weight_ref.shape
    group = channels // 32
    for pair in range(8):
        first = block_ref[2 * pair].astype(F32)
        second = block_ref[2 * pair + 1].astype(F32)
        for side in range(2):
            part = slice(side * group, (side + 1) * group)
            start = side * (channels // 2) + pair * 2 * group
            weight_ref[start : start + 2 * group] = jnp.concatenate(
                [first[part], second[part]], axis=0
            ).astype(BF16)
    hidden = hidden_ref[:rows]
    total = jnp.zeros((length, half), F32)
    for tap in range(wide // half):
        shifted[...] = jnp.dot(
            hidden, weight_ref[:, tap * half : (tap + 1) * half], preferred_element_type=F32
        )
        total = total + shifted[tap : tap + length]
    middle_ref[...] = (inner_ref[...].astype(F32) + total).astype(BF16)


def convolve(hidden, block, inner, taps):
    length, half = inner.shape
    channels = hidden.shape[1]
    vmem = pl.BlockSpec(memory_space=pltpu.VMEM)
    return pl.pallas_call(
        conv_kernel,
        grid=(1,),
        in_specs=[
            pl.BlockSpec(hidden.shape, lambda i: (0, 0)),
            pl.BlockSpec(block.shape[:2] + (taps * half,), lambda i: (0, 0, 0)),
            pl.BlockSpec(inner.shape, lambda i: (0, 0)),
        ],
        out_specs=[vmem, vmem],
        out_shape=[
            jax.ShapeDtypeStruct((length, half), BF16),
            jax.ShapeDtypeStruct((channels, taps * half), BF16),
        ],
        scratch_shapes=[pltpu.VMEM((length + 16, half), F32)],
        compiler_params=pltpu.CompilerParams(vmem_limit_bytes=58 * 1024 * 1024),
        cost_estimate=pl.CostEstimate(
            flops=2 * taps * channels * half * length, bytes_accessed=8 * channels * channels,
            transcendentals=0,
        ),
        name="convolve",
    )(hidden, block, inner)


def input_kernel(
    keep_ref,
    away_ref,
    before_ref,
    after_ref,
    weight_ref,
    other_ref,
    middle_ref,
    stream_ref,
    gain_ref,
    out_ref,
    term_ref,
    keep_wide,
    away_wide,
):
    step = pl.program_id(0)
    length, half = keep_ref.shape
    rows, model = stream_ref.shape
    channels = 2 * half
    reach = before_ref.shape[0]
    width = 2 * reach + 1

    @pl.when(step == 0)
    def _():
        for wide, rows_ref, flip in ((keep_wide, keep_ref, False), (away_wide, away_ref, True)):
            wide[8 : 8 + length] = rows_ref[...].astype(F32)
            for edge_ref, start in ((before_ref, 8 - reach), (after_ref, 8 + length)):
                edge = edge_ref[...].astype(F32)
                wide[start : start + reach] = edge[:, :half] if flip else edge[:, half:]
        term_ref[...] = jnp.zeros(term_ref.shape, F32)

    at = pl.multiple_of(step * rows, rows)
    hidden_grad = jnp.zeros((rows, channels), F32)
    for wide, weights in ((keep_wide, weight_ref), (away_wide, other_ref)):
        block = wide[pl.ds(at, rows + 16)]
        for offset in range(width):
            start = 8 + reach - offset
            hidden_grad = hidden_grad + lax.dot_general(
                block[start : start + rows].astype(BF16),
                weights[:, offset * half : (offset + 1) * half],
                (((1,), (1,)), ((), ())),
                preferred_element_type=F32,
            )
    stream = stream_ref[...].astype(F32)
    inverse, normed = rms_parts(stream)
    gain = gain_ref[...]
    narrow = normed[:, :channels]
    before_grad = hidden_grad * gelu_slope(narrow * gain)
    term_ref[...] += jnp.sum((before_grad * narrow).reshape(rows // 8, 8, channels), axis=0)
    lifted = before_grad * gain
    projected = jnp.sum(lifted * narrow, axis=-1, keepdims=True) * (1.0 / model)
    out_ref[:, :channels] = (
        middle_ref[:, :channels] + inverse * (lifted - narrow * projected)
    ).astype(BF16)
    out_ref[:, channels:] = (
        middle_ref[:, channels:] - inverse * normed[:, channels:] * projected
    ).astype(BF16)


def input_gradient(keep, away, before, behind, weights, other, middle, stream, gain):
    length, model = stream.shape
    half = keep.shape[1]
    rows = 128
    vmem = pl.BlockSpec(memory_space=pltpu.VMEM)
    row_spec = pl.BlockSpec((rows, model), lambda i: (i, 0))
    input_rows, terms = pl.pallas_call(
        input_kernel,
        grid=(length // rows,),
        in_specs=[vmem] * 6
        + [row_spec, row_spec, vmem],
        out_specs=[row_spec, pl.BlockSpec((8, 2 * half), lambda i: (0, 0))],
        out_shape=[
            jax.ShapeDtypeStruct((length, model), BF16),
            jax.ShapeDtypeStruct((8, 2 * half), F32),
        ],
        scratch_shapes=[pltpu.VMEM((length + 16, half), F32)] * 2,
        compiler_params=pltpu.CompilerParams(
            dimension_semantics=("arbitrary",), vmem_limit_bytes=58 * 1024 * 1024
        ),
        cost_estimate=pl.CostEstimate(
            flops=40 * length * half * half, bytes_accessed=16 * length * model, transcendentals=0
        ),
        name="input_gradient",
    )(
        keep, away, before, behind, weights, other, middle,
        stream, gain.reshape(1, -1),
    )
    return input_rows, jnp.sum(terms, axis=0)


def project_kernel(
    core_ref, half_ref, other_ref, own_ref, partner_ref, gain_ref, rest_ref, last_ref,
    attn_ref, kv_ref, qkv_ref, out_full,
):
    step = pl.program_id(0)
    rows, half = half_ref.shape
    model = gain_ref.shape[1]
    steps = pl.num_programs(0)
    groups = model // 32
    quarter = half - kv_ref.shape[1]
    share = quarter // 16

    @pl.when(step == 0)
    def _():
        for at in range(16):
            rest = jnp.concatenate([rest_ref[at], last_ref[at]], axis=1)
            for side in range(2):
                start = side * (model // 2) + at * groups
                qkv_ref[start : start + groups] = rest[:, side * half : (side + 1) * half]
            third = model // 3
            for part in range(3):
                out_full[at * share : (at + 1) * share, part * third : (part + 1) * third] = rest[
                    part * share : (part + 1) * share, 2 * half :
                ]

    second = core_ref[0] == 1
    mine = half_ref[...].astype(F32)
    other = other_ref[...].astype(F32)
    outer = jnp.where(step >= steps // 2, partner_ref[...], own_ref[...]).astype(F32)
    middle = jnp.concatenate(
        [jnp.where(second, other, mine), jnp.where(second, mine, other), outer], axis=1
    )
    _, normed = rms_parts(middle)
    attn = (normed * gain_ref[...]).astype(BF16)
    attn_ref[...] = attn
    kv_ref[...] = jnp.dot(attn, qkv_ref[:, quarter:], preferred_element_type=F32).astype(BF16)


def project(core, half_rows, other_rows, own, partner, gain, rest, quarter):
    length, half = half_rows.shape
    model = own.shape[1]
    rows = 256
    vmem = pl.BlockSpec(memory_space=pltpu.VMEM)

    steps = length // rows

    def by_rows(wide):
        return pl.BlockSpec(
            (rows, wide), lambda i, core: (lax.rem(i + core[0] * (steps // 2), steps), 0)
        )

    def whole(first, second):
        return pl.BlockSpec((first, second), lambda i, core: (0, 0))

    outer = model - 2 * half
    part = rest.shape[:2] + (rest.shape[2] // 5,)
    return pl.pallas_call(
        project_kernel,
        grid_spec=pltpu.PrefetchScalarGridSpec(
            num_scalar_prefetch=1,
            grid=(steps,),
            in_specs=[
                by_rows(half), by_rows(half),
                pl.BlockSpec((rows, outer), lambda i, core: (lax.min(i, steps // 2 - 1), 1)),
                pl.BlockSpec((rows, outer), lambda i, core: (lax.max(i - steps // 2, 0), 1)),
                whole(1, model),
                pl.BlockSpec(part, lambda i, core: (0, 0, 3)),
                pl.BlockSpec(part, lambda i, core: (0, 0, 4)),
            ],
            out_specs=[
                by_rows(model), by_rows(half - quarter), whole(model, half), whole(quarter, model)
            ],
        ),
        out_shape=[
            jax.ShapeDtypeStruct((length, model), BF16),
            jax.ShapeDtypeStruct((length, half - quarter), BF16),
            jax.ShapeDtypeStruct((model, half), BF16),
            jax.ShapeDtypeStruct((quarter, model), BF16),
        ],
        compiler_params=pltpu.CompilerParams(
            dimension_semantics=("arbitrary",), vmem_limit_bytes=58 * 1024 * 1024
        ),
        cost_estimate=pl.CostEstimate(
            flops=2 * length * model * (half - quarter), bytes_accessed=8 * length * model,
            transcendentals=0,
        ),
        name="project",
    )(core, half_rows, other_rows, own, partner, gain.reshape(1, -1), rest, rest)


def projection_kernel(
    core_ref, attn_ref, query_ref, attended_ref, upward_ref, partner_ref, out_ref
):
    tn = (((0,), (0,)), ((), ()))
    model = attn_ref.shape[1]
    wide = query_ref.shape[1]
    half = out_ref.shape[3]
    groups = model // 32
    share = wide // 16
    for side in range(2):
        rows = model // 2
        term = lax.dot_general(
            attn_ref[:, side * rows : (side + 1) * rows],
            query_ref[...],
            tn,
            preferred_element_type=F32,
        ).astype(BF16)
        for at in range(16):
            start = at * groups
            line = jnp.concatenate(
                [term[start + i * share : start + (i + 1) * share] for i in range(3)], axis=1
            )
            for i in range(2):
                start = (2 * side + i) * share
                out_ref[at % 4, at // 4, start : start + share] = line[
                    :, i * half : (i + 1) * half
                ]
    length = upward_ref.shape[0]
    core = core_ref[0]
    own = attended_ref[pl.ds(pl.multiple_of(core * length, length), length)]
    partner = attended_ref[pl.ds(pl.multiple_of((1 - core) * length, length), length)]
    for block in range(model // half):
        columns = slice(block * half, (block + 1) * half)
        term = lax.dot_general(own, upward_ref[:, columns], tn, preferred_element_type=F32)
        term = term + lax.dot_general(
            partner, partner_ref[:, columns], tn, preferred_element_type=F32
        )
        term = term.astype(BF16)
        start = (4 + block) * share
        for at in range(16):
            out_ref[at % 4, at // 4, start : start + share] = term[at * share : (at + 1) * share]


def projection_gradient(core, attn, queries, attended, upward, partner):
    length, model = attn.shape
    wide = queries.shape[1]
    vmem = pl.BlockSpec(memory_space=pltpu.VMEM)
    return pl.pallas_call(
        projection_kernel,
        in_specs=[pl.BlockSpec(memory_space=pltpu.SMEM)] + [vmem] * 5,
        out_specs=vmem,
        out_shape=jax.ShapeDtypeStruct((4, 4, 8 * wide // 16, model // 4), BF16),
        compiler_params=pltpu.CompilerParams(vmem_limit_bytes=48 * 1024 * 1024),
        cost_estimate=pl.CostEstimate(
            flops=8 * length * model * wide, bytes_accessed=16 * length * model, transcendentals=0
        ),
        name="projection_gradient",
    )(core, attn, queries, attended, upward, partner)


def middle_kernel(
    core_ref, query_ref, query_other_ref, kv_ref, kv_other_ref, weight_ref, other_ref,
    middle_ref, upward_ref, gain_ref, grad_ref, keep_ref, away_ref, term_ref,
):
    step = pl.program_id(0)
    nt = (((1,), (1,)), ((), ()))
    rows, model = middle_ref.shape
    wide = query_ref.shape[1]
    half = keep_ref.shape[1]
    grad = jnp.zeros((rows, model), F32)
    for q_ref, k_ref, w_ref in (
        (query_ref, kv_ref, weight_ref), (query_other_ref, kv_other_ref, other_ref)
    ):
        grad = grad + lax.dot_general(
            q_ref[...], w_ref[:, :wide], nt, preferred_element_type=F32
        )
        grad = grad + lax.dot_general(
            k_ref[...], w_ref[:, wide:], nt, preferred_element_type=F32
        )
    inverse, normed = rms_parts(middle_ref[...].astype(F32))
    product = grad * normed

    @pl.when(step == 0)
    def _():
        term_ref[...] = jnp.zeros(term_ref.shape, F32)

    term_ref[...] += jnp.sum(product.reshape(rows // 8, 8, model), axis=0)
    gain = gain_ref[...]
    mean = jnp.mean(product * gain, axis=-1, keepdims=True)
    result = upward_ref[...].astype(F32) + inverse * (grad * gain - normed * mean)
    grad_ref[...] = result
    low = result[:, :half].astype(BF16)
    high = result[:, half : 2 * half].astype(BF16)
    second = core_ref[0] == 1
    keep_ref[...] = jnp.where(second, high, low)
    away_ref[...] = jnp.where(second, low, high)


def middle_gradient(
    core, queries, queries_other, kv, kv_other, weights, other, middle, upward, gain
):
    length, model = middle.shape
    half = weights.shape[1]
    rows = 128

    def by_rows(wide):
        return pl.BlockSpec((rows, wide), lambda i: (i, 0))

    vmem = pl.BlockSpec(memory_space=pltpu.VMEM)
    grads, keep, away, terms = pl.pallas_call(
        middle_kernel,
        grid=(length // rows,),
        in_specs=[
            pl.BlockSpec(memory_space=pltpu.SMEM),
            by_rows(queries.shape[1]), by_rows(queries.shape[1]),
            by_rows(kv.shape[1]), by_rows(kv.shape[1]),
            vmem, vmem, by_rows(model), by_rows(model), vmem,
        ],
        out_specs=[
            by_rows(model), by_rows(half), by_rows(half),
            pl.BlockSpec((8, model), lambda i: (0, 0)),
        ],
        out_shape=[
            jax.ShapeDtypeStruct((length, model), F32),
            jax.ShapeDtypeStruct((length, half), BF16),
            jax.ShapeDtypeStruct((length, half), BF16),
            jax.ShapeDtypeStruct((8, model), F32),
        ],
        compiler_params=pltpu.CompilerParams(
            dimension_semantics=("arbitrary",), vmem_limit_bytes=40 * 1024 * 1024
        ),
        cost_estimate=pl.CostEstimate(
            flops=4 * length * model * half, bytes_accessed=12 * length * model, transcendentals=0
        ),
        name="middle_gradient",
    )(
        core, queries, queries_other, kv, kv_other, weights, other, middle, upward,
        gain.reshape(1, -1),
    )
    return grads, keep, away, jnp.sum(terms, axis=0)


def conv_term_kernel(core_ref, turned_ref, keep_ref, sent_ref, kv_ref, out_ref, wide):
    length, half = keep_ref.shape
    span = turned_ref.shape[1]
    taps = out_ref.shape[3] - 1
    group = out_ref.shape[4]
    first = core_ref[0] == 0
    keep = keep_ref[...].astype(F32)
    sent = sent_ref[...].astype(F32)
    wide[:8] = jnp.zeros((8, half), F32)
    wide[8 : 8 + length] = jnp.where(first, keep, sent)
    wide[8 + length : 8 + 2 * length] = jnp.where(first, sent, keep)
    wide[8 + 2 * length :] = jnp.zeros((span - 2 * length, half), F32)
    for tap in range(taps):
        shifted = wide[8 - tap : 8 - tap + span].astype(BF16)
        term = jnp.dot(turned_ref[...], shifted, preferred_element_type=F32)
        for at in range(32):
            out_ref[at // 4 % 4, at % 4, at // 16, tap] = term[
                at * group : (at + 1) * group
            ].astype(BF16)
    for at in range(32):
        out_ref[at // 4 % 4, at % 4, at // 16, taps] = kv_ref[at // 16, at // 4 % 4, at % 4]


def conv_terms(core, turned, keep, sent, kv, taps):
    channels, span = turned.shape
    length, half = keep.shape
    vmem = pl.BlockSpec(memory_space=pltpu.VMEM)
    return pl.pallas_call(
        conv_term_kernel,
        in_specs=[pl.BlockSpec(memory_space=pltpu.SMEM)] + [vmem] * 4,
        out_specs=vmem,
        out_shape=jax.ShapeDtypeStruct((4, 4, 2, taps + 1, channels // 32, half), BF16),
        scratch_shapes=[pltpu.VMEM((span + 8, half), F32)],
        compiler_params=pltpu.CompilerParams(vmem_limit_bytes=40 * 1024 * 1024),
        cost_estimate=pl.CostEstimate(
            flops=2 * taps * channels * half * span, bytes_accessed=4 * channels * span,
            transcendentals=0,
        ),
        name="conv_terms",
    )(core, turned, keep, sent, kv)


def on_device(
    inputs,
    cotangent,
    conv_weight,
    query_weight,
    key_weight,
    value_weight,
    output_weight,
    conv_gain,
    attention_gain,
):
    core = lax.axis_index("core")
    xl = lax.axis_index("xl")
    xh = lax.axis_index("xh")
    place = lax.axis_index(DP)
    rows_in, width, channels = conv_weight.shape
    half = channels // 2
    reach = width // 2
    length, model = inputs.shape[1:]
    head_size = key_weight.shape[1]
    query_size = query_weight.shape[1]
    quarter = query_size // 2
    rows_d = query_weight.shape[0]
    rows_o = output_weight.shape[0]
    upward_low = cotangent[0]
    stream_low = inputs[0]
    tn = (((0,), (0,)), ((), ()))
    nt = (((1,), (1,)), ((), ()))

    def both(mine, other):
        return jnp.concatenate([pick(core, mine, other), pick(core, other, mine)], axis=0)

    def own_rows(array):
        return pick(core, array[:length], array[length:])

    def partner_rows(array):
        return pick(core, array[length:], array[:length])

    with jax.named_scope("gather_conv"):
        own = conv_weight.astype(BF16)
        own = pick(core, own[:, :, :half], own[:, :, half:]).reshape(rows_in, width * half)
        own = jnp.pad(own, ((0, 0), (0, 128)))

    with jax.named_scope("gather"):
        qkv = jnp.concatenate(
            [
                pick(core, query_weight[:, :quarter], query_weight[:, quarter:]),
                pick(core, key_weight, value_weight),
            ],
            axis=1,
        ).astype(BF16)
        third = model // 3
        out_low = jnp.concatenate(
            [output_weight[:, i * third : (i + 1) * third].astype(BF16) for i in range(3)], axis=0
        )
        block = jnp.concatenate(
            [qkv, out_low, jnp.concatenate([own[:, : 2 * third], own[:, 2 * third :]], axis=0)],
            axis=1,
        )
        far = swap(block, "xh")
        pair = [pick(xh, block, far), pick(xh, far, block)]
        start = half + third
        left = width * half - 2 * third
        conv_pair = [
            jnp.concatenate([b[:rows_in, start:], b[rows_in:, start : start + left]], axis=1)
            for b in pair
        ]
        block = jnp.concatenate(
            [
                jnp.concatenate(conv_pair, axis=0),
                pair[0][:, :half],
                pair[1][:, :half],
                pick(xh ^ core, block[:, half:start], far[:, half:start]),
            ],
            axis=1,
        )
        own_block = block
        block = lax.all_gather(block, ("z", "y"), axis=0, tiled=False)

    with jax.named_scope("rows"):
        partner = swap(stream_low, "core")
        edge = after(pick(xl, stream_low[-reach:], stream_low[:reach]), own)
        edge = lax.ppermute(edge, SEQ, [(2, 0), (1, 3)]) + lax.ppermute(edge, SEQ, [(2, 1), (1, 2)])
        upward_partner = swap(upward_low, "core")
        inner = both(stream_low[:, :channels], partner[:, :channels])
        inner = pick(core, inner[:, :half], inner[:, half:])

    core_at = core.reshape(1).astype(jnp.int32)
    spots = jnp.stack([core, xl]).astype(jnp.int32)
    with jax.named_scope("gather_gains"):
        slot = lax.broadcasted_iota(jnp.int32, (32, rows_in + rows_d), 0)
        gains = jnp.concatenate([conv_gain, attention_gain]).astype(BF16)
        gains = after(gains, own_block)
        gains = jnp.where(slot == place, gains[None, :], jnp.zeros((), BF16))
        gains = sum_four(gains, "y")
        gains = sum_four(gains, "z")
        gains = (gains + swap(gains, "xh")).astype(F32)
        gain_one = gains[:, :rows_in].reshape(-1)
        gain_two = gains[:, rows_in:].reshape(-1)
    hidden, hidden_turned = prepare(
        spots, stream_low, partner, after(edge, upward_partner), gain_one
    )
    with jax.named_scope("conv"):
        middle_half, conv_half = convolve(hidden, block, inner, width)
        middle_other = swap(middle_half, "core")
        middle = jnp.concatenate(
            [
                own_rows(pick(core, middle_half, middle_other)),
                own_rows(pick(core, middle_other, middle_half)),
                stream_low[:, channels:],
            ],
            axis=1,
        )

    attn_pair, kv, qkv_half, out_half = project(
        core_at, middle_half, middle_other, stream_low, partner, gain_two, block, quarter
    )

    with jax.named_scope("project"):
        queries = jnp.dot(attn_pair, qkv_half[:, :quarter], preferred_element_type=F32).astype(BF16)
        upward_pair = both(upward_low, upward_partner)
        attended_grad = lax.dot_general(
            upward_pair, out_half, nt, preferred_element_type=F32
        ).astype(BF16)

    with jax.named_scope("keys"):
        kv_far = swap(kv, "xl")
        kv_near_other = swap(kv, "core")
        kv_far_other = swap(kv_far, "core")

    qkv_other = swap(qkv_half, "core")
    conv_other = swap(conv_half, "core")
    attended, query_grad_rows, kv_keep, kv_away = attention(
        after(core_at, conv_other, qkv_other), queries, kv, kv_far, kv_near_other, kv_far_other, attended_grad
    )

    with jax.named_scope("key_grads"):
        kv_sum = (kv_keep.astype(F32) + swap(kv_away, "core").astype(F32)).astype(BF16)
        kv_grad_low = (
            kv_sum[: 2 * length].astype(F32) + swap(kv_sum[2 * length :], "xl").astype(F32)
        ).astype(BF16)
        query_grad_other = swap(partner_rows(query_grad_rows), "core")
        kv_grad_other = swap(partner_rows(kv_grad_low), "core")

    with jax.named_scope("projection_grads"):
        rest_terms = projection_gradient(
            core_at, attn_pair, query_grad_rows, attended, upward_low, upward_partner
        )

    middle_grad, cg_keep, cg_away, second_term = middle_gradient(
        core_at, own_rows(query_grad_rows), query_grad_other, own_rows(kv_grad_low), kv_grad_other,
        qkv_half, qkv_other, middle, upward_low, gain_two,
    )

    with jax.named_scope("conv_grad"):
        cg_sent = swap(cg_away, "core")

        def ends(rows):
            return jnp.concatenate([cg_keep[rows], cg_away[rows]], axis=1)

        after_edge = lax.ppermute(ends(slice(0, reach)), SEQ, [(1, 0), (2, 1), (3, 2)])
        before_edge = lax.ppermute(ends(slice(length - reach, length)), SEQ, [(0, 1), (1, 2), (2, 3)])

    with jax.named_scope("key_term"):
        kv_low = lax.dot_general(
            attn_pair, kv_grad_low, tn, preferred_element_type=F32
        ).astype(BF16)
        third = rows_d // 3
        kv_low = kv_low.reshape(2, 4, 4, 3, third, head_size)
        kv_low = jnp.concatenate([kv_low[:, :, :, i] for i in range(3)], axis=-1)
        kv_low = jnp.pad(kv_low, ((0, 0),) * 3 + ((0, rows_in - third), (0, 0)))

    conv_term = conv_terms(core_at, hidden_turned, cg_keep, cg_sent, kv_low, width)

    with jax.named_scope("reduce_conv"):
        shares = lax.psum_scatter(
            conv_term.reshape(4, 4, -1, half), "z", scatter_dimension=0, tiled=False
        )

    input_rows, first_term = input_gradient(
        cg_keep, cg_away, before_edge, after_edge, conv_half, conv_other, middle_grad,
        stream_low, gain_one,
    )

    with jax.named_scope("reduce_gains"):
        terms = jnp.concatenate(
            [first_term.reshape(32, rows_in), second_term.reshape(32, rows_d)], axis=1
        )
        terms = terms.reshape(2, 4, 4, rows_in + rows_d).transpose(2, 0, 1, 3)
        terms = scatter_ring(terms.reshape(4, 8, rows_in + rows_d).astype(BF16), "y", 0)
        terms = terms.reshape(2, 4, rows_in + rows_d).transpose(1, 0, 2)[:, :, None]
        terms = jnp.pad(terms, ((0, 0), (0, 0), (0, 7), (0, half - rows_in - rows_d)))
        terms = terms.reshape(4, 16, half)

    with jax.named_scope("reduce_rest"):
        rest = scatter_ring(rest_terms, "y", 0, first_term)
        rest = scatter_ring(jnp.concatenate([rest, terms], axis=1), "z", 0)

    with jax.named_scope("reduce_all"):
        shares = scatter_ring(shares, "y", 0)
        everything = jnp.concatenate([shares, rest], axis=0)
        conv_rows = (width + 1) * rows_in
        query_rows = rows_d * quarter // half
        out_rows = rows_o * model // half
        sides = []
        start = 0
        for rows in (conv_rows, query_rows, out_rows, 8):
            if rows == out_rows:
                sides.append((everything[start : start + rows],) * 2)
                start += rows
            else:
                sides.append(
                    (everything[start : start + rows], everything[start + rows : start + 2 * rows])
                )
                start += 2 * rows
        keep = jnp.concatenate([pick(xh, a, b) for a, b in sides], axis=0)
        send = jnp.concatenate([pick(xh, b, a) for a, b in sides], axis=0)
        total = (keep.astype(F32) + swap(send, "xh").astype(F32)).astype(BF16)
        mine = total.astype(F32) + swap(total, "xl").astype(F32)
        other = swap(total, "core").astype(F32) + swap_both(total, SEQ).astype(F32)
        first = pick(core, mine, other)
        second = pick(core, other, mine)

        def conv_of(side):
            return side[: width * rows_in].reshape(width, rows_in, half)

        conv_total = jnp.concatenate([conv_of(first), conv_of(second)], axis=2).transpose(1, 0, 2)
        start = width * rows_in
        key_total, value_total = [
            jnp.concatenate(
                [
                    side[start : start + third, i * head_size : (i + 1) * head_size]
                    for i in range(3)
                ],
                axis=0,
            )
            for side in (first, second)
        ]

        def query_of(side):
            line = jnp.concatenate(
                [side[conv_rows : conv_rows + rows_o], side[conv_rows + rows_o : conv_rows + query_rows]],
                axis=1,
            )
            return jnp.concatenate(
                [line[:, i * quarter : (i + 1) * quarter] for i in range(3)], axis=0
            )

        query_total = jnp.concatenate([query_of(first), query_of(second)], axis=1)
        start = conv_rows + query_rows
        out_total = pick(xh, first, second)[start : start + out_rows]
        output_total = jnp.concatenate(
            [out_total[i * rows_o : (i + 1) * rows_o] for i in range(model // half)], axis=1
        )
        terms = (first + second)[start + out_rows, : rows_in + rows_d]

    return (
        input_rows[None],
        conv_total,
        query_total,
        key_total,
        value_total,
        output_total,
        terms[:rows_in],
        terms[rows_in:],
    )


def solution(mesh):
    grid = Mesh(mesh.devices.reshape(2, 4, 4, 2, 2), AXES)
    in_specs = (
        P(DP, SEQ, None),
        P(DP, SEQ, None),
        P(DP, None, None),
        P(DP, None),
        P(DP, None),
        P(DP, None),
        P(DP, None),
        P(DP),
        P(DP),
    )
    out_specs = (
        P(DP, SEQ, None),
        P(DP, None, None),
        P(DP, None),
        P(DP, None),
        P(DP, None),
        P(DP, None),
        P(DP),
        P(DP),
    )
    return jax.shard_map(
        on_device, mesh=grid, in_specs=in_specs, out_specs=out_specs, check_vma=False
    )
```

```python
import jax
import jax.numpy as jnp
from jax import lax
from jax.experimental import pallas as pl
from jax.experimental.pallas import tpu as pltpu
from jax.sharding import Mesh
from jax.sharding import PartitionSpec as P

EPS = 1e-05
ROOT_HALF = 0.7071067811865476
INV_ROOT_TWO_PI = 0.3989422804014327
LOG2_E = 1.4426950408889634
AXES = ("xh", "z", "y", "xl", "core")
DP = ("xh", "z", "y")
SEQ = ("xl", "core")
F32 = jnp.float32
BF16 = jnp.bfloat16


def gelu_value(before):
    return before * 0.5 * (1.0 + lax.erf(before * ROOT_HALF))


def gelu_slope(before):
    cumulative = 0.5 * (1.0 + lax.erf(before * ROOT_HALF))
    return cumulative + before * INV_ROOT_TWO_PI * jnp.exp(-0.5 * before * before)


def rms_parts(stream):
    inverse = lax.rsqrt(jnp.mean(stream * stream, axis=-1, keepdims=True) + EPS)
    return (inverse, stream * inverse)


def rotate(block, axis, step):
    return lax.ppermute(block, axis, [(i, (i + step) % 4) for i in range(4)])


def swap(block, axis):
    return lax.ppermute(block, axis, [(0, 1), (1, 0)])


def swap_both(block, axes):
    return lax.ppermute(block, axes, [(i, 3 - i) for i in range(4)])


def piece(array, at, dim):
    return lax.dynamic_index_in_dim(array, lax.rem(at, 4), dim, keepdims=False)


def scatter_ring(block, axis, dim, *others):
    place = lax.axis_index(axis)
    total = after(piece(block, place, dim).astype(F32), *others)
    for step in (2, 1, 3):
        total = total + rotate(piece(block, place + step, dim), axis, step).astype(F32)
    return total.astype(BF16)


def sum_four(block, axis):
    total = block
    for step in (1, 3, 2):
        total = total + rotate(block, axis, step)
    return total


def after(array, *others):
    for other in others:
        array = array + (other[(0,) * other.ndim] * 0).astype(array.dtype)
    return array


def pick(flag, first, second):
    return jnp.where(flag == 0, first, second)


def attention_kernel(
    core_ref, q_ref, near_ref, far_ref, near_other_ref, far_other_ref, g_ref,
    o_ref, dq_ref, keep_ref, away_ref,
    k_rows, v_rows, k_turned, v_turned, dk_sum, dv_sum,
):
    step = pl.program_id(0)
    scale = 128 ** (-0.5)
    first = core_ref[0] == 0
    rows = near_ref.shape[0]

    @pl.when(step == 0)
    def _():
        for start, mine_ref, other_ref in (
            (0, near_ref, near_other_ref), (rows, far_ref, far_other_ref)
        ):
            mine = mine_ref[...]
            other = other_ref[...]
            k = jnp.where(first, mine, other)
            v = jnp.where(first, other, mine)
            k_rows[start : start + rows] = k
            v_rows[start : start + rows] = v
            k_turned[:, start : start + rows] = k.T
            v_turned[:, start : start + rows] = v.T

    q = q_ref[...]
    g = g_ref[...]
    nt = (((1,), (1,)), ((), ()))
    scores = lax.dot_general(k_rows[...], q, nt, preferred_element_type=F32)
    top = jnp.max(scores, axis=0, keepdims=True)
    raised = jnp.exp2((scores - top) * (scale * LOG2_E))
    probs = raised * (1.0 / jnp.sum(raised, axis=0, keepdims=True))
    probs_low = probs.astype(BF16)
    o_ref[...] = jnp.dot(v_turned[...], probs_low, preferred_element_type=F32).T.astype(BF16)
    dv = jnp.dot(probs_low, g, preferred_element_type=F32)
    dp = lax.dot_general(v_rows[...], g, nt, preferred_element_type=F32)
    centre = jnp.sum(probs * dp, axis=0, keepdims=True)
    ds = (probs * ((dp - centre) * scale)).astype(BF16)
    dq_ref[...] = jnp.dot(k_turned[...], ds, preferred_element_type=F32).T.astype(BF16)
    dk = jnp.dot(ds, q, preferred_element_type=F32)

    @pl.when(step == 0)
    def _():
        dk_sum[...] = dk
        dv_sum[...] = dv

    @pl.when(step > 0)
    def _():
        dk_sum[...] += dk
        dv_sum[...] += dv

    @pl.when(step == pl.num_programs(0) - 1)
    def _():
        dk = dk_sum[...]
        dv = dv_sum[...]
        keep_ref[...] = jnp.where(first, dk, dv).astype(BF16)
        away_ref[...] = jnp.where(first, dv, dk).astype(BF16)


def attention(core, queries, near, far, near_other, far_other, grads, rows=512):
    length, wide = queries.shape
    half, size = near.shape
    total = 2 * half
    blocks = length // rows
    steps = blocks * (wide // size)
    row_spec = pl.BlockSpec((rows, size), lambda i: (i % blocks, i // blocks))
    full_spec = pl.BlockSpec((half, size), lambda i: (0, 0))
    return pl.pallas_call(
        attention_kernel,
        grid=(steps,),
        in_specs=[pl.BlockSpec(memory_space=pltpu.SMEM), row_spec]
        + [full_spec] * 4
        + [row_spec],
        out_specs=[row_spec] * 2 + [pl.BlockSpec((total, size), lambda i: (0, 0))] * 2,
        out_shape=[jax.ShapeDtypeStruct((length, wide), BF16)] * 2
        + [jax.ShapeDtypeStruct((total, size), BF16)] * 2,
        scratch_shapes=[pltpu.VMEM((total, size), BF16)] * 2
        + [pltpu.VMEM((size, total), BF16)] * 2
        + [pltpu.VMEM((total, size), F32)] * 2,
        compiler_params=pltpu.CompilerParams(
            dimension_semantics=("arbitrary",), vmem_limit_bytes=48 * 1024 * 1024
        ),
        cost_estimate=pl.CostEstimate(
            flops=10 * length * wide * total, bytes_accessed=8 * length * wide, transcendentals=0
        ),
        name="attention",
    )(core, queries, near, far, near_other, far_other, grads)


def prepare_kernel(
    place_ref, own_ref, partner_ref, edge_ref, gain_ref, hidden_ref, turned_ref, wide
):
    core, xl = place_ref[0], place_ref[1]
    channels = hidden_ref.shape[1]
    length = own_ref.shape[0]
    gain = gain_ref[...]

    def rows_of(rows):
        _, normed = rms_parts(rows.astype(F32))
        return gelu_value(normed[:, :channels] * gain)

    chunk = 128

    def body(i, carry):
        at = pl.multiple_of(i * chunk, chunk)
        wide[pl.ds(pl.multiple_of(8 + core * length + at, 8), chunk)] = rows_of(
            own_ref[pl.ds(at, chunk)]
        )
        wide[pl.ds(pl.multiple_of(8 + (1 - core) * length + at, 8), chunk)] = rows_of(
            partner_ref[pl.ds(at, chunk)]
        )
        return carry

    lax.fori_loop(0, length // chunk, body, 0)
    edge = rows_of(edge_ref[...])
    reach = edge.shape[0]
    wide[8 - reach : 8] = jnp.where(xl == 1, edge, 0.0)
    end = 8 + 2 * length
    wide[end : end + 16] = jnp.zeros((16, channels), F32)
    wide[end : end + reach] = jnp.where(xl == 0, edge, 0.0)
    for i in range(2 * length // chunk):
        start = 8 - reach + i * chunk
        hidden_ref[i * chunk : (i + 1) * chunk] = wide[start : start + chunk].astype(BF16)
    start = end - reach
    hidden_ref[2 * length : 2 * length + 16] = wide[start : start + 16].astype(BF16)
    hidden_ref[2 * length + 16 :] = jnp.zeros(
        (hidden_ref.shape[0] - 2 * length - 16, channels), BF16
    )
    turned_ref[...] = hidden_ref[...].T


def prepare(place, own, partner, edge, gain):
    length = own.shape[0]
    channels = gain.shape[0]
    vmem = pl.BlockSpec(memory_space=pltpu.VMEM)
    return pl.pallas_call(
        prepare_kernel,
        in_specs=[pl.BlockSpec(memory_space=pltpu.SMEM)] + [vmem] * 4,
        out_specs=[vmem, vmem],
        out_shape=[
            jax.ShapeDtypeStruct((2 * length + 128, channels), BF16),
            jax.ShapeDtypeStruct((channels, 2 * length + 128), BF16),
        ],
        scratch_shapes=[pltpu.VMEM((2 * length + 32, channels), F32)],
        compiler_params=pltpu.CompilerParams(vmem_limit_bytes=40 * 1024 * 1024),
        name="prepare",
    )(place, own, partner, edge, gain.reshape(1, -1))


def conv_kernel(hidden_ref, block_ref, inner_ref, middle_ref, weight_ref, shifted):
    length, half = inner_ref.shape
    rows = shifted.shape[0]
    channels, wide = weight_ref.shape
    group = channels // 32
    for pair in range(8):
        first = block_ref[2 * pair].astype(F32)
        second = block_ref[2 * pair + 1].astype(F32)
        for side in range(2):
            part = slice(side * group, (side + 1) * group)
            start = side * (channels // 2) + pair * 2 * group
            weight_ref[start : start + 2 * group] = jnp.concatenate(
                [first[part], second[part]], axis=0
            ).astype(BF16)
    hidden = hidden_ref[:rows]
    total = jnp.zeros((length, half), F32)
    for tap in range(wide // half):
        shifted[...] = jnp.dot(
            hidden, weight_ref[:, tap * half : (tap + 1) * half], preferred_element_type=F32
        )
        total = total + shifted[tap : tap + length]
    middle_ref[...] = (inner_ref[...].astype(F32) + total).astype(BF16)


def convolve(hidden, block, inner, taps):
    length, half = inner.shape
    channels = hidden.shape[1]
    vmem = pl.BlockSpec(memory_space=pltpu.VMEM)
    return pl.pallas_call(
        conv_kernel,
        grid=(1,),
        in_specs=[
            pl.BlockSpec(hidden.shape, lambda i: (0, 0)),
            pl.BlockSpec(block.shape[:2] + (taps * half,), lambda i: (0, 0, 0)),
            pl.BlockSpec(inner.shape, lambda i: (0, 0)),
        ],
        out_specs=[vmem, vmem],
        out_shape=[
            jax.ShapeDtypeStruct((length, half), BF16),
            jax.ShapeDtypeStruct((channels, taps * half), BF16),
        ],
        scratch_shapes=[pltpu.VMEM((length + 16, half), F32)],
        compiler_params=pltpu.CompilerParams(vmem_limit_bytes=58 * 1024 * 1024),
        cost_estimate=pl.CostEstimate(
            flops=2 * taps * channels * half * length, bytes_accessed=8 * channels * channels,
            transcendentals=0,
        ),
        name="convolve",
    )(hidden, block, inner)


def input_kernel(
    keep_ref,
    away_ref,
    before_ref,
    after_ref,
    weight_ref,
    other_ref,
    middle_ref,
    stream_ref,
    gain_ref,
    out_ref,
    term_ref,
    keep_wide,
    away_wide,
):
    step = pl.program_id(0)
    length, half = keep_ref.shape
    rows, model = stream_ref.shape
    channels = 2 * half
    reach = before_ref.shape[0]
    width = 2 * reach + 1

    @pl.when(step == 0)
    def _():
        for wide, rows_ref, flip in ((keep_wide, keep_ref, False), (away_wide, away_ref, True)):
            wide[8 : 8 + length] = rows_ref[...].astype(F32)
            for edge_ref, start in ((before_ref, 8 - reach), (after_ref, 8 + length)):
                edge = edge_ref[...].astype(F32)
                wide[start : start + reach] = edge[:, :half] if flip else edge[:, half:]
        term_ref[...] = jnp.zeros(term_ref.shape, F32)

    at = pl.multiple_of(step * rows, rows)
    hidden_grad = jnp.zeros((rows, channels), F32)
    for wide, weights in ((keep_wide, weight_ref), (away_wide, other_ref)):
        block = wide[pl.ds(at, rows + 16)]
        for offset in range(width):
            start = 8 + reach - offset
            hidden_grad = hidden_grad + lax.dot_general(
                block[start : start + rows].astype(BF16),
                weights[:, offset * half : (offset + 1) * half],
                (((1,), (1,)), ((), ())),
                preferred_element_type=F32,
            )
    stream = stream_ref[...].astype(F32)
    inverse, normed = rms_parts(stream)
    gain = gain_ref[...]
    narrow = normed[:, :channels]
    before_grad = hidden_grad * gelu_slope(narrow * gain)
    term_ref[...] += jnp.sum((before_grad * narrow).reshape(rows // 8, 8, channels), axis=0)
    lifted = before_grad * gain
    projected = jnp.sum(lifted * narrow, axis=-1, keepdims=True) * (1.0 / model)
    out_ref[:, :channels] = (
        middle_ref[:, :channels] + inverse * (lifted - narrow * projected)
    ).astype(BF16)
    out_ref[:, channels:] = (
        middle_ref[:, channels:] - inverse * normed[:, channels:] * projected
    ).astype(BF16)


def input_gradient(keep, away, before, behind, weights, other, middle, stream, gain):
    length, model = stream.shape
    half = keep.shape[1]
    rows = 128
    vmem = pl.BlockSpec(memory_space=pltpu.VMEM)
    row_spec = pl.BlockSpec((rows, model), lambda i: (i, 0))
    input_rows, terms = pl.pallas_call(
        input_kernel,
        grid=(length // rows,),
        in_specs=[vmem] * 6
        + [row_spec, row_spec, vmem],
        out_specs=[row_spec, pl.BlockSpec((8, 2 * half), lambda i: (0, 0))],
        out_shape=[
            jax.ShapeDtypeStruct((length, model), BF16),
            jax.ShapeDtypeStruct((8, 2 * half), F32),
        ],
        scratch_shapes=[pltpu.VMEM((length + 16, half), F32)] * 2,
        compiler_params=pltpu.CompilerParams(
            dimension_semantics=("arbitrary",), vmem_limit_bytes=58 * 1024 * 1024
        ),
        cost_estimate=pl.CostEstimate(
            flops=40 * length * half * half, bytes_accessed=16 * length * model, transcendentals=0
        ),
        name="input_gradient",
    )(
        keep, away, before, behind, weights, other, middle,
        stream, gain.reshape(1, -1),
    )
    return input_rows, jnp.sum(terms, axis=0)


def project_kernel(
    core_ref, half_ref, other_ref, own_ref, partner_ref, gain_ref, rest_ref, last_ref,
    attn_ref, kv_ref, qkv_ref, out_full,
):
    step = pl.program_id(0)
    rows, half = half_ref.shape
    model = gain_ref.shape[1]
    steps = pl.num_programs(0)
    groups = model // 32
    quarter = half - kv_ref.shape[1]
    share = quarter // 16

    @pl.when(step == 0)
    def _():
        for at in range(16):
            rest = jnp.concatenate([rest_ref[at], last_ref[at]], axis=1)
            for side in range(2):
                start = side * (model // 2) + at * groups
                qkv_ref[start : start + groups] = rest[:, side * half : (side + 1) * half]
            third = model // 3
            for part in range(3):
                out_full[at * share : (at + 1) * share, part * third : (part + 1) * third] = rest[
                    part * share : (part + 1) * share, 2 * half :
                ]

    second = core_ref[0] == 1
    mine = half_ref[...].astype(F32)
    other = other_ref[...].astype(F32)
    outer = jnp.where(step >= steps // 2, partner_ref[...], own_ref[...]).astype(F32)
    middle = jnp.concatenate(
        [jnp.where(second, other, mine), jnp.where(second, mine, other), outer], axis=1
    )
    _, normed = rms_parts(middle)
    attn = (normed * gain_ref[...]).astype(BF16)
    attn_ref[...] = attn
    kv_ref[...] = jnp.dot(attn, qkv_ref[:, quarter:], preferred_element_type=F32).astype(BF16)


def project(core, half_rows, other_rows, own, partner, gain, rest, quarter):
    length, half = half_rows.shape
    model = own.shape[1]
    rows = 256
    vmem = pl.BlockSpec(memory_space=pltpu.VMEM)

    steps = length // rows

    def by_rows(wide):
        return pl.BlockSpec(
            (rows, wide), lambda i, core: (lax.rem(i + core[0] * (steps // 2), steps), 0)
        )

    def whole(first, second):
        return pl.BlockSpec((first, second), lambda i, core: (0, 0))

    outer = model - 2 * half
    part = rest.shape[:2] + (rest.shape[2] // 5,)
    return pl.pallas_call(
        project_kernel,
        grid_spec=pltpu.PrefetchScalarGridSpec(
            num_scalar_prefetch=1,
            grid=(steps,),
            in_specs=[
                by_rows(half), by_rows(half),
                pl.BlockSpec((rows, outer), lambda i, core: (lax.min(i, steps // 2 - 1), 1)),
                pl.BlockSpec((rows, outer), lambda i, core: (lax.max(i - steps // 2, 0), 1)),
                whole(1, model),
                pl.BlockSpec(part, lambda i, core: (0, 0, 3)),
                pl.BlockSpec(part, lambda i, core: (0, 0, 4)),
            ],
            out_specs=[
                by_rows(model), by_rows(half - quarter), whole(model, half), whole(quarter, model)
            ],
        ),
        out_shape=[
            jax.ShapeDtypeStruct((length, model), BF16),
            jax.ShapeDtypeStruct((length, half - quarter), BF16),
            jax.ShapeDtypeStruct((model, half), BF16),
            jax.ShapeDtypeStruct((quarter, model), BF16),
        ],
        compiler_params=pltpu.CompilerParams(
            dimension_semantics=("arbitrary",), vmem_limit_bytes=58 * 1024 * 1024
        ),
        cost_estimate=pl.CostEstimate(
            flops=2 * length * model * (half - quarter), bytes_accessed=8 * length * model,
            transcendentals=0,
        ),
        name="project",
    )(core, half_rows, other_rows, own, partner, gain.reshape(1, -1), rest, rest)


def projection_kernel(
    core_ref, attn_ref, query_ref, attended_ref, upward_ref, partner_ref, kv_ref, out_ref
):
    tn = (((0,), (0,)), ((), ()))
    model = attn_ref.shape[1]
    wide = query_ref.shape[1]
    half = out_ref.shape[3]
    groups = model // 32
    share = wide // 16
    for side in range(2):
        rows = model // 2
        part = attn_ref[:, side * rows : (side + 1) * rows]
        term = lax.dot_general(part, kv_ref[...], tn, preferred_element_type=F32).astype(BF16)
        for at in range(16):
            start = at * groups
            line = jnp.concatenate(
                [term[start + i * share : start + (i + 1) * share] for i in range(3)], axis=1
            )
            start = (8 + side) * share
            out_ref[at % 4, at // 4, start : start + share] = line
        term = lax.dot_general(part, query_ref[...], tn, preferred_element_type=F32).astype(BF16)
        for at in range(16):
            start = at * groups
            line = jnp.concatenate(
                [term[start + i * share : start + (i + 1) * share] for i in range(3)], axis=1
            )
            for i in range(2):
                start = (2 * side + i) * share
                out_ref[at % 4, at // 4, start : start + share] = line[
                    :, i * half : (i + 1) * half
                ]
    length = upward_ref.shape[0]
    core = core_ref[0]
    own = attended_ref[pl.ds(pl.multiple_of(core * length, length), length)]
    partner = attended_ref[pl.ds(pl.multiple_of((1 - core) * length, length), length)]
    for block in range(model // half):
        columns = slice(block * half, (block + 1) * half)
        term = lax.dot_general(own, upward_ref[:, columns], tn, preferred_element_type=F32)
        term = term + lax.dot_general(
            partner, partner_ref[:, columns], tn, preferred_element_type=F32
        )
        term = term.astype(BF16)
        start = (4 + block) * share
        for at in range(16):
            out_ref[at % 4, at // 4, start : start + share] = term[at * share : (at + 1) * share]


def projection_gradient(core, attn, queries, attended, upward, partner, kv):
    length, model = attn.shape
    wide = queries.shape[1]
    vmem = pl.BlockSpec(memory_space=pltpu.VMEM)
    return pl.pallas_call(
        projection_kernel,
        in_specs=[pl.BlockSpec(memory_space=pltpu.SMEM)] + [vmem] * 6,
        out_specs=vmem,
        out_shape=jax.ShapeDtypeStruct((4, 4, 10 * wide // 16, model // 4), BF16),
        compiler_params=pltpu.CompilerParams(vmem_limit_bytes=48 * 1024 * 1024),
        cost_estimate=pl.CostEstimate(
            flops=8 * length * model * wide, bytes_accessed=16 * length * model, transcendentals=0
        ),
        name="projection_gradient",
    )(core, attn, queries, attended, upward, partner, kv)


def middle_kernel(
    core_ref, query_ref, query_other_ref, kv_ref, kv_other_ref, weight_ref, other_ref,
    middle_ref, upward_ref, gain_ref, grad_ref, keep_ref, away_ref, term_ref,
):
    step = pl.program_id(0)
    nt = (((1,), (1,)), ((), ()))
    rows, model = middle_ref.shape
    wide = query_ref.shape[1]
    half = keep_ref.shape[1]
    grad = jnp.zeros((rows, model), F32)
    for q_ref, k_ref, w_ref in (
        (query_ref, kv_ref, weight_ref), (query_other_ref, kv_other_ref, other_ref)
    ):
        grad = grad + lax.dot_general(
            q_ref[...], w_ref[:, :wide], nt, preferred_element_type=F32
        )
        grad = grad + lax.dot_general(
            k_ref[...], w_ref[:, wide:], nt, preferred_element_type=F32
        )
    inverse, normed = rms_parts(middle_ref[...].astype(F32))
    product = grad * normed

    @pl.when(step == 0)
    def _():
        term_ref[...] = jnp.zeros(term_ref.shape, F32)

    term_ref[...] += jnp.sum(product.reshape(rows // 8, 8, model), axis=0)
    gain = gain_ref[...]
    mean = jnp.mean(product * gain, axis=-1, keepdims=True)
    result = upward_ref[...].astype(F32) + inverse * (grad * gain - normed * mean)
    grad_ref[...] = result
    low = result[:, :half].astype(BF16)
    high = result[:, half : 2 * half].astype(BF16)
    second = core_ref[0] == 1
    keep_ref[...] = jnp.where(second, high, low)
    away_ref[...] = jnp.where(second, low, high)


def middle_gradient(
    core, queries, queries_other, kv, kv_other, weights, other, middle, upward, gain
):
    length, model = middle.shape
    half = weights.shape[1]
    rows = 128

    def by_rows(wide):
        return pl.BlockSpec((rows, wide), lambda i: (i, 0))

    vmem = pl.BlockSpec(memory_space=pltpu.VMEM)
    grads, keep, away, terms = pl.pallas_call(
        middle_kernel,
        grid=(length // rows,),
        in_specs=[
            pl.BlockSpec(memory_space=pltpu.SMEM),
            by_rows(queries.shape[1]), by_rows(queries.shape[1]),
            by_rows(kv.shape[1]), by_rows(kv.shape[1]),
            vmem, vmem, by_rows(model), by_rows(model), vmem,
        ],
        out_specs=[
            by_rows(model), by_rows(half), by_rows(half),
            pl.BlockSpec((8, model), lambda i: (0, 0)),
        ],
        out_shape=[
            jax.ShapeDtypeStruct((length, model), F32),
            jax.ShapeDtypeStruct((length, half), BF16),
            jax.ShapeDtypeStruct((length, half), BF16),
            jax.ShapeDtypeStruct((8, model), F32),
        ],
        compiler_params=pltpu.CompilerParams(
            dimension_semantics=("arbitrary",), vmem_limit_bytes=40 * 1024 * 1024
        ),
        cost_estimate=pl.CostEstimate(
            flops=4 * length * model * half, bytes_accessed=12 * length * model, transcendentals=0
        ),
        name="middle_gradient",
    )(
        core, queries, queries_other, kv, kv_other, weights, other, middle, upward,
        gain.reshape(1, -1),
    )
    return grads, keep, away, jnp.sum(terms, axis=0)


def conv_term_kernel(core_ref, turned_ref, keep_ref, sent_ref, out_ref, wide):
    length, half = keep_ref.shape
    span = turned_ref.shape[1]
    taps = out_ref.shape[3]
    group = out_ref.shape[4]
    first = core_ref[0] == 0
    keep = keep_ref[...].astype(F32)
    sent = sent_ref[...].astype(F32)
    wide[:8] = jnp.zeros((8, half), F32)
    wide[8 : 8 + length] = jnp.where(first, keep, sent)
    wide[8 + length : 8 + 2 * length] = jnp.where(first, sent, keep)
    wide[8 + 2 * length :] = jnp.zeros((span - 2 * length, half), F32)
    for tap in range(taps):
        shifted = wide[8 - tap : 8 - tap + span].astype(BF16)
        term = jnp.dot(turned_ref[...], shifted, preferred_element_type=F32)
        for at in range(32):
            out_ref[at // 4 % 4, at % 4, at // 16, tap] = term[
                at * group : (at + 1) * group
            ].astype(BF16)


def conv_terms(core, turned, keep, sent, taps):
    channels, span = turned.shape
    length, half = keep.shape
    vmem = pl.BlockSpec(memory_space=pltpu.VMEM)
    return pl.pallas_call(
        conv_term_kernel,
        in_specs=[pl.BlockSpec(memory_space=pltpu.SMEM)] + [vmem] * 3,
        out_specs=vmem,
        out_shape=jax.ShapeDtypeStruct((4, 4, 2, taps, channels // 32, half), BF16),
        scratch_shapes=[pltpu.VMEM((span + 8, half), F32)],
        compiler_params=pltpu.CompilerParams(vmem_limit_bytes=40 * 1024 * 1024),
        cost_estimate=pl.CostEstimate(
            flops=2 * taps * channels * half * span, bytes_accessed=4 * channels * span,
            transcendentals=0,
        ),
        name="conv_terms",
    )(core, turned, keep, sent)


def on_device(
    inputs,
    cotangent,
    conv_weight,
    query_weight,
    key_weight,
    value_weight,
    output_weight,
    conv_gain,
    attention_gain,
):
    core = lax.axis_index("core")
    xl = lax.axis_index("xl")
    xh = lax.axis_index("xh")
    place = lax.axis_index(DP)
    rows_in, width, channels = conv_weight.shape
    half = channels // 2
    reach = width // 2
    length, model = inputs.shape[1:]
    head_size = key_weight.shape[1]
    query_size = query_weight.shape[1]
    quarter = query_size // 2
    rows_d = query_weight.shape[0]
    rows_o = output_weight.shape[0]
    upward_low = cotangent[0]
    stream_low = inputs[0]
    tn = (((0,), (0,)), ((), ()))
    nt = (((1,), (1,)), ((), ()))

    def both(mine, other):
        return jnp.concatenate([pick(core, mine, other), pick(core, other, mine)], axis=0)

    def own_rows(array):
        return pick(core, array[:length], array[length:])

    def partner_rows(array):
        return pick(core, array[length:], array[:length])

    with jax.named_scope("gather_conv"):
        own = conv_weight.astype(BF16)
        own = pick(core, own[:, :, :half], own[:, :, half:]).reshape(rows_in, width * half)
        own = jnp.pad(own, ((0, 0), (0, 128)))

    with jax.named_scope("gather"):
        qkv = jnp.concatenate(
            [
                pick(core, query_weight[:, :quarter], query_weight[:, quarter:]),
                pick(core, key_weight, value_weight),
            ],
            axis=1,
        ).astype(BF16)
        third = model // 3
        out_low = jnp.concatenate(
            [output_weight[:, i * third : (i + 1) * third].astype(BF16) for i in range(3)], axis=0
        )
        block = jnp.concatenate(
            [qkv, out_low, jnp.concatenate([own[:, : 2 * third], own[:, 2 * third :]], axis=0)],
            axis=1,
        )
        far = swap(block, "xh")
        pair = [pick(xh, block, far), pick(xh, far, block)]
        start = half + third
        left = width * half - 2 * third
        conv_pair = [
            jnp.concatenate([b[:rows_in, start:], b[rows_in:, start : start + left]], axis=1)
            for b in pair
        ]
        block = jnp.concatenate(
            [
                jnp.concatenate(conv_pair, axis=0),
                pair[0][:, :half],
                pair[1][:, :half],
                pick(xh ^ core, block[:, half:start], far[:, half:start]),
            ],
            axis=1,
        )
        own_block = block
        block = lax.all_gather(block, ("z", "y"), axis=0, tiled=False)

    with jax.named_scope("rows"):
        partner = swap(stream_low, "core")
        edge = after(pick(xl, stream_low[-reach:], stream_low[:reach]), own)
        edge = lax.ppermute(edge, SEQ, [(2, 0), (1, 3)]) + lax.ppermute(edge, SEQ, [(2, 1), (1, 2)])
        upward_partner = swap(upward_low, "core")
        upward_pair = both(upward_low, upward_partner)
        inner = both(stream_low[:, :channels], partner[:, :channels])
        inner = pick(core, inner[:, :half], inner[:, half:])

    core_at = core.reshape(1).astype(jnp.int32)
    spots = jnp.stack([core, xl]).astype(jnp.int32)
    with jax.named_scope("gather_gains"):
        slot = lax.broadcasted_iota(jnp.int32, (32, rows_in + rows_d), 0)
        gains = jnp.concatenate([conv_gain, attention_gain]).astype(BF16)
        gains = after(gains, own_block)
        gains = jnp.where(slot == place, gains[None, :], jnp.zeros((), BF16))
        gains = sum_four(gains, "y")
        gains = sum_four(gains, "z")
        gains = (gains + swap(gains, "xh")).astype(F32)
        gain_one = gains[:, :rows_in].reshape(-1)
        gain_two = gains[:, rows_in:].reshape(-1)
    hidden, hidden_turned = prepare(
        spots, stream_low, partner, after(edge, upward_pair), gain_one
    )
    with jax.named_scope("conv"):
        middle_half, conv_half = convolve(hidden, block, inner, width)
        middle_other = swap(middle_half, "core")
        middle = jnp.concatenate(
            [
                own_rows(pick(core, middle_half, middle_other)),
                own_rows(pick(core, middle_other, middle_half)),
                stream_low[:, channels:],
            ],
            axis=1,
        )

    attn_pair, kv, qkv_half, out_half = project(
        core_at, middle_half, middle_other, stream_low, partner, gain_two, block, quarter
    )

    with jax.named_scope("project"):
        queries = jnp.dot(attn_pair, qkv_half[:, :quarter], preferred_element_type=F32).astype(BF16)
        attended_grad = lax.dot_general(
            upward_pair, out_half, nt, preferred_element_type=F32
        ).astype(BF16)

    with jax.named_scope("keys"):
        kv_far = swap(kv, "xl")
        kv_near_other = swap(kv, "core")
        kv_far_other = swap(kv_far, "core")

    qkv_other = swap(qkv_half, "core")
    conv_other = swap(conv_half, "core")
    attended, query_grad_rows, kv_keep, kv_away = attention(
        core_at, queries, kv, kv_far, kv_near_other, kv_far_other, attended_grad
    )

    with jax.named_scope("key_grads"):
        kv_sum = (kv_keep.astype(F32) + swap(kv_away, "core").astype(F32)).astype(BF16)
        kv_grad_low = (
            kv_sum[: 2 * length].astype(F32) + swap(kv_sum[2 * length :], "xl").astype(F32)
        ).astype(BF16)
        query_grad_other = swap(partner_rows(query_grad_rows), "core")
        kv_grad_other = swap(partner_rows(kv_grad_low), "core")

    middle_grad, cg_keep, cg_away, second_term = middle_gradient(
        after(core_at, conv_other, qkv_other), own_rows(query_grad_rows), query_grad_other, own_rows(kv_grad_low), kv_grad_other,
        qkv_half, qkv_other, middle, upward_low, gain_two,
    )

    with jax.named_scope("conv_grad"):
        cg_sent = swap(cg_away, "core")

        def ends(rows):
            return jnp.concatenate([cg_keep[rows], cg_away[rows]], axis=1)

        after_edge = lax.ppermute(ends(slice(0, reach)), SEQ, [(1, 0), (2, 1), (3, 2)])
        before_edge = lax.ppermute(ends(slice(length - reach, length)), SEQ, [(0, 1), (1, 2), (2, 3)])

    with jax.named_scope("projection_grads"):
        rest_terms = projection_gradient(
            core_at, attn_pair, query_grad_rows, attended, upward_low, upward_partner, kv_grad_low
        )

    conv_term = conv_terms(core_at, hidden_turned, cg_keep, cg_sent, width)

    with jax.named_scope("reduce_conv"):
        shares = lax.psum_scatter(
            conv_term.reshape(4, 4, -1, half), "z", scatter_dimension=0, tiled=False
        )

    input_rows, first_term = input_gradient(
        cg_keep, cg_away, before_edge, after_edge, conv_half, conv_other, middle_grad,
        stream_low, gain_one,
    )

    with jax.named_scope("reduce_gains"):
        terms = jnp.concatenate(
            [first_term.reshape(32, rows_in), second_term.reshape(32, rows_d)], axis=1
        )
        terms = terms.reshape(2, 4, 4, rows_in + rows_d).transpose(2, 0, 1, 3)
        terms = scatter_ring(terms.reshape(4, 8, rows_in + rows_d).astype(BF16), "y", 0)
        terms = terms.reshape(2, 4, rows_in + rows_d).transpose(1, 0, 2)[:, :, None]
        terms = jnp.pad(terms, ((0, 0), (0, 0), (0, 7), (0, half - rows_in - rows_d)))
        terms = terms.reshape(4, 16, half)

    with jax.named_scope("reduce_rest"):
        rest = scatter_ring(rest_terms, "y", 0, first_term)
        rest = scatter_ring(jnp.concatenate([rest, terms], axis=1), "z", 0)

    third = rows_d // 3
    with jax.named_scope("reduce_all"):
        shares = scatter_ring(shares, "y", 0)
        everything = jnp.concatenate([shares, rest], axis=0)
        conv_rows = width * rows_in
        query_rows = rows_d * quarter // half
        out_rows = rows_o * model // half
        sides = []
        start = 0
        for rows in (conv_rows, query_rows, out_rows, third, 8):
            if rows == out_rows:
                sides.append((everything[start : start + rows],) * 2)
                start += rows
            else:
                sides.append(
                    (everything[start : start + rows], everything[start + rows : start + 2 * rows])
                )
                start += 2 * rows
        keep = jnp.concatenate([pick(xh, a, b) for a, b in sides], axis=0)
        send = jnp.concatenate([pick(xh, b, a) for a, b in sides], axis=0)
        total = (keep.astype(F32) + swap(send, "xh").astype(F32)).astype(BF16)
        mine = total.astype(F32) + swap(total, "xl").astype(F32)
        other = swap(total, "core").astype(F32) + swap_both(total, SEQ).astype(F32)
        first = pick(core, mine, other)
        second = pick(core, other, mine)

        def conv_of(side):
            return side[: width * rows_in].reshape(width, rows_in, half)

        conv_total = jnp.concatenate([conv_of(first), conv_of(second)], axis=2).transpose(1, 0, 2)
        start = conv_rows + query_rows + out_rows
        key_total, value_total = [
            jnp.concatenate(
                [
                    side[start : start + third, i * head_size : (i + 1) * head_size]
                    for i in range(3)
                ],
                axis=0,
            )
            for side in (first, second)
        ]

        def query_of(side):
            line = jnp.concatenate(
                [side[conv_rows : conv_rows + rows_o], side[conv_rows + rows_o : conv_rows + query_rows]],
                axis=1,
            )
            return jnp.concatenate(
                [line[:, i * quarter : (i + 1) * quarter] for i in range(3)], axis=0
            )

        query_total = jnp.concatenate([query_of(first), query_of(second)], axis=1)
        start = conv_rows + query_rows
        out_total = pick(xh, first, second)[start : start + out_rows]
        output_total = jnp.concatenate(
            [out_total[i * rows_o : (i + 1) * rows_o] for i in range(model // half)], axis=1
        )
        terms = (first + second)[start + out_rows + third, : rows_in + rows_d]

    return (
        input_rows[None],
        conv_total,
        query_total,
        key_total,
        value_total,
        output_total,
        terms[:rows_in],
        terms[rows_in:],
    )


def solution(mesh):
    grid = Mesh(mesh.devices.reshape(2, 4, 4, 2, 2), AXES)
    in_specs = (
        P(DP, SEQ, None),
        P(DP, SEQ, None),
        P(DP, None, None),
        P(DP, None),
        P(DP, None),
        P(DP, None),
        P(DP, None),
        P(DP),
        P(DP),
    )
    out_specs = (
        P(DP, SEQ, None),
        P(DP, None, None),
        P(DP, None),
        P(DP, None),
        P(DP, None),
        P(DP, None),
        P(DP),
        P(DP),
    )
    return jax.shard_map(
        on_device, mesh=grid, in_specs=in_specs, out_specs=out_specs, check_vma=False
    )
```

```python
import jax
import jax.numpy as jnp
from jax import lax
from jax.experimental import pallas as pl
from jax.experimental.pallas import tpu as pltpu
from jax.sharding import Mesh
from jax.sharding import PartitionSpec as P

EPS = 1e-05
ROOT_HALF = 0.7071067811865476
INV_ROOT_TWO_PI = 0.3989422804014327
LOG2_E = 1.4426950408889634
AXES = ("xh", "z", "y", "xl", "core")
DP = ("xh", "z", "y")
SEQ = ("xl", "core")
F32 = jnp.float32
BF16 = jnp.bfloat16


def gelu_value(before):
    return before * 0.5 * (1.0 + lax.erf(before * ROOT_HALF))


def gelu_slope(before):
    cumulative = 0.5 * (1.0 + lax.erf(before * ROOT_HALF))
    return cumulative + before * INV_ROOT_TWO_PI * jnp.exp(-0.5 * before * before)


def rms_parts(stream):
    inverse = lax.rsqrt(jnp.mean(stream * stream, axis=-1, keepdims=True) + EPS)
    return (inverse, stream * inverse)


def rotate(block, axis, step):
    return lax.ppermute(block, axis, [(i, (i + step) % 4) for i in range(4)])


def swap(block, axis):
    return lax.ppermute(block, axis, [(0, 1), (1, 0)])


def swap_both(block, axes):
    return lax.ppermute(block, axes, [(i, 3 - i) for i in range(4)])


def piece(array, at, dim):
    return lax.dynamic_index_in_dim(array, lax.rem(at, 4), dim, keepdims=False)


def scatter_ring(block, axis, dim, *others):
    place = lax.axis_index(axis)
    total = after(piece(block, place, dim).astype(F32), *others)
    for step in (2, 1, 3):
        total = total + rotate(piece(block, place + step, dim), axis, step).astype(F32)
    return total.astype(BF16)


def sum_four(block, axis):
    total = block
    for step in (1, 3, 2):
        total = total + rotate(block, axis, step)
    return total


def after(array, *others):
    for other in others:
        array = array + (other[(0,) * other.ndim] * 0).astype(array.dtype)
    return array


def pick(flag, first, second):
    return jnp.where(flag == 0, first, second)


def attention_kernel(
    core_ref, q_ref, near_ref, far_ref, near_other_ref, far_other_ref, g_ref,
    o_ref, dq_ref, keep_ref, away_ref,
    k_rows, v_rows, k_turned, v_turned, dk_sum, dv_sum,
):
    step = pl.program_id(0)
    scale = 128 ** (-0.5)
    first = core_ref[0] == 0
    rows = near_ref.shape[0]

    @pl.when(step == 0)
    def _():
        for start, mine_ref, other_ref in (
            (0, near_ref, near_other_ref), (rows, far_ref, far_other_ref)
        ):
            mine = mine_ref[...]
            other = other_ref[...]
            k = jnp.where(first, mine, other)
            v = jnp.where(first, other, mine)
            k_rows[start : start + rows] = k
            v_rows[start : start + rows] = v
            k_turned[:, start : start + rows] = k.T
            v_turned[:, start : start + rows] = v.T

    q = q_ref[...]
    g = g_ref[...]
    nt = (((1,), (1,)), ((), ()))
    scores = lax.dot_general(k_rows[...], q, nt, preferred_element_type=F32)
    top = jnp.max(scores, axis=0, keepdims=True)
    raised = jnp.exp2((scores - top) * (scale * LOG2_E))
    probs = raised * (1.0 / jnp.sum(raised, axis=0, keepdims=True))
    probs_low = probs.astype(BF16)
    o_ref[...] = jnp.dot(v_turned[...], probs_low, preferred_element_type=F32).T.astype(BF16)
    dv = jnp.dot(probs_low, g, preferred_element_type=F32)
    dp = lax.dot_general(v_rows[...], g, nt, preferred_element_type=F32)
    centre = jnp.sum(probs * dp, axis=0, keepdims=True)
    ds = (probs * ((dp - centre) * scale)).astype(BF16)
    dq_ref[...] = jnp.dot(k_turned[...], ds, preferred_element_type=F32).T.astype(BF16)
    dk = jnp.dot(ds, q, preferred_element_type=F32)

    @pl.when(step == 0)
    def _():
        dk_sum[...] = dk
        dv_sum[...] = dv

    @pl.when(step > 0)
    def _():
        dk_sum[...] += dk
        dv_sum[...] += dv

    @pl.when(step == pl.num_programs(0) - 1)
    def _():
        dk = dk_sum[...]
        dv = dv_sum[...]
        keep_ref[...] = jnp.where(first, dk, dv).astype(BF16)
        away_ref[...] = jnp.where(first, dv, dk).astype(BF16)


def attention(core, queries, near, far, near_other, far_other, grads, rows=512):
    length, wide = queries.shape
    half, size = near.shape
    total = 2 * half
    blocks = length // rows
    steps = blocks * (wide // size)
    row_spec = pl.BlockSpec((rows, size), lambda i: (i % blocks, i // blocks))
    full_spec = pl.BlockSpec((half, size), lambda i: (0, 0))
    return pl.pallas_call(
        attention_kernel,
        grid=(steps,),
        in_specs=[pl.BlockSpec(memory_space=pltpu.SMEM), row_spec]
        + [full_spec] * 4
        + [row_spec],
        out_specs=[row_spec] * 2 + [pl.BlockSpec((total, size), lambda i: (0, 0))] * 2,
        out_shape=[jax.ShapeDtypeStruct((length, wide), BF16)] * 2
        + [jax.ShapeDtypeStruct((total, size), BF16)] * 2,
        scratch_shapes=[pltpu.VMEM((total, size), BF16)] * 2
        + [pltpu.VMEM((size, total), BF16)] * 2
        + [pltpu.VMEM((total, size), F32)] * 2,
        compiler_params=pltpu.CompilerParams(
            dimension_semantics=("arbitrary",), vmem_limit_bytes=48 * 1024 * 1024
        ),
        cost_estimate=pl.CostEstimate(
            flops=10 * length * wide * total, bytes_accessed=8 * length * wide, transcendentals=0
        ),
        name="attention",
    )(core, queries, near, far, near_other, far_other, grads)


def prepare_kernel(
    place_ref, own_ref, partner_ref, edge_ref, gain_ref, hidden_ref, turned_ref, wide
):
    core, xl = place_ref[0], place_ref[1]
    channels = hidden_ref.shape[1]
    length = own_ref.shape[0]
    gain = gain_ref[...]

    def rows_of(rows):
        _, normed = rms_parts(rows.astype(F32))
        return gelu_value(normed[:, :channels] * gain)

    chunk = 128

    def body(i, carry):
        at = pl.multiple_of(i * chunk, chunk)
        wide[pl.ds(pl.multiple_of(8 + core * length + at, 8), chunk)] = rows_of(
            own_ref[pl.ds(at, chunk)]
        )
        wide[pl.ds(pl.multiple_of(8 + (1 - core) * length + at, 8), chunk)] = rows_of(
            partner_ref[pl.ds(at, chunk)]
        )
        return carry

    lax.fori_loop(0, length // chunk, body, 0)
    edge = rows_of(edge_ref[...])
    reach = edge.shape[0]
    wide[8 - reach : 8] = jnp.where(xl == 1, edge, 0.0)
    end = 8 + 2 * length
    wide[end : end + 16] = jnp.zeros((16, channels), F32)
    wide[end : end + reach] = jnp.where(xl == 0, edge, 0.0)
    for i in range(2 * length // chunk):
        start = 8 - reach + i * chunk
        hidden_ref[i * chunk : (i + 1) * chunk] = wide[start : start + chunk].astype(BF16)
    start = end - reach
    hidden_ref[2 * length : 2 * length + 16] = wide[start : start + 16].astype(BF16)
    hidden_ref[2 * length + 16 :] = jnp.zeros(
        (hidden_ref.shape[0] - 2 * length - 16, channels), BF16
    )
    turned_ref[...] = hidden_ref[...].T


def prepare(place, own, partner, edge, gain):
    length = own.shape[0]
    channels = gain.shape[0]
    vmem = pl.BlockSpec(memory_space=pltpu.VMEM)
    return pl.pallas_call(
        prepare_kernel,
        in_specs=[pl.BlockSpec(memory_space=pltpu.SMEM)] + [vmem] * 4,
        out_specs=[vmem, vmem],
        out_shape=[
            jax.ShapeDtypeStruct((2 * length + 128, channels), BF16),
            jax.ShapeDtypeStruct((channels, 2 * length + 128), BF16),
        ],
        scratch_shapes=[pltpu.VMEM((2 * length + 32, channels), F32)],
        compiler_params=pltpu.CompilerParams(vmem_limit_bytes=40 * 1024 * 1024),
        name="prepare",
    )(place, own, partner, edge, gain.reshape(1, -1))


def conv_kernel(hidden_ref, block_ref, inner_ref, middle_ref, weight_ref, shifted):
    length, half = inner_ref.shape
    rows = shifted.shape[0]
    channels, wide = weight_ref.shape
    group = channels // 32
    for pair in range(8):
        first = block_ref[2 * pair].astype(F32)
        second = block_ref[2 * pair + 1].astype(F32)
        for side in range(2):
            part = slice(side * group, (side + 1) * group)
            start = side * (channels // 2) + pair * 2 * group
            weight_ref[start : start + 2 * group] = jnp.concatenate(
                [first[part], second[part]], axis=0
            ).astype(BF16)
    hidden = hidden_ref[:rows]
    total = jnp.zeros((length, half), F32)
    for tap in range(wide // half):
        shifted[...] = jnp.dot(
            hidden, weight_ref[:, tap * half : (tap + 1) * half], preferred_element_type=F32
        )
        total = total + shifted[tap : tap + length]
    middle_ref[...] = (inner_ref[...].astype(F32) + total).astype(BF16)


def convolve(hidden, block, inner, taps):
    length, half = inner.shape
    channels = hidden.shape[1]
    vmem = pl.BlockSpec(memory_space=pltpu.VMEM)
    return pl.pallas_call(
        conv_kernel,
        grid=(1,),
        in_specs=[
            pl.BlockSpec(hidden.shape, lambda i: (0, 0)),
            pl.BlockSpec(block.shape[:2] + (taps * half,), lambda i: (0, 0, 0)),
            pl.BlockSpec(inner.shape, lambda i: (0, 0)),
        ],
        out_specs=[vmem, vmem],
        out_shape=[
            jax.ShapeDtypeStruct((length, half), BF16),
            jax.ShapeDtypeStruct((channels, taps * half), BF16),
        ],
        scratch_shapes=[pltpu.VMEM((length + 16, half), F32)],
        compiler_params=pltpu.CompilerParams(vmem_limit_bytes=58 * 1024 * 1024),
        cost_estimate=pl.CostEstimate(
            flops=2 * taps * channels * half * length, bytes_accessed=8 * channels * channels,
            transcendentals=0,
        ),
        name="convolve",
    )(hidden, block, inner)


def input_kernel(
    keep_ref,
    away_ref,
    before_ref,
    after_ref,
    weight_ref,
    other_ref,
    middle_ref,
    stream_ref,
    gain_ref,
    out_ref,
    term_ref,
    keep_wide,
    away_wide,
):
    step = pl.program_id(0)
    length, half = keep_ref.shape
    rows, model = stream_ref.shape
    channels = 2 * half
    reach = before_ref.shape[0]
    width = 2 * reach + 1

    @pl.when(step == 0)
    def _():
        for wide, rows_ref, flip in ((keep_wide, keep_ref, False), (away_wide, away_ref, True)):
            wide[8 : 8 + length] = rows_ref[...].astype(F32)
            for edge_ref, start in ((before_ref, 8 - reach), (after_ref, 8 + length)):
                edge = edge_ref[...].astype(F32)
                wide[start : start + reach] = edge[:, :half] if flip else edge[:, half:]
        term_ref[...] = jnp.zeros(term_ref.shape, F32)

    at = pl.multiple_of(step * rows, rows)
    hidden_grad = jnp.zeros((rows, channels), F32)
    for wide, weights in ((keep_wide, weight_ref), (away_wide, other_ref)):
        block = wide[pl.ds(at, rows + 16)]
        for offset in range(width):
            start = 8 + reach - offset
            hidden_grad = hidden_grad + lax.dot_general(
                block[start : start + rows].astype(BF16),
                weights[:, offset * half : (offset + 1) * half],
                (((1,), (1,)), ((), ())),
                preferred_element_type=F32,
            )
    stream = stream_ref[...].astype(F32)
    inverse, normed = rms_parts(stream)
    gain = gain_ref[...]
    narrow = normed[:, :channels]
    before_grad = hidden_grad * gelu_slope(narrow * gain)
    term_ref[...] += jnp.sum((before_grad * narrow).reshape(rows // 8, 8, channels), axis=0)
    lifted = before_grad * gain
    projected = jnp.sum(lifted * narrow, axis=-1, keepdims=True) * (1.0 / model)
    out_ref[:, :channels] = (
        middle_ref[:, :channels] + inverse * (lifted - narrow * projected)
    ).astype(BF16)
    out_ref[:, channels:] = (
        middle_ref[:, channels:] - inverse * normed[:, channels:] * projected
    ).astype(BF16)


def input_gradient(keep, away, before, behind, weights, other, middle, stream, gain):
    length, model = stream.shape
    half = keep.shape[1]
    rows = 256
    vmem = pl.BlockSpec(memory_space=pltpu.VMEM)
    row_spec = pl.BlockSpec((rows, model), lambda i: (i, 0))
    input_rows, terms = pl.pallas_call(
        input_kernel,
        grid=(length // rows,),
        in_specs=[vmem] * 6
        + [row_spec, row_spec, vmem],
        out_specs=[row_spec, pl.BlockSpec((8, 2 * half), lambda i: (0, 0))],
        out_shape=[
            jax.ShapeDtypeStruct((length, model), BF16),
            jax.ShapeDtypeStruct((8, 2 * half), F32),
        ],
        scratch_shapes=[pltpu.VMEM((length + 16, half), F32)] * 2,
        compiler_params=pltpu.CompilerParams(
            dimension_semantics=("arbitrary",), vmem_limit_bytes=58 * 1024 * 1024
        ),
        cost_estimate=pl.CostEstimate(
            flops=40 * length * half * half, bytes_accessed=16 * length * model, transcendentals=0
        ),
        name="input_gradient",
    )(
        keep, away, before, behind, weights, other, middle,
        stream, gain.reshape(1, -1),
    )
    return input_rows, jnp.sum(terms, axis=0)


def project_kernel(
    core_ref, half_ref, other_ref, own_ref, partner_ref, gain_ref, rest_ref, last_ref,
    attn_ref, kv_ref, qkv_ref, out_full,
):
    step = pl.program_id(0)
    rows, half = half_ref.shape
    model = gain_ref.shape[1]
    steps = pl.num_programs(0)
    groups = model // 32
    quarter = half - kv_ref.shape[1]
    share = quarter // 16

    @pl.when(step == 0)
    def _():
        for at in range(16):
            rest = jnp.concatenate([rest_ref[at], last_ref[at]], axis=1)
            for side in range(2):
                start = side * (model // 2) + at * groups
                qkv_ref[start : start + groups] = rest[:, side * half : (side + 1) * half]
            third = model // 3
            for part in range(3):
                out_full[at * share : (at + 1) * share, part * third : (part + 1) * third] = rest[
                    part * share : (part + 1) * share, 2 * half :
                ]

    second = core_ref[0] == 1
    mine = half_ref[...].astype(F32)
    other = other_ref[...].astype(F32)
    outer = jnp.where(step >= steps // 2, partner_ref[...], own_ref[...]).astype(F32)
    middle = jnp.concatenate(
        [jnp.where(second, other, mine), jnp.where(second, mine, other), outer], axis=1
    )
    _, normed = rms_parts(middle)
    attn = (normed * gain_ref[...]).astype(BF16)
    attn_ref[...] = attn
    kv_ref[...] = jnp.dot(attn, qkv_ref[:, quarter:], preferred_element_type=F32).astype(BF16)


def project(core, half_rows, other_rows, own, partner, gain, rest, quarter):
    length, half = half_rows.shape
    model = own.shape[1]
    rows = 512
    vmem = pl.BlockSpec(memory_space=pltpu.VMEM)

    steps = length // rows

    def by_rows(wide):
        return pl.BlockSpec(
            (rows, wide), lambda i, core: (lax.rem(i + core[0] * (steps // 2), steps), 0)
        )

    def whole(first, second):
        return pl.BlockSpec((first, second), lambda i, core: (0, 0))

    outer = model - 2 * half
    part = rest.shape[:2] + (rest.shape[2] // 5,)
    return pl.pallas_call(
        project_kernel,
        grid_spec=pltpu.PrefetchScalarGridSpec(
            num_scalar_prefetch=1,
            grid=(steps,),
            in_specs=[
                by_rows(half), by_rows(half),
                pl.BlockSpec((rows, outer), lambda i, core: (lax.min(i, steps // 2 - 1), 1)),
                pl.BlockSpec((rows, outer), lambda i, core: (lax.max(i - steps // 2, 0), 1)),
                whole(1, model),
                pl.BlockSpec(part, lambda i, core: (0, 0, 3)),
                pl.BlockSpec(part, lambda i, core: (0, 0, 4)),
            ],
            out_specs=[
                by_rows(model), by_rows(half - quarter), whole(model, half), whole(quarter, model)
            ],
        ),
        out_shape=[
            jax.ShapeDtypeStruct((length, model), BF16),
            jax.ShapeDtypeStruct((length, half - quarter), BF16),
            jax.ShapeDtypeStruct((model, half), BF16),
            jax.ShapeDtypeStruct((quarter, model), BF16),
        ],
        compiler_params=pltpu.CompilerParams(
            dimension_semantics=("arbitrary",), vmem_limit_bytes=58 * 1024 * 1024
        ),
        cost_estimate=pl.CostEstimate(
            flops=2 * length * model * (half - quarter), bytes_accessed=8 * length * model,
            transcendentals=0,
        ),
        name="project",
    )(core, half_rows, other_rows, own, partner, gain.reshape(1, -1), rest, rest)


def projection_kernel(
    core_ref, attn_ref, query_ref, attended_ref, upward_ref, partner_ref, kv_ref, out_ref
):
    tn = (((0,), (0,)), ((), ()))
    model = attn_ref.shape[1]
    wide = query_ref.shape[1]
    half = out_ref.shape[3]
    groups = model // 32
    share = wide // 16
    for side in range(2):
        rows = model // 2
        part = attn_ref[:, side * rows : (side + 1) * rows]
        term = lax.dot_general(part, kv_ref[...], tn, preferred_element_type=F32).astype(BF16)
        for at in range(16):
            start = at * groups
            line = jnp.concatenate(
                [term[start + i * share : start + (i + 1) * share] for i in range(3)], axis=1
            )
            start = (8 + side) * share
            out_ref[at % 4, at // 4, start : start + share] = line
        term = lax.dot_general(part, query_ref[...], tn, preferred_element_type=F32).astype(BF16)
        for at in range(16):
            start = at * groups
            line = jnp.concatenate(
                [term[start + i * share : start + (i + 1) * share] for i in range(3)], axis=1
            )
            for i in range(2):
                start = (2 * side + i) * share
                out_ref[at % 4, at // 4, start : start + share] = line[
                    :, i * half : (i + 1) * half
                ]
    length = upward_ref.shape[0]
    core = core_ref[0]
    own = attended_ref[pl.ds(pl.multiple_of(core * length, length), length)]
    partner = attended_ref[pl.ds(pl.multiple_of((1 - core) * length, length), length)]
    for block in range(model // half):
        columns = slice(block * half, (block + 1) * half)
        term = lax.dot_general(own, upward_ref[:, columns], tn, preferred_element_type=F32)
        term = term + lax.dot_general(
            partner, partner_ref[:, columns], tn, preferred_element_type=F32
        )
        term = term.astype(BF16)
        start = (4 + block) * share
        for at in range(16):
            out_ref[at % 4, at // 4, start : start + share] = term[at * share : (at + 1) * share]


def projection_gradient(core, attn, queries, attended, upward, partner, kv):
    length, model = attn.shape
    wide = queries.shape[1]
    vmem = pl.BlockSpec(memory_space=pltpu.VMEM)
    return pl.pallas_call(
        projection_kernel,
        in_specs=[pl.BlockSpec(memory_space=pltpu.SMEM)] + [vmem] * 6,
        out_specs=vmem,
        out_shape=jax.ShapeDtypeStruct((4, 4, 10 * wide // 16, model // 4), BF16),
        compiler_params=pltpu.CompilerParams(vmem_limit_bytes=48 * 1024 * 1024),
        cost_estimate=pl.CostEstimate(
            flops=8 * length * model * wide, bytes_accessed=16 * length * model, transcendentals=0
        ),
        name="projection_gradient",
    )(core, attn, queries, attended, upward, partner, kv)


def middle_kernel(
    core_ref, query_ref, query_other_ref, kv_ref, kv_other_ref, weight_ref, other_ref,
    middle_ref, upward_ref, gain_ref, grad_ref, keep_ref, away_ref, term_ref,
):
    step = pl.program_id(0)
    nt = (((1,), (1,)), ((), ()))
    rows, model = middle_ref.shape
    wide = query_ref.shape[1]
    half = keep_ref.shape[1]
    grad = jnp.zeros((rows, model), F32)
    for q_ref, k_ref, w_ref in (
        (query_ref, kv_ref, weight_ref), (query_other_ref, kv_other_ref, other_ref)
    ):
        grad = grad + lax.dot_general(
            q_ref[...], w_ref[:, :wide], nt, preferred_element_type=F32
        )
        grad = grad + lax.dot_general(
            k_ref[...], w_ref[:, wide:], nt, preferred_element_type=F32
        )
    inverse, normed = rms_parts(middle_ref[...].astype(F32))
    product = grad * normed

    @pl.when(step == 0)
    def _():
        term_ref[...] = jnp.zeros(term_ref.shape, F32)

    term_ref[...] += jnp.sum(product.reshape(rows // 8, 8, model), axis=0)
    gain = gain_ref[...]
    mean = jnp.mean(product * gain, axis=-1, keepdims=True)
    result = upward_ref[...].astype(F32) + inverse * (grad * gain - normed * mean)
    grad_ref[...] = result
    low = result[:, :half].astype(BF16)
    high = result[:, half : 2 * half].astype(BF16)
    second = core_ref[0] == 1
    keep_ref[...] = jnp.where(second, high, low)
    away_ref[...] = jnp.where(second, low, high)


def middle_gradient(
    core, queries, queries_other, kv, kv_other, weights, other, middle, upward, gain
):
    length, model = middle.shape
    half = weights.shape[1]
    rows = 256

    def by_rows(wide):
        return pl.BlockSpec((rows, wide), lambda i: (i, 0))

    vmem = pl.BlockSpec(memory_space=pltpu.VMEM)
    grads, keep, away, terms = pl.pallas_call(
        middle_kernel,
        grid=(length // rows,),
        in_specs=[
            pl.BlockSpec(memory_space=pltpu.SMEM),
            by_rows(queries.shape[1]), by_rows(queries.shape[1]),
            by_rows(kv.shape[1]), by_rows(kv.shape[1]),
            vmem, vmem, by_rows(model), by_rows(model), vmem,
        ],
        out_specs=[
            by_rows(model), by_rows(half), by_rows(half),
            pl.BlockSpec((8, model), lambda i: (0, 0)),
        ],
        out_shape=[
            jax.ShapeDtypeStruct((length, model), F32),
            jax.ShapeDtypeStruct((length, half), BF16),
            jax.ShapeDtypeStruct((length, half), BF16),
            jax.ShapeDtypeStruct((8, model), F32),
        ],
        compiler_params=pltpu.CompilerParams(
            dimension_semantics=("arbitrary",), vmem_limit_bytes=40 * 1024 * 1024
        ),
        cost_estimate=pl.CostEstimate(
            flops=4 * length * model * half, bytes_accessed=12 * length * model, transcendentals=0
        ),
        name="middle_gradient",
    )(
        core, queries, queries_other, kv, kv_other, weights, other, middle, upward,
        gain.reshape(1, -1),
    )
    return grads, keep, away, jnp.sum(terms, axis=0)


def conv_term_kernel(core_ref, turned_ref, keep_ref, sent_ref, out_ref, wide):
    length, half = keep_ref.shape
    span = turned_ref.shape[1]
    taps = out_ref.shape[3]
    group = out_ref.shape[4]
    first = core_ref[0] == 0
    keep = keep_ref[...].astype(F32)
    sent = sent_ref[...].astype(F32)
    wide[:8] = jnp.zeros((8, half), F32)
    wide[8 : 8 + length] = jnp.where(first, keep, sent)
    wide[8 + length : 8 + 2 * length] = jnp.where(first, sent, keep)
    wide[8 + 2 * length :] = jnp.zeros((span - 2 * length, half), F32)
    for tap in range(taps):
        shifted = wide[8 - tap : 8 - tap + span].astype(BF16)
        term = jnp.dot(turned_ref[...], shifted, preferred_element_type=F32)
        for at in range(32):
            out_ref[at // 4 % 4, at % 4, at // 16, tap] = term[
                at * group : (at + 1) * group
            ].astype(BF16)


def conv_terms(core, turned, keep, sent, taps):
    channels, span = turned.shape
    length, half = keep.shape
    vmem = pl.BlockSpec(memory_space=pltpu.VMEM)
    return pl.pallas_call(
        conv_term_kernel,
        in_specs=[pl.BlockSpec(memory_space=pltpu.SMEM)] + [vmem] * 3,
        out_specs=vmem,
        out_shape=jax.ShapeDtypeStruct((4, 4, 2, taps, channels // 32, half), BF16),
        scratch_shapes=[pltpu.VMEM((span + 8, half), F32)],
        compiler_params=pltpu.CompilerParams(vmem_limit_bytes=40 * 1024 * 1024),
        cost_estimate=pl.CostEstimate(
            flops=2 * taps * channels * half * span, bytes_accessed=4 * channels * span,
            transcendentals=0,
        ),
        name="conv_terms",
    )(core, turned, keep, sent)


def on_device(
    inputs,
    cotangent,
    conv_weight,
    query_weight,
    key_weight,
    value_weight,
    output_weight,
    conv_gain,
    attention_gain,
):
    core = lax.axis_index("core")
    xl = lax.axis_index("xl")
    xh = lax.axis_index("xh")
    place = lax.axis_index(DP)
    rows_in, width, channels = conv_weight.shape
    half = channels // 2
    reach = width // 2
    length, model = inputs.shape[1:]
    head_size = key_weight.shape[1]
    query_size = query_weight.shape[1]
    quarter = query_size // 2
    rows_d = query_weight.shape[0]
    rows_o = output_weight.shape[0]
    upward_low = cotangent[0]
    stream_low = inputs[0]
    tn = (((0,), (0,)), ((), ()))
    nt = (((1,), (1,)), ((), ()))

    def both(mine, other):
        return jnp.concatenate([pick(core, mine, other), pick(core, other, mine)], axis=0)

    def own_rows(array):
        return pick(core, array[:length], array[length:])

    def partner_rows(array):
        return pick(core, array[length:], array[:length])

    with jax.named_scope("gather_conv"):
        own = conv_weight.astype(BF16)
        own = pick(core, own[:, :, :half], own[:, :, half:]).reshape(rows_in, width * half)
        own = jnp.pad(own, ((0, 0), (0, 128)))

    with jax.named_scope("gather"):
        qkv = jnp.concatenate(
            [
                pick(core, query_weight[:, :quarter], query_weight[:, quarter:]),
                pick(core, key_weight, value_weight),
            ],
            axis=1,
        ).astype(BF16)
        third = model // 3
        out_low = jnp.concatenate(
            [output_weight[:, i * third : (i + 1) * third].astype(BF16) for i in range(3)], axis=0
        )
        block = jnp.concatenate(
            [qkv, out_low, jnp.concatenate([own[:, : 2 * third], own[:, 2 * third :]], axis=0)],
            axis=1,
        )
        far = swap(block, "xh")
        pair = [pick(xh, block, far), pick(xh, far, block)]
        start = half + third
        left = width * half - 2 * third
        conv_pair = [
            jnp.concatenate([b[:rows_in, start:], b[rows_in:, start : start + left]], axis=1)
            for b in pair
        ]
        block = jnp.concatenate(
            [
                jnp.concatenate(conv_pair, axis=0),
                pair[0][:, :half],
                pair[1][:, :half],
                pick(xh ^ core, block[:, half:start], far[:, half:start]),
            ],
            axis=1,
        )
        own_block = block
        block = lax.all_gather(block, ("z", "y"), axis=0, tiled=False)

    with jax.named_scope("rows"):
        partner = swap(stream_low, "core")
        edge = after(pick(xl, stream_low[-reach:], stream_low[:reach]), own)
        edge = lax.ppermute(edge, SEQ, [(2, 0), (1, 3)]) + lax.ppermute(edge, SEQ, [(2, 1), (1, 2)])
        upward_partner = swap(upward_low, "core")
        upward_pair = both(upward_low, upward_partner)
        inner = both(stream_low[:, :channels], partner[:, :channels])
        inner = pick(core, inner[:, :half], inner[:, half:])

    core_at = core.reshape(1).astype(jnp.int32)
    spots = jnp.stack([core, xl]).astype(jnp.int32)
    with jax.named_scope("gather_gains"):
        slot = lax.broadcasted_iota(jnp.int32, (32, rows_in + rows_d), 0)
        gains = jnp.concatenate([conv_gain, attention_gain]).astype(BF16)
        gains = after(gains, own_block)
        gains = jnp.where(slot == place, gains[None, :], jnp.zeros((), BF16))
        gains = sum_four(gains, "y")
        gains = sum_four(gains, "z")
        gains = (gains + swap(gains, "xh")).astype(F32)
        gain_one = gains[:, :rows_in].reshape(-1)
        gain_two = gains[:, rows_in:].reshape(-1)
    hidden, hidden_turned = prepare(
        spots, stream_low, partner, after(edge, upward_pair), gain_one
    )
    with jax.named_scope("conv"):
        middle_half, conv_half = convolve(hidden, block, inner, width)
        middle_other = swap(middle_half, "core")
        middle = jnp.concatenate(
            [
                own_rows(pick(core, middle_half, middle_other)),
                own_rows(pick(core, middle_other, middle_half)),
                stream_low[:, channels:],
            ],
            axis=1,
        )

    attn_pair, kv, qkv_half, out_half = project(
        core_at, middle_half, middle_other, stream_low, partner, gain_two, block, quarter
    )

    with jax.named_scope("project"):
        queries = jnp.dot(attn_pair, qkv_half[:, :quarter], preferred_element_type=F32).astype(BF16)
        attended_grad = lax.dot_general(
            upward_pair, out_half, nt, preferred_element_type=F32
        ).astype(BF16)

    with jax.named_scope("keys"):
        kv_far = swap(kv, "xl")
        kv_near_other = swap(kv, "core")
        kv_far_other = swap(kv_far, "core")

    qkv_other = swap(qkv_half, "core")
    conv_other = swap(conv_half, "core")
    attended, query_grad_rows, kv_keep, kv_away = attention(
        core_at, queries, kv, kv_far, kv_near_other, kv_far_other, attended_grad
    )

    with jax.named_scope("key_grads"):
        kv_sum = (kv_keep.astype(F32) + swap(kv_away, "core").astype(F32)).astype(BF16)
        kv_grad_low = (
            kv_sum[: 2 * length].astype(F32) + swap(kv_sum[2 * length :], "xl").astype(F32)
        ).astype(BF16)
        query_grad_other = swap(partner_rows(query_grad_rows), "core")
        kv_grad_other = swap(partner_rows(kv_grad_low), "core")

    middle_grad, cg_keep, cg_away, second_term = middle_gradient(
        after(core_at, conv_other, qkv_other), own_rows(query_grad_rows), query_grad_other, own_rows(kv_grad_low), kv_grad_other,
        qkv_half, qkv_other, middle, upward_low, gain_two,
    )

    with jax.named_scope("conv_grad"):
        cg_sent = swap(cg_away, "core")

        def ends(rows):
            return jnp.concatenate([cg_keep[rows], cg_away[rows]], axis=1)

        after_edge = lax.ppermute(ends(slice(0, reach)), SEQ, [(1, 0), (2, 1), (3, 2)])
        before_edge = lax.ppermute(ends(slice(length - reach, length)), SEQ, [(0, 1), (1, 2), (2, 3)])

    with jax.named_scope("projection_grads"):
        rest_terms = projection_gradient(
            core_at, attn_pair, query_grad_rows, attended, upward_low, upward_partner, kv_grad_low
        )

    conv_term = conv_terms(core_at, hidden_turned, cg_keep, cg_sent, width)

    with jax.named_scope("reduce_conv"):
        shares = lax.psum_scatter(
            conv_term.reshape(4, 4, -1, half), "z", scatter_dimension=0, tiled=False
        )

    input_rows, first_term = input_gradient(
        cg_keep, cg_away, before_edge, after_edge, conv_half, conv_other, middle_grad,
        stream_low, gain_one,
    )

    with jax.named_scope("reduce_gains"):
        terms = jnp.concatenate(
            [first_term.reshape(32, rows_in), second_term.reshape(32, rows_d)], axis=1
        )
        terms = terms.reshape(2, 4, 4, rows_in + rows_d).transpose(2, 0, 1, 3)
        terms = scatter_ring(terms.reshape(4, 8, rows_in + rows_d).astype(BF16), "y", 0)
        terms = terms.reshape(2, 4, rows_in + rows_d).transpose(1, 0, 2)[:, :, None]
        terms = jnp.pad(terms, ((0, 0), (0, 0), (0, 7), (0, half - rows_in - rows_d)))
        terms = terms.reshape(4, 16, half)

    with jax.named_scope("reduce_rest"):
        rest = scatter_ring(rest_terms, "y", 0, first_term)
        rest = scatter_ring(jnp.concatenate([rest, terms], axis=1), "z", 0)

    third = rows_d // 3
    with jax.named_scope("reduce_all"):
        shares = scatter_ring(shares, "y", 0)
        everything = jnp.concatenate([shares, rest], axis=0)
        conv_rows = width * rows_in
        query_rows = rows_d * quarter // half
        out_rows = rows_o * model // half
        sides = []
        start = 0
        for rows in (conv_rows, query_rows, out_rows, third, 8):
            if rows == out_rows:
                sides.append((everything[start : start + rows],) * 2)
                start += rows
            else:
                sides.append(
                    (everything[start : start + rows], everything[start + rows : start + 2 * rows])
                )
                start += 2 * rows
        keep = jnp.concatenate([pick(xh, a, b) for a, b in sides], axis=0)
        send = jnp.concatenate([pick(xh, b, a) for a, b in sides], axis=0)
        total = (keep.astype(F32) + swap(send, "xh").astype(F32)).astype(BF16)
        mine = total.astype(F32) + swap(total, "xl").astype(F32)
        other = swap(total, "core").astype(F32) + swap_both(total, SEQ).astype(F32)
        first = pick(core, mine, other)
        second = pick(core, other, mine)

        def conv_of(side):
            return side[: width * rows_in].reshape(width, rows_in, half)

        conv_total = jnp.concatenate([conv_of(first), conv_of(second)], axis=2).transpose(1, 0, 2)
        start = conv_rows + query_rows + out_rows
        key_total, value_total = [
            jnp.concatenate(
                [
                    side[start : start + third, i * head_size : (i + 1) * head_size]
                    for i in range(3)
                ],
                axis=0,
            )
            for side in (first, second)
        ]

        def query_of(side):
            line = jnp.concatenate(
                [side[conv_rows : conv_rows + rows_o], side[conv_rows + rows_o : conv_rows + query_rows]],
                axis=1,
            )
            return jnp.concatenate(
                [line[:, i * quarter : (i + 1) * quarter] for i in range(3)], axis=0
            )

        query_total = jnp.concatenate([query_of(first), query_of(second)], axis=1)
        start = conv_rows + query_rows
        out_total = pick(xh, first, second)[start : start + out_rows]
        output_total = jnp.concatenate(
            [out_total[i * rows_o : (i + 1) * rows_o] for i in range(model // half)], axis=1
        )
        terms = (first + second)[start + out_rows + third, : rows_in + rows_d]

    return (
        input_rows[None],
        conv_total,
        query_total,
        key_total,
        value_total,
        output_total,
        terms[:rows_in],
        terms[rows_in:],
    )


def solution(mesh):
    grid = Mesh(mesh.devices.reshape(2, 4, 4, 2, 2), AXES)
    in_specs = (
        P(DP, SEQ, None),
        P(DP, SEQ, None),
        P(DP, None, None),
        P(DP, None),
        P(DP, None),
        P(DP, None),
        P(DP, None),
        P(DP),
        P(DP),
    )
    out_specs = (
        P(DP, SEQ, None),
        P(DP, None, None),
        P(DP, None),
        P(DP, None),
        P(DP, None),
        P(DP, None),
        P(DP),
        P(DP),
    )
    return jax.shard_map(
        on_device, mesh=grid, in_specs=in_specs, out_specs=out_specs, check_vma=False
    )
```
